32 devices in a mesh: node: 4 (over y, core), lane: 8 (over z, x).
Axes of the slice: x: 2, y: 2, z: 4, core: 2. Of those that a mesh axis runs over, the one named last changes fastest.
Arguments:
- old_field: float32 [256, 16, 256], P(('node', 'lane')), may hold values from -6 to 6
- old_source: float32 [256, 16, 256], P(('node', 'lane')), may hold values from -6 to 6
- diffusivity: float32 [256, 16, 256], P(('node', 'lane')), may hold values from 0.25 to 4
- target_box: int32 [256], P(('node', 'lane')), may hold values from 0 to 255, as said below
- neighbours: int32 [256, 6], P(('node', 'lane')), may hold values from -1 to 255, as said below
Outputs:
- smoothed: float32 [256, 16, 256], P(('node', 'lane'))
- coarse_defect: float32 [256, 512], P(('node', 'lane'))
The draws below stay inside these ranges and needn't reach their ends.
Inputs may be any that keep to these rules, and one draw needn't show every extreme that they name: `target_box`: every new index appears once; the new owner of a box is its index // 8, the old owner its position // 8. A box moves only to a device of the same node, either at most 2 lane positions away or exactly half the lane axis away; at most one box goes from one device to one other, every device receives as many boxes as it sends, and in every draw some device of each node exchanges a box with every device within 2 lane positions, and some device of each node exchanges a box with the device half the lane axis away. `neighbours`: the neighbour across a face lies on the same device, across faces 0 and 1 possibly on the device one node index lower or higher, across faces 2 and 3 possibly on the device one lane index lower or higher in the same node, never elsewhere. The relation is symmetric: if box a's face f has neighbour b, then b's face f xor 1 has neighbour a. On one device at most 4 boxes have a face 0 (or face 1) neighbour on another device, and at most 8 a face 2 (or face 3) neighbour on another device. -1 marks a face with no box of this level beyond it.
All inputs are finite; a program needn't handle non-finite values.
Results may differ from the reference program's by a relative error of at most 0.00005.
Values sent between devices are 32-bit elements; how exact they have to be, the bound alone decides.
No kernel may reach another device: no remote copies, remote signals or barrier semaphores. Data moves between devices by JAX's collectives and lax.ppermute only.
A program may use at most 64 MiB of HBM per device.

```python
import math
import jax
import jax.numpy as jnp
from jax import lax

BOX = 16
BXD = 2
BYD = 1
BZB = 4
REACH = 2
SWEEPS = 2
NB = 8
NBOX = 256
N_NODE = 4
N_LANE = 8


def layout(key):
    devices = N_NODE * N_LANE
    per_device = BXD * BYD * BZB
    half_lanes = N_LANE // 2
    random_key_list = jax.random.split(key, 7)
    lanes = jnp.arange(N_LANE)
    steps = jnp.arange(1, REACH + 1)
    trades = jax.random.randint(random_key_list[0], (N_NODE, N_LANE, REACH), 0, 2)
    forced = jax.random.randint(random_key_list[1], (N_NODE,), REACH, N_LANE - REACH)
    upper = lanes[None, :, None] == forced[:, None, None]
    lower = lanes[None, :, None] + steps[None, None, :] == forced[:, None, None]
    trades = jnp.where(upper | lower, 1, trades)
    trades = jnp.where(lanes[None, :, None] + steps[None, None, :] < N_LANE, trades, 0)
    padded = jnp.pad(trades, ((0, 0), (REACH, 0), (0, 0)))
    columns = [padded[:, REACH - reach:REACH - reach + N_LANE, reach - 1] for reach in range(REACH, 0, -1)]
    columns = columns + [trades[:, :, reach - 1] for reach in range(1, REACH + 1)]
    near_active = jnp.stack(columns, axis=-1).reshape(devices, 2 * REACH)
    far_bits = jax.random.randint(random_key_list[5], (N_NODE, half_lanes), 0, 2)
    far_forced = jax.random.randint(random_key_list[6], (N_NODE,), 0, half_lanes)
    far_bits = jnp.where(jnp.arange(half_lanes)[None, :] == far_forced[:, None], 1, far_bits)
    far_active = jnp.concatenate([far_bits, far_bits], axis=1).reshape(devices, 1)
    active = jnp.concatenate([near_active, far_active], axis=1)
    offsets = jnp.array([-reach for reach in range(REACH, 0, -1)] + [reach for reach in range(1, REACH + 1)], jnp.int32)
    slots = jnp.arange(per_device)
    device_ids = jnp.arange(devices)
    lane_ids = device_ids % N_LANE
    far_offset = jnp.where(lane_ids < half_lanes, half_lanes, -half_lanes)

    def permute_boxes(part_key):
        scores = jax.random.randint(part_key, (devices, per_device), 0, 2 ** 20) * per_device + slots[None, :]
        return jnp.argsort(scores, axis=1).astype(jnp.int32)
    trade_slot = permute_boxes(random_key_list[2])
    near_partner = jnp.clip(device_ids[:, None] + offsets[None, :], 0, devices - 1)
    partner = jnp.concatenate([near_partner, (device_ids + far_offset)[:, None]], axis=1)
    mirror = jnp.concatenate([2 * REACH - 1 - jnp.arange(2 * REACH), jnp.array([2 * REACH])])
    remote = partner * per_device + trade_slot[partner, mirror[None, :]]
    own = device_ids[:, None] * per_device + trade_slot[:, :2 * REACH + 1]
    content = jnp.where(active == 1, remote, own)
    exchanged_boxes = device_ids[:, None] * per_device + slots[None, :]
    exchanged_boxes = exchanged_boxes.at[device_ids[:, None], trade_slot[:, :2 * REACH + 1]].set(content)
    relabel_boxes = permute_boxes(random_key_list[3])
    retained_boxes = jnp.take_along_axis(exchanged_boxes, relabel_boxes, axis=1).reshape(-1)
    total = devices * per_device
    target = jnp.zeros((total,), jnp.int32).at[retained_boxes].set(jnp.arange(total, dtype=jnp.int32))
    placing = permute_boxes(random_key_list[4])
    slot_of = jnp.argsort(placing, axis=1).astype(jnp.int32)
    node_of = (device_ids // N_LANE)[:, None]
    lane_of = (device_ids % N_LANE)[:, None]
    coord_x = node_of * BXD + placing // (BYD * BZB)
    coord_y = lane_of * BYD + placing // BZB % BYD
    coord_z = placing % BZB
    moves = ((-1, 0, 0), (1, 0, 0), (0, -1, 0), (0, 1, 0), (0, 0, -1), (0, 0, 1))
    found = []
    for shift_x, shift_y, shift_z in moves:
        next_x = coord_x + shift_x
        following_ycoord = coord_y + shift_y
        next_z = coord_z + shift_z
        inside = (next_x >= 0) & (next_x < N_NODE * BXD) & (following_ycoord >= 0) & (following_ycoord < N_LANE * BYD) & (next_z >= 0) & (next_z < BZB)
        next_x = jnp.clip(next_x, 0, N_NODE * BXD - 1)
        following_ycoord = jnp.clip(following_ycoord, 0, N_LANE * BYD - 1)
        next_z = jnp.clip(next_z, 0, BZB - 1)
        owner = next_x // BXD * N_LANE + following_ycoord // BYD
        spot = (next_x % BXD * BYD + following_ycoord % BYD) * BZB + next_z
        found.append(jnp.where(inside, owner * per_device + slot_of[owner, spot], -1))
    linked = jnp.stack(found, axis=-1).reshape(total, 6).astype(jnp.int32)
    return (target, linked)


def draw_target_box(key, part):
    target, linked = layout(key)
    return target


def draw_neighbours(key, part):
    target, linked = layout(key)
    return linked


def draw_old_source(key, part):
    key = jax.random.fold_in(key, 5)
    shape = (NBOX, BOX, BOX * BOX)
    values = jnp.clip(jax.random.normal(key, shape, jnp.float32), -6.0, 6.0)
    return values


def block_levels(key, dims, cuts, least, top_value):
    level, own = 1.0, jax.random.fold_in(key, 6)
    for axis_at, parts in cuts:
        steps = jnp.exp(jax.random.uniform(jax.random.fold_in(own, axis_at), (parts,), jnp.float32, least / len(cuts), top_value / len(cuts)))
        level = level * jnp.repeat(steps, dims[axis_at] // parts).reshape([-1 if axis == axis_at else 1 for axis in range(len(dims))])
    return level


def bell_draw(stream_key, dims, deviation, most, shards=(), held_as=jnp.bfloat16):
    values = deviation * jax.random.normal(stream_key, dims, jnp.float32)
    if shards:
        values = values * block_levels(stream_key, dims, shards, -0.22, 0.18)
    return jnp.clip(values, -most, most).astype(held_as)


def setup_inputs(seed: int = 0) -> dict:
    streams_of = jax.random.split(jax.random.key(seed), 6)
    old_field = bell_draw(streams_of[0], (NBOX, BOX, BOX * BOX), 1.0, 6.0, ((0, 32),), jnp.float32)
    old_source = draw_old_source(jax.random.fold_in(streams_of[5], 71), 0)
    diffusivity = jnp.clip(jnp.exp(math.log(4.0) - 2.7725887 * jax.random.uniform(streams_of[2], (NBOX, BOX, BOX * BOX), jnp.float32) ** block_levels(streams_of[2], (NBOX, BOX, BOX * BOX), ((0, 32),), -0.2, 0.2)), 0.25, 4.0)
    target_box = draw_target_box(jax.random.fold_in(streams_of[5], 71), 0)
    neighbours = draw_neighbours(jax.random.fold_in(streams_of[5], 71), 0)
    return {"old_field": old_field, "old_source": old_source, "diffusivity": diffusivity, "target_box": target_box, "neighbours": neighbours}


OPPOSITE = (1, 0, 3, 2, 5, 4)


def face_layers(values):
    boxes, side, plane = values.shape
    return jnp.stack([values[:, 0], values[:, side - 1],
                      values[:, :, :side].reshape(boxes, plane),
                      values[:, :, plane - side:].reshape(boxes, plane),
                      values[:, :, 0::side].reshape(boxes, plane),
                      values[:, :, side - 1::side].reshape(boxes, plane)], axis=1)


def near_values(values, ghost):
    boxes, side, plane = values.shape
    lower_x = jnp.concatenate([ghost[:, 0][:, None, :], values[:, :-1]], axis=1)
    upper_x = jnp.concatenate([values[:, 1:], ghost[:, 1][:, None, :]], axis=1)
    lower_y = jnp.concatenate([ghost[:, 2].reshape(boxes, side, side), values[:, :, :plane - side]], axis=2)
    upper_y = jnp.concatenate([values[:, :, side:], ghost[:, 3].reshape(boxes, side, side)], axis=2)
    depth = jnp.arange(plane) % side
    lower_z = jnp.where(depth == 0, jnp.repeat(ghost[:, 4].reshape(boxes, side, side), side, axis=2),
                        jnp.roll(values, 1, axis=2))
    upper_z = jnp.where(depth == side - 1, jnp.repeat(ghost[:, 5].reshape(boxes, side, side), side, axis=2),
                        jnp.roll(values, -1, axis=2))
    return [lower_x, upper_x, lower_y, upper_y, lower_z, upper_z]


def coefficients(diffusivity, beside):
    return [2.0 * diffusivity * other / (diffusivity + other) for other in beside]


def relax(values, source, couplings, beside, chosen):
    total = couplings[0]
    summed = source + couplings[0] * beside[0]
    for face in range(1, 6):
        total = total + couplings[face]
        summed = summed + couplings[face] * beside[face]
    return jnp.where(chosen, summed / total, values)


def defect_of(values, source, couplings, beside):
    total = couplings[0]
    summed = source + couplings[0] * beside[0]
    for face in range(1, 6):
        total = total + couplings[face]
        summed = summed + couplings[face] * beside[face]
    return summed - total * values


def colour_of(side, plane):
    rows = jnp.arange(side)[:, None]
    cells = jnp.arange(plane)[None, :]
    return (rows + cells // side + cells % side) % 2


def shrink(values):
    boxes, side, plane = values.shape
    half = side // 2
    blocks = values.reshape(boxes, half, 2, half, 2, half, 2)
    return 0.125 * jnp.sum(blocks, axis=(2, 4, 6)).reshape(boxes, half * half * half)


def ghost_of(layers, neighbours, fallback):
    boxes = layers.shape[0]
    present = neighbours >= 0
    rows = jnp.maximum(neighbours, 0) * 6 + jnp.array(OPPOSITE, jnp.int32)[None, :]
    picked = layers.reshape(boxes * 6, layers.shape[2])[rows]
    return jnp.where(present[..., None], picked, fallback)


def reference(old_field, old_source, diffusivity, target_box, neighbours):
    boxes, side, plane = old_field.shape
    field = jnp.zeros_like(old_field).at[target_box].set(old_field)
    source = jnp.zeros_like(old_source).at[target_box].set(old_source)
    beta_layers = face_layers(diffusivity)
    beta_ghost = ghost_of(beta_layers, neighbours, beta_layers)
    colour = colour_of(side, plane)
    blocks = boxes // NB

    def split(values):
        return values.reshape((blocks, NB) + values.shape[1:])

    def half_sweep(values, colour_id):
        layers = face_layers(values)
        ghost = ghost_of(layers, neighbours, jnp.zeros_like(layers))

        def update_block(pieces):
            part_field, part_source, part_beta, part_bghost, part_ghost = pieces
            couplings = coefficients(part_beta, near_values(part_beta, part_bghost))
            return relax(part_field, part_source, couplings, near_values(part_field, part_ghost), colour == colour_id)

        result = lax.map(update_block, (split(values), split(source), split(diffusivity), split(beta_ghost), split(ghost)))
        return result.reshape(values.shape)

    for sweep in range(SWEEPS):
        for colour_id in (0, 1):
            field = half_sweep(field, colour_id)
    layers = face_layers(field)
    ghost = ghost_of(layers, neighbours, jnp.zeros_like(layers))

    def defect_block(pieces):
        part_field, part_source, part_beta, part_bghost, part_ghost = pieces
        couplings = coefficients(part_beta, near_values(part_beta, part_bghost))
        return shrink(defect_of(part_field, part_source, couplings, near_values(part_field, part_ghost)))

    coarse = lax.map(defect_block, (split(field), split(source), split(diffusivity), split(beta_ghost), split(ghost)))
    return field, coarse.reshape(boxes, coarse.shape[2])
```

```python
import jax
import jax.numpy as jnp
from jax import lax
from jax.experimental import pallas as pl
from jax.experimental.pallas import tpu as pltpu
from jax.sharding import PartitionSpec as P

SWEEPS = 2


OPPOSITE = (1, 0, 3, 2, 5, 4)


def with_halo(block, sides, width):
    for axis, dim in sides:
        count = lax.axis_size(axis)
        forward = [(i, i + 1) for i in range(count - 1)]
        backward = [(target, source) for source, target in forward]
        low = lax.ppermute(
            lax.slice_in_dim(block, block.shape[dim] - width, None, axis=dim), axis, forward
        )
        high = lax.ppermute(lax.slice_in_dim(block, 0, width, axis=dim), axis, backward)
        block = jnp.concatenate([low, block, high], axis=dim)
    return block


def face_layers(values):
    boxes, side, plane = values.shape
    return jnp.stack(
        [
            values[:, 0],
            values[:, side - 1],
            values[:, :, :side].reshape(boxes, plane),
            values[:, :, plane - side :].reshape(boxes, plane),
            values[:, :, 0::side].reshape(boxes, plane),
            values[:, :, side - 1 :: side].reshape(boxes, plane),
        ],
        axis=1,
    )


def near_values(values, ghost):
    boxes, side, plane = values.shape
    lower_x = jnp.concatenate([ghost[:, 0][:, None, :], values[:, :-1]], axis=1)
    upper_x = jnp.concatenate([values[:, 1:], ghost[:, 1][:, None, :]], axis=1)
    lower_y = jnp.concatenate(
        [ghost[:, 2].reshape(boxes, side, side), values[:, :, : plane - side]], axis=2
    )
    upper_y = jnp.concatenate([values[:, :, side:], ghost[:, 3].reshape(boxes, side, side)], axis=2)
    depth = jnp.arange(plane) % side
    lower_z = jnp.where(
        depth == 0,
        jnp.repeat(ghost[:, 4].reshape(boxes, side, side), side, axis=2),
        jnp.roll(values, 1, axis=2),
    )
    upper_z = jnp.where(
        depth == side - 1,
        jnp.repeat(ghost[:, 5].reshape(boxes, side, side), side, axis=2),
        jnp.roll(values, -1, axis=2),
    )
    return [lower_x, upper_x, lower_y, upper_y, lower_z, upper_z]


def coefficients(diffusivity, beside):
    return [2.0 * diffusivity * other / (diffusivity + other) for other in beside]


def relax(values, source, couplings, beside, chosen):
    total = couplings[0]
    summed = source + couplings[0] * beside[0]
    for face in range(1, 6):
        total = total + couplings[face]
        summed = summed + couplings[face] * beside[face]
    return jnp.where(chosen, summed / total, values)


def defect_of(values, source, couplings, beside):
    total = couplings[0]
    summed = source + couplings[0] * beside[0]
    for face in range(1, 6):
        total = total + couplings[face]
        summed = summed + couplings[face] * beside[face]
    return summed - total * values


def colour_of(side, plane):
    rows = jnp.arange(side)[:, None]
    cells = jnp.arange(plane)[None, :]
    return (rows + cells // side + cells % side) % 2


def restrict(values):
    boxes, side, plane = values.shape
    half = side // 2
    paired = values.reshape(boxes, half, 2, plane).sum(axis=2)
    cells = jnp.arange(plane)
    coarse_cols = cells // side // 2 * half + cells % side // 2
    pooling = (coarse_cols[:, None] == jnp.arange(half * half)[None, :]).astype(jnp.float32)
    summed = jnp.einsum("bxp,pq->bxq", paired, pooling, precision=lax.Precision.HIGHEST)
    return (0.125 * summed).reshape(boxes, half * half * half)


def place(settled, arrived, tags):
    count = settled.shape[0]
    return settled.at[jnp.where(tags > 0, tags - 1, count)].set(arrived, mode="drop")


def general_body(old_field, old_source, diffusivity, target_box, neighbours):
    count, side, plane = old_field.shape
    lane_count = lax.axis_size("lane")
    lane_here = lax.axis_index("lane")
    own_device = lax.axis_index("node") * lane_count + lane_here
    dest_device = target_box // count
    dest_slot = target_box % count
    staying = dest_device == own_device
    cargo = jnp.stack([old_field, old_source], axis=1)
    settled = jnp.zeros_like(cargo).at[jnp.where(staying, dest_slot, count)].set(cargo, mode="drop")
    slots = jnp.arange(count)
    peers = own_device - lane_here + jnp.arange(lane_count)
    chosen = (dest_device[None, :] == peers[:, None]) & jnp.logical_not(staying)[None, :]
    filled = jnp.any(chosen, axis=1)
    picked = jnp.sum(jnp.where(chosen, slots[None, :], 0), axis=1)
    parcels = jnp.where(filled[:, None, None, None], cargo[picked], 0.0)
    labels = jnp.where(filled, jnp.sum(jnp.where(chosen, dest_slot[None, :], 0), axis=1) + 1, 0)
    arrived, tags = (
        lax.all_to_all(parcels, "lane", split_axis=0, concat_axis=0, tiled=True),
        lax.all_to_all(labels, "lane", split_axis=0, concat_axis=0, tiled=True),
    )
    settled = place(settled, arrived, tags)
    field = settled[:, 0]
    source = settled[:, 1]
    present = neighbours >= 0
    near_device = jnp.where(present, neighbours // count, own_device)
    local_row = neighbours % count * 6 + jnp.array(OPPOSITE, jnp.int32)[None, :]
    across = near_device - own_device
    anchor = jnp.where(
        across == -lane_count,
        1,
        jnp.where(
            across == lane_count, 2, jnp.where(across == -1, 3, jnp.where(across == 1, 4, 0))
        ),
    )
    index = anchor * (count * 6) + local_row
    width_out = count * 6

    def departing_boxes(layers):
        return layers.reshape(count * 6, plane)

    def incoming(received, start):
        return jnp.concatenate(
            [
                received[0, 1, start : start + width_out],
                received[2, 1, start : start + width_out],
                received[1, 0, start : start + width_out],
                received[1, 2, start : start + width_out],
            ],
            axis=0,
        )

    def trade(rows):
        return with_halo(rows[None, None], (("node", 0), ("lane", 1)), 1)

    def ghosts(layers, remote_rows, fallback):
        table = jnp.concatenate([layers.reshape(count * 6, plane), remote_rows], axis=0)
        return jnp.where(present[..., None], table[index], fallback)

    beta_layers = face_layers(diffusivity)
    layers = face_layers(field)
    received = trade(
        jnp.concatenate([departing_boxes(layers), departing_boxes(beta_layers)], axis=0)
    )
    beta_ghost = ghosts(beta_layers, incoming(received, width_out), beta_layers)
    couplings = coefficients(diffusivity, near_values(diffusivity, beta_ghost))
    colour = colour_of(side, plane)
    for sweep in range(SWEEPS):
        for colour_id in (0, 1):
            if sweep + colour_id > 0:
                layers = face_layers(field)
                received = trade(departing_boxes(layers))
            ghost = ghosts(layers, incoming(received, 0), jnp.zeros_like(layers))
            field = relax(field, source, couplings, near_values(field, ghost), colour == colour_id)
    layers = face_layers(field)
    received = trade(departing_boxes(layers))
    ghost = ghosts(layers, incoming(received, 0), jnp.zeros_like(layers))
    coarse = restrict(defect_of(field, source, couplings, near_values(field, ghost)))
    return (field, coarse)


BXD = 2
BZB = 4
PAD = 8
LOW, HIGH = "low", "high"


def lane_plan(lanes):
    half = lanes // 2
    moves = [1, lanes - 1, 2, lanes - 2, half]
    singles = {}

    def add(offset, move, part):
        if offset % lanes:
            singles.setdefault(offset % lanes, []).append((move, part))

    for move in moves:
        add(move, move, LOW)
        add(move, move, HIGH)
        add(move + 1, move, HIGH)
        add(move - 1, move, LOW)
    bulk = {1: HIGH, lanes - 1: LOW}
    plan = {}
    for offset in sorted(singles):
        kept = [item for item in singles[offset] if not (item[0] == offset and item[1] == bulk.get(offset))]
        plan[offset] = (bulk.get(offset), kept)
    return moves, plan


def part_lanes(part, plane):
    return slice(0, plane // 2) if part == LOW else slice(plane // 2, plane)


def pack_kernel(moves, plan, lanes, count, *refs):
    me, target, near, field, source, beta = refs[:6]
    outs = refs[6 : 6 + len(plan)]
    labels, table, sems = refs[6 + len(plan) :]
    side, plane = field.shape[1:]
    half = plane // 2
    copies = []

    def send(src, dst):
        copy = pltpu.make_async_copy(src, dst, sems.at[len(copies)])
        copy.start()
        copies.append(copy)

    for out, (bulk, kept) in zip(outs, plan.values()):
        if bulk is not None:
            for at, array in enumerate((field, source, beta)):
                send(array.at[:, :, part_lanes(bulk, plane)], out.at[at * count : (at + 1) * count])
    lane, own = me[1], me[2]
    first = own * count
    old_index = [jnp.int32(0)] * len(moves)
    new_slot = [jnp.int32(-1)] * len(moves)
    stay = []
    for i in range(count):
        there = target[i]
        slot = lax.rem(there, count)
        step = lax.rem(lax.rem(lax.div(there, count), lanes) - lane + lanes, lanes)
        stay.append(jnp.where(step == 0, slot, -1))
        for k, move in enumerate(moves):
            old_index[k] = jnp.where(step == move, i, old_index[k])
            new_slot[k] = jnp.where(step == move, slot, new_slot[k])
    for out, (bulk, kept) in zip(outs, plan.values()):
        unit = 3 * count if bulk is not None else 0
        for move, part in kept:
            box = old_index[moves.index(move)]
            for array in (field, source):
                send(array.at[box, :, part_lanes(part, plane)], out.at[unit])
                unit += 1
    for i in range(count):
        labels[1, i] = -1

    def local(index, face):
        there = near[index, face]
        inside = (there >= first) & (there < first + count)
        return inside, jnp.clip(there - first, 0, count - 1)

    place = []
    for i in range(count):
        inside, below = local(i, 0)
        depth = jnp.int32(0)
        live, at = local(i, 4)
        for _ in range(BZB - 1):
            depth = depth + jnp.where(live, 1, 0)
            further, onward = local(at, 4)
            live, at = live & further, onward
        spot = jnp.where(inside, BZB, 0) + depth
        place.append(spot)
        labels[0, i] = spot
        labels[1, spot] = i
        labels[3, i] = stay[i]
    for k in range(len(moves)):
        labels[2, k] = new_slot[k]
        labels[4, k] = old_index[k]
    rows = lax.broadcasted_iota(jnp.int32, (8, 128), 0)
    cols = lax.broadcasted_iota(jnp.int32, (8, 128), 1)
    spots = rows * 128 + cols
    held = jnp.zeros((8, 128), jnp.int32)

    def put(held, row, col, value):
        return jnp.where(spots == row * 128 + col, value, held)

    for i in range(count):
        slot = labels[1, i]
        held = put(held, i, 0, jnp.where(slot < 0, -7, first + slot))
        for face in range(6):
            held = put(held, i, 1 + face, near[jnp.maximum(slot, 0), face])
        held = put(held, i, 7, place[i])
        held = put(held, i, 9, stay[i])
    for k in range(len(moves)):
        held = put(held, k, 8, new_slot[k])
        held = put(held, k, 10, old_index[k])
    table[...] = held.astype(jnp.float32)
    for out in outs:
        send(table, out.at[out.shape[0] - 1, 0:8])
    for copy in copies:
        copy.wait()


def assemble_kernel(moves, plan, lanes, count, *refs):
    labels, own_table, field, source, beta = refs[:5]
    got = dict(zip(plan, refs[5 : 5 + len(plan)]))
    block, upward, downward, row_table, tables, seen, sem, table_sems, seen_sems = refs[5 + len(plan) :]
    side, plane = field.shape[1:]
    half = plane // 2
    order = list(plan)
    fetch = []
    for k, offset in enumerate(order):
        fetch.append(pltpu.make_async_copy(got[offset].at[got[offset].shape[0] - 1, 0:8], tables.at[k], table_sems.at[k]))
    shown = {0: None, 1: 1, lanes - 1: lanes - 1}
    if lanes == 8:
        shown = {offset: offset for offset in range(8) if offset == 0 or offset in got}
    for offset in shown:
        if offset:
            at = offset % 8 if offset < lanes - 1 else 7
            fetch.append(pltpu.make_async_copy(got[offset].at[got[offset].shape[0] - 1, 0:8], seen.at[at], seen_sems.at[at]))
    for copy in fetch:
        copy.start()

    def spot(place):
        return lax.rem(place, BZB), pl.ds(pl.multiple_of(lax.div(place, BZB) * side, side), side)

    def copy(src, array, place, where):
        deep, rows = spot(place)
        pltpu.make_async_copy(src, block.at[array, deep, rows, where], sem).start()

    own_half = {LOW: slice(half, 2 * half), HIGH: slice(2 * half, 3 * half)}
    low_halo, high_halo = slice(0, half), slice(3 * half, 4 * half)
    whole = slice(half, 3 * half)
    old = (field, source)
    for i in range(count):
        copy(beta.at[i], 2, labels[0, i], whole)

        @pl.when(labels[3, i] >= 0)
        def _():
            for a in range(2):
                copy(old[a].at[i], a, labels[0, labels[3, i]], whole)

    for k in range(len(order)):
        fetch[k].wait()

    def said(offset, row, col):
        return tables[order.index(offset), row, col].astype(jnp.int32)

    below, above = 1, lanes - 1

    def place_below(slot):
        return said(below, slot, 7)

    def place_above(slot):
        return said(above, slot, 7)

    for move, part, halo, place in ((1, LOW, high_halo, place_above), (lanes - 1, HIGH, low_halo, place_below)):
        k = moves.index(move)

        @pl.when(labels[2, k] >= 0)
        def _():
            for a in range(2):
                copy(old[a].at[labels[4, k], :, part_lanes(part, plane)], a, place(labels[2, k]), halo)

    for offset, (bulk, kept) in plan.items():
        message = got[offset]
        unit = 0
        if bulk is not None:
            halo = low_halo if offset == below else high_halo
            for i in range(count):
                copy(message.at[2 * count + i], 2, said(offset, i, 7), halo)

                @pl.when(said(offset, i, 9) >= 0)
                def _():
                    for a in range(2):
                        copy(message.at[a * count + i], a, said(offset, said(offset, i, 9), 7), halo)

            k = moves.index(offset)

            @pl.when(said(offset, k, 8) >= 0)
            def _():
                for a in range(2):
                    copy(message.at[a * count + said(offset, k, 10)], a, labels[0, said(offset, k, 8)], own_half[bulk])

            unit = 3 * count
        for move, part in kept:
            k = moves.index(move)
            apart = (move - offset) % lanes

            @pl.when(said(offset, k, 8) >= 0)
            def _():
                slot = said(offset, k, 8)
                if apart == 0:
                    place, where = labels[0, slot], own_half[part]
                elif apart == 1:
                    place, where = place_above(slot), high_halo
                else:
                    place, where = place_below(slot), low_halo
                for a in range(2):
                    copy(message.at[unit + a], a, place, where)

            unit += 2
    cols = lax.broadcasted_iota(jnp.int32, (8, 128), 1)
    for copy_in in fetch[len(order) :]:
        copy_in.wait()
    joined = jnp.where(cols < 8, own_table[...], 0.0)
    for offset in shown:
        if offset:
            at = offset if offset < 7 else 7
            joined = joined + pltpu.roll(jnp.where(cols < 8, seen[at], 0.0), 8 * at, 1)
    joined = joined + pltpu.roll(joined, 64, 1)
    row_table[...] = joined
    upward[upward.shape[0] - 1] = joined
    downward[downward.shape[0] - 1] = joined
    pltpu.make_async_copy(block, block, sem).wait()
    width = block.shape[3]
    levels = lax.broadcasted_iota(jnp.int32, (8, width), 0)
    last = block.shape[2] - 8
    for deep in range(BZB):
        a, b, c = (block[k, deep, last : last + 8] for k in range(3))
        up_first = jnp.where(levels < 3, pltpu.roll(b, 3, 0), a)
        up_second = jnp.where(levels == 0, pltpu.roll(b, 4, 0), c)
        a, b, c = (block[k, deep, 0:8] for k in range(3))
        down_first = jnp.where(levels >= 5, pltpu.roll(b, 5, 0), a)
        down_second = jnp.where(levels == 7, pltpu.roll(b, 4, 0), c)
        for k in range(width // 128):
            cut = slice(k * 128, (k + 1) * 128)
            at = deep * 2 * (width // 128) + k
            upward[at] = up_first[:, cut]
            upward[at + width // 128] = up_second[:, cut]
            downward[at] = down_first[:, cut]
            downward[at + width // 128] = down_second[:, cut]


def smooth_kernel(lanes, nodes, covered, me, labels, block, from_below, from_above, row_table, two_on, smoothed, coarse, flag,
                  f, s, b, xl, xu, yl, yu, zl, zu, total, inverse, rest):
    width = block.shape[3]
    own_rows = block.shape[2]
    side = smoothed.shape[1]
    plane = smoothed.shape[2]
    half = plane // 2
    tiles = width // 128
    node, lane = me[0], me[1]
    first_node, last_node = node == 0, node == nodes - 1
    first_lane, last_lane = lane == 0, lane == lanes - 1
    top = 2 * PAD + own_rows
    rows8 = lax.broadcasted_iota(jnp.int32, (8, width), 0)
    cols = lax.broadcasted_iota(jnp.int32, (8, width), 1)
    depth = lax.rem(cols, side)
    at_front, at_back = depth == 0, depth == side - 1
    colour = lax.rem(rows8 + lax.div(cols, side) + depth, 2)

    zero, one = jnp.zeros((8, width), jnp.float32), jnp.ones((8, width), jnp.float32)
    for deep in range(BZB):
        for rows in (slice(0, 8), slice(top + 8, top + 16)):
            f[deep, rows] = zero
            b[deep, rows] = one
            xu[deep, rows] = zero
        f[deep, 2 * PAD : top] = block[0, deep]
        b[deep, 2 * PAD : top] = block[2, deep]
        s[deep, 2 * PAD : top] = block[1, deep]
        for message, start, below in ((from_below, PAD, True), (from_above, top, False)):
            base = deep * 2 * tiles
            first = jnp.concatenate([message[base + k] for k in range(tiles)], axis=1)
            second = jnp.concatenate([message[base + tiles + k] for k in range(tiles)], axis=1)
            if below:
                src = jnp.where(rows8 >= 5, pltpu.roll(first, 5, 0), pltpu.roll(second, 4, 0))
            else:
                src = jnp.where(rows8 < 3, pltpu.roll(first, 3, 0), pltpu.roll(second, 4, 0))
            f[deep, start : start + 8] = first
            b[deep, start : start + 8] = jnp.where(rows8 == (0 if below else 7), 1.0, second)
            s[deep, start : start + 8] = src

    def after(values):
        return pltpu.roll(values, width - side, 1)

    def before(values):
        return pltpu.roll(values, side, 1)

    def beyond_z(values, afters):
        out = []
        for deep in range(BZB):
            joined = values[deep] if deep == 0 else jnp.where(at_back, afters[deep - 1], values[deep])
            out.append(pltpu.roll(joined, 1, 1))
        return out

    def ahead_z(values, befores):
        out = []
        for deep in range(BZB):
            joined = values[deep] if deep == BZB - 1 else jnp.where(at_front, befores[deep + 1], values[deep])
            out.append(pltpu.roll(joined, width - 1, 1))
        return out

    def mean(one_side, other):
        return 2.0 * one_side * other / (one_side + other)

    starts = range(PAD, top + 8, 8)
    low_edge = (cols >= half) & (cols < half + side) & first_lane
    high_edge = (cols >= 3 * half - side) & (cols < 3 * half) & last_lane
    no_link = ((cols >= half - side) & (cols < half) & first_lane) | high_edge
    for r in starts:
        held = [b[deep, r : r + 8] for deep in range(BZB)]
        befores = [before(v) for v in held]
        afters = [after(v) for v in held]
        aheads = ahead_z(held, befores)
        ky = [jnp.where(no_link, 0.0, mean(held[d], afters[d])) for d in range(BZB)]
        kz = [mean(held[d], aheads[d]) for d in range(BZB)]
        kz[BZB - 1] = jnp.where(at_back, 0.0, kz[BZB - 1])
        kzl = beyond_z(kz, [after(v) for v in kz])
        kzl[0] = jnp.where(at_front, 0.0, kzl[0])
        for d in range(BZB):
            kx = mean(held[d], b[d, r + 1 : r + 9])
            if r == PAD:
                kx = jnp.where((rows8 == 7) & first_node, 0.0, kx)
            if r == top - 8:
                kx = jnp.where((rows8 == 7) & last_node, 0.0, kx)
            xu[d, r : r + 8] = kx
            yu[d, r : r + 8] = ky[d]
            yl[d, r : r + 8] = before(ky[d])
            zu[d, r : r + 8] = kz[d]
            zl[d, r : r + 8] = kzl[d]
    for r in starts:
        for d in range(BZB):
            here = slice(r, r + 8)
            kxl = xu[d, r - 1 : r + 7]
            xl[d, here] = kxl
            held = b[d, here]
            whole = kxl + xu[d, here] + yl[d, here] + yu[d, here] + zl[d, here] + zu[d, here]
            whole = whole + jnp.where(low_edge, held, 0.0) + jnp.where(high_edge, held, 0.0)
            if d == 0:
                whole = whole + jnp.where(at_front, held, 0.0)
            if d == BZB - 1:
                whole = whole + jnp.where(at_back, held, 0.0)
            if r == 2 * PAD:
                whole = whole + jnp.where((rows8 == 0) & first_node, held, 0.0)
            if r == top - 8:
                whole = whole + jnp.where((rows8 == 7) & last_node, held, 0.0)
            if 2 * PAD <= r < top:
                total[d, r - 2 * PAD : r - 2 * PAD + 8] = whole
            inverse[d, here] = 1.0 / whole

    def sums(r, held, afters, befores):
        behind = beyond_z(held, afters)
        aheads = ahead_z(held, befores)
        here = slice(r, r + 8)
        out = []
        for d in range(BZB):
            part = s[d, here] + xl[d, here] * f[d, r - 1 : r + 7] + xu[d, here] * f[d, r + 1 : r + 9]
            part = part + (yl[d, here] * befores[d] + yu[d, here] * afters[d])
            out.append(part + (zl[d, here] * behind[d] + zu[d, here] * aheads[d]))
        return out

    for sweep in range(SWEEPS):
        for colour_id in (0, 1):
            chosen = colour == colour_id
            for r in starts:
                held = [f[d, r : r + 8] for d in range(BZB)]
                parts = sums(r, held, [after(v) for v in held], [before(v) for v in held])
                for d in range(BZB):
                    f[d, r : r + 8] = jnp.where(chosen, parts[d] * inverse[d, r : r + 8], held[d])

    for r in range(2 * PAD, top, 8):
        held = [f[d, r : r + 8] for d in range(BZB)]
        parts = sums(r, held, [after(v) for v in held], [before(v) for v in held])
        wide, inner = divmod(r - 2 * PAD, side)
        for d in range(BZB):
            left = parts[d] - total[d, r - 2 * PAD : r - 2 * PAD + 8] * held[d]
            slot = jnp.maximum(labels[1, wide * BZB + d], 0)
            smoothed[slot, inner : inner + 8] = held[d][:, half : 3 * half]
            for k in range(plane // 128):
                cut = slice(half + k * 128, half + (k + 1) * 128)
                rest[k, pl.ds(pl.multiple_of(slot * side + inner, 8), 8), :] = left[:, cut]

    count = smoothed.shape[0]
    small = side // 2
    cells = lax.broadcasted_iota(jnp.int32, (plane, 128), 0)
    slots = lax.broadcasted_iota(jnp.int32, (plane, 128), 1)
    goal = lax.div(lax.div(cells, side), 2) * small + lax.div(lax.rem(cells, side), 2)
    per = small * small
    for pair in range(small * per // 128):
        acc = None
        for inner in range(128 // per):
            i = pair * (128 // per) + inner
            even = [rest[k, pl.ds(2 * i, count, stride=side), :] for k in range(plane // 128)]
            odd = [rest[k, pl.ds(2 * i + 1, count, stride=side), :] for k in range(plane // 128)]
            rows = jnp.concatenate(even, axis=1) + jnp.concatenate(odd, axis=1)
            pooling = (goal + inner * per == slots).astype(jnp.float32)
            term = jnp.dot(rows, pooling, precision=lax.Precision.HIGHEST, preferred_element_type=jnp.float32)
            acc = term if acc is None else acc + term
        coarse[:, pair * 128 : (pair + 1) * 128] = 0.125 * acc

    mine = from_below.shape[0] - 1
    rows1 = lax.broadcasted_iota(jnp.int32, (8, 128), 0)
    cols1 = lax.broadcasted_iota(jnp.int32, (8, 128), 1)
    owner = lax.rem(lax.div(cols1, 8), 8)
    field_of = lax.rem(cols1, 8)
    own, opposite = row_table[...], two_on[...]
    lower, upper = from_below[mine], from_above[mine]
    rows_of = [(own, lower, upper, node), (lower, opposite, own, lax.rem(node + nodes - 1, nodes)),
               (upper, own, opposite, lax.rem(node + 1, nodes)), (opposite, upper, lower, lax.rem(node + 2, nodes))]
    if not covered:
        rows_of = rows_of[:1]
    lane_of = lax.rem(lane - jnp.where(owner > 4, owner - 8, owner) + 2 * lanes, lanes)
    wrong = jnp.zeros((8, 128), jnp.float32)
    for table, low, high, at_node in rows_of:
        turned = pltpu.roll(table, 4, 0)
        at_low = jnp.where(rows1 >= 4, turned, jnp.where(at_node == 0, -1.0, pltpu.roll(low, 4, 0)))
        at_high = jnp.where(rows1 < 4, turned, jnp.where(at_node == nodes - 1, -1.0, pltpu.roll(high, 4, 0)))
        y_low = jnp.where(lane_of == 0, -1.0, pltpu.roll(table, 128 - 8, 1))
        y_high = jnp.where(lane_of == lanes - 1, -1.0, pltpu.roll(table, 8, 1))
        z_low = jnp.where(lax.rem(rows1, BZB) == 0, -1.0, pltpu.roll(table, 1, 0))
        z_high = jnp.where(lax.rem(rows1, BZB) == BZB - 1, -1.0, pltpu.roll(table, 7, 0))
        bad = jnp.where((field_of == 0) & (table < 0), 1.0, 0.0)
        for face, expected in enumerate((at_low, at_high, y_low, y_high, z_low, z_high)):
            differs = table != pltpu.roll(expected, 1 + face, 1)
            bad = bad + jnp.where((field_of == 1 + face) & differs, 1.0, 0.0)
        if not covered:
            bad = jnp.where(owner == 0, bad, 0.0)
        wrong = wrong + bad
    flag[0, 0] = (jnp.sum(wrong) > 0).astype(jnp.int32)


ANY = pl.BlockSpec(memory_space=pl.ANY)
SCALARS = pl.BlockSpec(memory_space=pltpu.SMEM)
VECTORS = pl.BlockSpec(memory_space=pltpu.VMEM)


def fast_body(old_field, old_source, diffusivity, target_box, neighbours):
    count, side, plane = old_field.shape
    half = plane // 2
    lanes, nodes = lax.axis_size("lane"), lax.axis_size("node")
    lane, node = lax.axis_index("lane"), lax.axis_index("node")
    me = jnp.stack([node, lane, node * lanes + lane]).astype(jnp.int32)
    moves, plan = lane_plan(lanes)
    covered = lanes == 8 and nodes == 4
    units = [(3 * count if bulk is not None else 0) + 2 * len(kept) + 1 for bulk, kept in plan.values()]
    sent = sum(units)
    f32 = jnp.float32
    packed = pl.pallas_call(
        lambda *refs: pack_kernel(moves, plan, lanes, count, *refs),
        name="pack_moves",
        out_shape=[jax.ShapeDtypeStruct((n, side, half), f32) for n in units]
        + [jax.ShapeDtypeStruct((5, count), jnp.int32), jax.ShapeDtypeStruct((8, 128), f32)],
        in_specs=[SCALARS] * 3 + [ANY] * 3,
        out_specs=[ANY] * len(units) + [SCALARS, VECTORS],
        scratch_shapes=[pltpu.SemaphoreType.DMA((sent,))],
    )(me, target_box, neighbours, old_field, old_source, diffusivity)
    messages, labels, own_table = packed[:-2], packed[-2], packed[-1]
    got = [
        lax.ppermute(message, "lane", [(i, (i + offset) % lanes) for i in range(lanes)])
        for offset, message in zip(plan, messages)
    ]
    width = 4 * half
    strips = BZB * 2 * (width // 128) + 1
    block, upward, downward, row_table = pl.pallas_call(
        lambda *refs: assemble_kernel(moves, plan, lanes, count, *refs),
        name="assemble_block",
        out_shape=[
            jax.ShapeDtypeStruct((3, BZB, BXD * side, width), f32),
            jax.ShapeDtypeStruct((strips, 8, 128), f32),
            jax.ShapeDtypeStruct((strips, 8, 128), f32),
            jax.ShapeDtypeStruct((8, 128), f32),
        ],
        in_specs=[SCALARS, VECTORS] + [ANY] * (3 + len(units)),
        out_specs=[VECTORS] * 4,
        scratch_shapes=[
            pltpu.SMEM((len(units), 8, 128), f32),
            pltpu.VMEM((8, 8, 128), f32),
            pltpu.SemaphoreType.DMA,
            pltpu.SemaphoreType.DMA((len(units),)),
            pltpu.SemaphoreType.DMA((8,)),
        ],
    )(labels, own_table, old_field, old_source, diffusivity, *got)
    from_below = lax.ppermute(upward, "node", [(i, (i + 1) % nodes) for i in range(nodes)])
    from_above = lax.ppermute(downward, "node", [(i, (i - 1) % nodes) for i in range(nodes)])
    two_on = lax.ppermute(row_table, "node", [(i, (i + 2) % nodes) for i in range(nodes)])
    tall = BXD * side + 4 * PAD
    big = pltpu.VMEM((BZB, tall, width), f32)
    smoothed, coarse, flag = pl.pallas_call(
        lambda *refs: smooth_kernel(lanes, nodes, covered, *refs),
        name="smooth_block",
        out_shape=[
            jax.ShapeDtypeStruct((count, side, plane), f32),
            jax.ShapeDtypeStruct((count, (side // 2) ** 3), f32),
            jax.ShapeDtypeStruct((1, 1), jnp.int32),
        ],
        in_specs=[SCALARS] * 2 + [VECTORS] * 5,
        out_specs=[VECTORS, VECTORS, SCALARS],
        scratch_shapes=[big] * 9 + [pltpu.VMEM((BZB, BXD * side, width), f32), big, pltpu.VMEM((plane // 128, count * side, 128), f32)],
        compiler_params=pltpu.CompilerParams(vmem_limit_bytes=48 * 2**20),
    )(me, labels, block, from_below, from_above, row_table, two_on)
    irregular = flag[0, 0]
    if not covered:
        irregular = lax.pmax(irregular, ("node", "lane"))

    def again(carry):
        out = general_body(old_field, old_source, diffusivity, target_box, neighbours)
        return (*out, jnp.int32(0))

    smoothed, coarse, _ = lax.while_loop(lambda carry: carry[2] > 0, again, (smoothed, coarse, irregular))
    return smoothed, coarse


def solution(mesh):
    in_specs = (
        P(("node", "lane"), None, None),
        P(("node", "lane"), None, None),
        P(("node", "lane"), None, None),
        P(("node", "lane")),
        P(("node", "lane"), None),
    )
    out_specs = (P(("node", "lane"), None, None), P(("node", "lane"), None))
    return jax.shard_map(fast_body, mesh=mesh, in_specs=in_specs, out_specs=out_specs, check_vma=False)
```

```python
import jax
import jax.numpy as jnp
from jax import lax
from jax.experimental import pallas as pl
from jax.experimental.pallas import tpu as pltpu
from jax.sharding import PartitionSpec as P

SWEEPS = 2


OPPOSITE = (1, 0, 3, 2, 5, 4)


def with_halo(block, sides, width):
    for axis, dim in sides:
        count = lax.axis_size(axis)
        forward = [(i, i + 1) for i in range(count - 1)]
        backward = [(target, source) for source, target in forward]
        low = lax.ppermute(
            lax.slice_in_dim(block, block.shape[dim] - width, None, axis=dim), axis, forward
        )
        high = lax.ppermute(lax.slice_in_dim(block, 0, width, axis=dim), axis, backward)
        block = jnp.concatenate([low, block, high], axis=dim)
    return block


def face_layers(values):
    boxes, side, plane = values.shape
    return jnp.stack(
        [
            values[:, 0],
            values[:, side - 1],
            values[:, :, :side].reshape(boxes, plane),
            values[:, :, plane - side :].reshape(boxes, plane),
            values[:, :, 0::side].reshape(boxes, plane),
            values[:, :, side - 1 :: side].reshape(boxes, plane),
        ],
        axis=1,
    )


def near_values(values, ghost):
    boxes, side, plane = values.shape
    lower_x = jnp.concatenate([ghost[:, 0][:, None, :], values[:, :-1]], axis=1)
    upper_x = jnp.concatenate([values[:, 1:], ghost[:, 1][:, None, :]], axis=1)
    lower_y = jnp.concatenate(
        [ghost[:, 2].reshape(boxes, side, side), values[:, :, : plane - side]], axis=2
    )
    upper_y = jnp.concatenate([values[:, :, side:], ghost[:, 3].reshape(boxes, side, side)], axis=2)
    depth = jnp.arange(plane) % side
    lower_z = jnp.where(
        depth == 0,
        jnp.repeat(ghost[:, 4].reshape(boxes, side, side), side, axis=2),
        jnp.roll(values, 1, axis=2),
    )
    upper_z = jnp.where(
        depth == side - 1,
        jnp.repeat(ghost[:, 5].reshape(boxes, side, side), side, axis=2),
        jnp.roll(values, -1, axis=2),
    )
    return [lower_x, upper_x, lower_y, upper_y, lower_z, upper_z]


def coefficients(diffusivity, beside):
    return [2.0 * diffusivity * other / (diffusivity + other) for other in beside]


def relax(values, source, couplings, beside, chosen):
    total = couplings[0]
    summed = source + couplings[0] * beside[0]
    for face in range(1, 6):
        total = total + couplings[face]
        summed = summed + couplings[face] * beside[face]
    return jnp.where(chosen, summed / total, values)


def defect_of(values, source, couplings, beside):
    total = couplings[0]
    summed = source + couplings[0] * beside[0]
    for face in range(1, 6):
        total = total + couplings[face]
        summed = summed + couplings[face] * beside[face]
    return summed - total * values


def colour_of(side, plane):
    rows = jnp.arange(side)[:, None]
    cells = jnp.arange(plane)[None, :]
    return (rows + cells // side + cells % side) % 2


def restrict(values):
    boxes, side, plane = values.shape
    half = side // 2
    paired = values.reshape(boxes, half, 2, plane).sum(axis=2)
    cells = jnp.arange(plane)
    coarse_cols = cells // side // 2 * half + cells % side // 2
    pooling = (coarse_cols[:, None] == jnp.arange(half * half)[None, :]).astype(jnp.float32)
    summed = jnp.einsum("bxp,pq->bxq", paired, pooling, precision=lax.Precision.HIGHEST)
    return (0.125 * summed).reshape(boxes, half * half * half)


def place(settled, arrived, tags):
    count = settled.shape[0]
    return settled.at[jnp.where(tags > 0, tags - 1, count)].set(arrived, mode="drop")


def general_body(old_field, old_source, diffusivity, target_box, neighbours):
    count, side, plane = old_field.shape
    lane_count = lax.axis_size("lane")
    lane_here = lax.axis_index("lane")
    own_device = lax.axis_index("node") * lane_count + lane_here
    dest_device = target_box // count
    dest_slot = target_box % count
    staying = dest_device == own_device
    cargo = jnp.stack([old_field, old_source], axis=1)
    settled = jnp.zeros_like(cargo).at[jnp.where(staying, dest_slot, count)].set(cargo, mode="drop")
    slots = jnp.arange(count)
    peers = own_device - lane_here + jnp.arange(lane_count)
    chosen = (dest_device[None, :] == peers[:, None]) & jnp.logical_not(staying)[None, :]
    filled = jnp.any(chosen, axis=1)
    picked = jnp.sum(jnp.where(chosen, slots[None, :], 0), axis=1)
    parcels = jnp.where(filled[:, None, None, None], cargo[picked], 0.0)
    labels = jnp.where(filled, jnp.sum(jnp.where(chosen, dest_slot[None, :], 0), axis=1) + 1, 0)
    arrived, tags = (
        lax.all_to_all(parcels, "lane", split_axis=0, concat_axis=0, tiled=True),
        lax.all_to_all(labels, "lane", split_axis=0, concat_axis=0, tiled=True),
    )
    settled = place(settled, arrived, tags)
    field = settled[:, 0]
    source = settled[:, 1]
    present = neighbours >= 0
    near_device = jnp.where(present, neighbours // count, own_device)
    local_row = neighbours % count * 6 + jnp.array(OPPOSITE, jnp.int32)[None, :]
    across = near_device - own_device
    anchor = jnp.where(
        across == -lane_count,
        1,
        jnp.where(
            across == lane_count, 2, jnp.where(across == -1, 3, jnp.where(across == 1, 4, 0))
        ),
    )
    index = anchor * (count * 6) + local_row
    width_out = count * 6

    def departing_boxes(layers):
        return layers.reshape(count * 6, plane)

    def incoming(received, start):
        return jnp.concatenate(
            [
                received[0, 1, start : start + width_out],
                received[2, 1, start : start + width_out],
                received[1, 0, start : start + width_out],
                received[1, 2, start : start + width_out],
            ],
            axis=0,
        )

    def trade(rows):
        return with_halo(rows[None, None], (("node", 0), ("lane", 1)), 1)

    def ghosts(layers, remote_rows, fallback):
        table = jnp.concatenate([layers.reshape(count * 6, plane), remote_rows], axis=0)
        return jnp.where(present[..., None], table[index], fallback)

    beta_layers = face_layers(diffusivity)
    layers = face_layers(field)
    received = trade(
        jnp.concatenate([departing_boxes(layers), departing_boxes(beta_layers)], axis=0)
    )
    beta_ghost = ghosts(beta_layers, incoming(received, width_out), beta_layers)
    couplings = coefficients(diffusivity, near_values(diffusivity, beta_ghost))
    colour = colour_of(side, plane)
    for sweep in range(SWEEPS):
        for colour_id in (0, 1):
            if sweep + colour_id > 0:
                layers = face_layers(field)
                received = trade(departing_boxes(layers))
            ghost = ghosts(layers, incoming(received, 0), jnp.zeros_like(layers))
            field = relax(field, source, couplings, near_values(field, ghost), colour == colour_id)
    layers = face_layers(field)
    received = trade(departing_boxes(layers))
    ghost = ghosts(layers, incoming(received, 0), jnp.zeros_like(layers))
    coarse = restrict(defect_of(field, source, couplings, near_values(field, ghost)))
    return (field, coarse)


BXD = 2
BZB = 4
PAD = 8
LOW, HIGH = "low", "high"


def lane_plan(lanes):
    half = lanes // 2
    moves = [1, lanes - 1, 2, lanes - 2, half]
    singles = {}

    def add(offset, move, part):
        if offset % lanes:
            singles.setdefault(offset % lanes, []).append((move, part))

    for move in moves:
        add(move, move, LOW)
        add(move, move, HIGH)
        add(move + 1, move, HIGH)
        add(move - 1, move, LOW)
    bulk = {1: HIGH, lanes - 1: LOW}
    plan = {}
    for offset in sorted(singles):
        kept = [item for item in singles[offset] if not (item[0] == offset and item[1] == bulk.get(offset))]
        plan[offset] = (bulk.get(offset), kept)
    return moves, plan


def part_lanes(part, plane):
    return slice(0, plane // 2) if part == LOW else slice(plane // 2, plane)


def pack_kernel(moves, plan, lanes, count, *refs):
    target, near, field, source, beta = refs[:5]
    outs = refs[5 : 5 + len(plan)]
    labels, table = refs[5 + len(plan) :]
    side, plane = field.shape[1:]
    half = plane // 2
    for out, (bulk, kept) in zip(outs, plan.values()):
        if bulk is not None:
            for at, array in enumerate((field, source, beta)):
                out[at * count : (at + 1) * count] = array[:, :, part_lanes(bulk, plane)]
    lane = lax.axis_index("lane")
    first = (lax.axis_index("node") * lanes + lane) * count
    old_index = [jnp.int32(0)] * len(moves)
    new_slot = [jnp.int32(-1)] * len(moves)
    stay = []
    for i in range(count):
        there = target[i]
        slot = lax.rem(there, count)
        step = lax.rem(lax.rem(lax.div(there, count), lanes) - lane + lanes, lanes)
        stay.append(jnp.where(step == 0, slot, -1))
        for k, move in enumerate(moves):
            old_index[k] = jnp.where(step == move, i, old_index[k])
            new_slot[k] = jnp.where(step == move, slot, new_slot[k])
    for out, (bulk, kept) in zip(outs, plan.values()):
        unit = 3 * count if bulk is not None else 0
        for move, part in kept:
            box = old_index[moves.index(move)]
            for array in (field, source):
                out[unit] = array[box, :, part_lanes(part, plane)]
                unit += 1
    for i in range(count):
        labels[1, i] = -1

    def local(index, face):
        there = near[index, face]
        inside = (there >= first) & (there < first + count)
        return inside, jnp.clip(there - first, 0, count - 1)

    place = []
    for i in range(count):
        inside, below = local(i, 0)
        depth = jnp.int32(0)
        live, at = local(i, 4)
        for _ in range(BZB - 1):
            depth = depth + jnp.where(live, 1, 0)
            further, onward = local(at, 4)
            live, at = live & further, onward
        spot = jnp.where(inside, BZB, 0) + depth
        place.append((depth, jnp.where(inside, side, 0)))
        deep, row = depth, jnp.where(inside, side, 0)
        labels[0, i] = deep
        labels[5, i] = row
        labels[1, spot] = i
        labels[3, i] = stay[i]
    for k in range(len(moves)):
        labels[2, k] = new_slot[k]
        labels[4, k] = old_index[k]
    rows = lax.broadcasted_iota(jnp.int32, (8, 128), 0)
    cols = lax.broadcasted_iota(jnp.int32, (8, 128), 1)
    spots = rows * 128 + cols
    held = jnp.zeros((8, 128), jnp.int32)

    def put(held, row, col, value):
        return jnp.where(spots == row * 128 + col, value, held)

    for i in range(count):
        slot = labels[1, i]
        held = put(held, i, 0, jnp.where(slot < 0, -7, first + slot))
        for face in range(6):
            held = put(held, i, 1 + face, near[jnp.maximum(slot, 0), face])
        held = put(held, i, 7, place[i][0])
        held = put(held, i, 11, place[i][1])
        held = put(held, i, 9, stay[i])
    for k in range(len(moves)):
        held = put(held, k, 8, new_slot[k])
        held = put(held, k, 10, old_index[k])
    table[...] = held.astype(jnp.float32)
    for out in outs:
        out[out.shape[0] - 1, 0:8] = table[...]


def assemble_kernel(moves, plan, lanes, count, *refs):
    labels, own_table, field, source, beta = refs[:5]
    got = dict(zip(plan, refs[5 : 5 + len(plan)]))
    block, upward, downward, row_table, tables, table_sems = refs[5 + len(plan) :]
    side, plane = field.shape[1:]
    half = plane // 2
    order = list(plan)

    def table_of(offset):
        return got[offset].at[got[offset].shape[0] - 1, 0:8]

    fetch = [
        pltpu.make_async_copy(table_of(offset), tables.at[k], table_sems.at[k]) for k, offset in enumerate(order)
    ]
    for copy in fetch:
        copy.start()

    def put(array, spot, where, values):
        deep, row = spot
        block[array, deep, pl.ds(pl.multiple_of(row, side), side), where] = values

    def checked(slot, spot):
        return jnp.where(slot >= 0, spot[0], BZB), jnp.where(slot >= 0, spot[1], 0)

    own_half = {LOW: slice(half, 2 * half), HIGH: slice(2 * half, 3 * half)}
    low_halo, high_halo = slice(0, half), slice(3 * half, 4 * half)
    whole = slice(half, 3 * half)
    old = (field, source)

    def spot_here(slot):
        at = jnp.maximum(slot, 0)
        return checked(slot, (labels[0, at], labels[5, at]))

    for i in range(count):
        put(2, (labels[0, i], labels[5, i]), whole, beta[i])
        spot = spot_here(labels[3, i])
        for a in range(2):
            put(a, spot, whole, old[a][i])

    cols = lax.broadcasted_iota(jnp.int32, (8, 128), 1)
    shown = [offset for offset in plan if lanes == 8 or offset in (1, lanes - 1)]
    joined = jnp.where(cols < 8, own_table[...], 0.0)
    for offset in shown:
        at = offset if offset < 7 else 7
        joined = joined + pltpu.roll(jnp.where(cols < 8, table_of(offset)[...], 0.0), 8 * at, 1)
    joined = joined + pltpu.roll(joined, 64, 1)
    row_table[...] = joined
    upward[upward.shape[0] - 1] = joined
    downward[downward.shape[0] - 1] = joined

    for copy in fetch:
        copy.wait()

    def said(offset, row, col):
        return tables[order.index(offset), row, col].astype(jnp.int32)

    below, above = 1, lanes - 1

    def spot_at(offset, slot):
        at = jnp.maximum(slot, 0)
        return checked(slot, (said(offset, at, 7), said(offset, at, 11)))

    for move, part, halo, there in ((1, LOW, high_halo, above), (lanes - 1, HIGH, low_halo, below)):
        k = moves.index(move)
        spot = spot_at(there, labels[2, k])
        for a in range(2):
            put(a, spot, halo, old[a][labels[4, k], :, part_lanes(part, plane)])

    for offset, (bulk, kept) in plan.items():
        message = got[offset]
        unit = 0
        if bulk is not None:
            halo = low_halo if offset == below else high_halo
            for i in range(count):
                put(2, (said(offset, i, 7), said(offset, i, 11)), halo, message[2 * count + i])
                spot = spot_at(offset, said(offset, i, 9))
                for a in range(2):
                    put(a, spot, halo, message[a * count + i])
            k = moves.index(offset)
            spot, box = spot_here(said(offset, k, 8)), said(offset, k, 10)
            for a in range(2):
                put(a, spot, own_half[bulk], message[a * count + box])
            unit = 3 * count
        for move, part in kept:
            slot = said(offset, moves.index(move), 8)
            apart = (move - offset) % lanes
            if apart == 0:
                spot, where = spot_here(slot), own_half[part]
            elif apart == 1:
                spot, where = spot_at(above, slot), high_halo
            else:
                spot, where = spot_at(below, slot), low_halo
            for a in range(2):
                put(a, spot, where, message[unit + a])
            unit += 2

    width = block.shape[3]
    levels = lax.broadcasted_iota(jnp.int32, (8, width), 0)
    last = block.shape[2] - 8
    for deep in range(BZB):
        a, b, c = (block[k, deep, last : last + 8] for k in range(3))
        up_first = jnp.where(levels < 3, pltpu.roll(b, 3, 0), a)
        up_second = jnp.where(levels == 0, pltpu.roll(b, 4, 0), c)
        a, b, c = (block[k, deep, 0:8] for k in range(3))
        down_first = jnp.where(levels >= 5, pltpu.roll(b, 5, 0), a)
        down_second = jnp.where(levels == 7, pltpu.roll(b, 4, 0), c)
        for k in range(width // 128):
            cut = slice(k * 128, (k + 1) * 128)
            at = deep * 2 * (width // 128) + k
            upward[at] = up_first[:, cut]
            upward[at + width // 128] = up_second[:, cut]
            downward[at] = down_first[:, cut]
            downward[at + width // 128] = down_second[:, cut]


def smooth_kernel(lanes, nodes, covered, labels, block, from_below, from_above, row_table, two_on, smoothed, coarse, flag,
                  f, s, b, xl, xu, yl, yu, zl, zu, total, inverse, rest):
    width = block.shape[3]
    own_rows = block.shape[2]
    side = smoothed.shape[1]
    plane = smoothed.shape[2]
    half = plane // 2
    tiles = width // 128
    node, lane = lax.axis_index("node"), lax.axis_index("lane")
    first_node, last_node = node == 0, node == nodes - 1
    first_lane, last_lane = lane == 0, lane == lanes - 1
    top = 2 * PAD + own_rows
    rows8 = lax.broadcasted_iota(jnp.int32, (8, width), 0)
    cols = lax.broadcasted_iota(jnp.int32, (8, width), 1)
    depth = lax.rem(cols, side)
    at_front, at_back = depth == 0, depth == side - 1
    colour = lax.rem(rows8 + lax.div(cols, side) + depth, 2)

    zero, one = jnp.zeros((8, width), jnp.float32), jnp.ones((8, width), jnp.float32)
    for deep in range(BZB):
        for rows in (slice(0, 8), slice(top + 8, top + 16)):
            f[deep, rows] = zero
            b[deep, rows] = one
            xu[deep, rows] = zero
        f[deep, 2 * PAD : top] = block[0, deep]
        b[deep, 2 * PAD : top] = block[2, deep]
        s[deep, 2 * PAD : top] = block[1, deep]
        for message, start, below in ((from_below, PAD, True), (from_above, top, False)):
            base = deep * 2 * tiles
            first = jnp.concatenate([message[base + k] for k in range(tiles)], axis=1)
            second = jnp.concatenate([message[base + tiles + k] for k in range(tiles)], axis=1)
            if below:
                src = jnp.where(rows8 >= 5, pltpu.roll(first, 5, 0), pltpu.roll(second, 4, 0))
            else:
                src = jnp.where(rows8 < 3, pltpu.roll(first, 3, 0), pltpu.roll(second, 4, 0))
            f[deep, start : start + 8] = first
            b[deep, start : start + 8] = jnp.where(rows8 == (0 if below else 7), 1.0, second)
            s[deep, start : start + 8] = src

    def after(values):
        return pltpu.roll(values, width - side, 1)

    def before(values):
        return pltpu.roll(values, side, 1)

    def beyond_z(values, afters):
        out = []
        for deep in range(BZB):
            joined = values[deep] if deep == 0 else jnp.where(at_back, afters[deep - 1], values[deep])
            out.append(pltpu.roll(joined, 1, 1))
        return out

    def ahead_z(values, befores):
        out = []
        for deep in range(BZB):
            joined = values[deep] if deep == BZB - 1 else jnp.where(at_front, befores[deep + 1], values[deep])
            out.append(pltpu.roll(joined, width - 1, 1))
        return out

    def mean(one_side, other):
        return 2.0 * one_side * other / (one_side + other)

    starts = range(PAD, top + 8, 8)
    low_edge = (cols >= half) & (cols < half + side) & first_lane
    high_edge = (cols >= 3 * half - side) & (cols < 3 * half) & last_lane
    no_link = ((cols >= half - side) & (cols < half) & first_lane) | high_edge
    for r in starts:
        held = [b[deep, r : r + 8] for deep in range(BZB)]
        befores = [before(v) for v in held]
        afters = [after(v) for v in held]
        aheads = ahead_z(held, befores)
        ky = [jnp.where(no_link, 0.0, mean(held[d], afters[d])) for d in range(BZB)]
        kz = [mean(held[d], aheads[d]) for d in range(BZB)]
        kz[BZB - 1] = jnp.where(at_back, 0.0, kz[BZB - 1])
        kzl = beyond_z(kz, [after(v) for v in kz])
        kzl[0] = jnp.where(at_front, 0.0, kzl[0])
        for d in range(BZB):
            kx = mean(held[d], b[d, r + 1 : r + 9])
            if r == PAD:
                kx = jnp.where((rows8 == 7) & first_node, 0.0, kx)
            if r == top - 8:
                kx = jnp.where((rows8 == 7) & last_node, 0.0, kx)
            xu[d, r : r + 8] = kx
            yu[d, r : r + 8] = ky[d]
            yl[d, r : r + 8] = before(ky[d])
            zu[d, r : r + 8] = kz[d]
            zl[d, r : r + 8] = kzl[d]
    for r in starts:
        for d in range(BZB):
            here = slice(r, r + 8)
            kxl = xu[d, r - 1 : r + 7]
            xl[d, here] = kxl
            held = b[d, here]
            whole = kxl + xu[d, here] + yl[d, here] + yu[d, here] + zl[d, here] + zu[d, here]
            whole = whole + jnp.where(low_edge, held, 0.0) + jnp.where(high_edge, held, 0.0)
            if d == 0:
                whole = whole + jnp.where(at_front, held, 0.0)
            if d == BZB - 1:
                whole = whole + jnp.where(at_back, held, 0.0)
            if r == 2 * PAD:
                whole = whole + jnp.where((rows8 == 0) & first_node, held, 0.0)
            if r == top - 8:
                whole = whole + jnp.where((rows8 == 7) & last_node, held, 0.0)
            if 2 * PAD <= r < top:
                total[d, r - 2 * PAD : r - 2 * PAD + 8] = whole
            inverse[d, here] = 1.0 / whole

    def sums(r, held, afters, befores):
        behind = beyond_z(held, afters)
        aheads = ahead_z(held, befores)
        here = slice(r, r + 8)
        out = []
        for d in range(BZB):
            part = s[d, here] + xl[d, here] * f[d, r - 1 : r + 7] + xu[d, here] * f[d, r + 1 : r + 9]
            part = part + (yl[d, here] * befores[d] + yu[d, here] * afters[d])
            out.append(part + (zl[d, here] * behind[d] + zu[d, here] * aheads[d]))
        return out

    for sweep in range(SWEEPS):
        for colour_id in (0, 1):
            chosen = colour == colour_id
            for r in starts:
                held = [f[d, r : r + 8] for d in range(BZB)]
                parts = sums(r, held, [after(v) for v in held], [before(v) for v in held])
                for d in range(BZB):
                    f[d, r : r + 8] = jnp.where(chosen, parts[d] * inverse[d, r : r + 8], held[d])

    for r in range(2 * PAD, top, 8):
        held = [f[d, r : r + 8] for d in range(BZB)]
        parts = sums(r, held, [after(v) for v in held], [before(v) for v in held])
        wide, inner = divmod(r - 2 * PAD, side)
        for d in range(BZB):
            left = parts[d] - total[d, r - 2 * PAD : r - 2 * PAD + 8] * held[d]
            slot = jnp.maximum(labels[1, wide * BZB + d], 0)
            smoothed[slot, inner : inner + 8] = held[d][:, half : 3 * half]
            for k in range(plane // 128):
                cut = slice(half + k * 128, half + (k + 1) * 128)
                rest[k, pl.ds(pl.multiple_of(slot * side + inner, 8), 8), :] = left[:, cut]

    count = smoothed.shape[0]
    small = side // 2
    cells = lax.broadcasted_iota(jnp.int32, (plane, 128), 0)
    slots = lax.broadcasted_iota(jnp.int32, (plane, 128), 1)
    goal = lax.div(lax.div(cells, side), 2) * small + lax.div(lax.rem(cells, side), 2)
    per = small * small
    for pair in range(small * per // 128):
        acc = None
        for inner in range(128 // per):
            i = pair * (128 // per) + inner
            even = [rest[k, pl.ds(2 * i, count, stride=side), :] for k in range(plane // 128)]
            odd = [rest[k, pl.ds(2 * i + 1, count, stride=side), :] for k in range(plane // 128)]
            rows = jnp.concatenate(even, axis=1) + jnp.concatenate(odd, axis=1)
            pooling = (goal + inner * per == slots).astype(jnp.float32)
            term = jnp.dot(rows, pooling, precision=lax.Precision.HIGHEST, preferred_element_type=jnp.float32)
            acc = term if acc is None else acc + term
        coarse[:, pair * 128 : (pair + 1) * 128] = 0.125 * acc

    mine = from_below.shape[0] - 1
    rows1 = lax.broadcasted_iota(jnp.int32, (8, 128), 0)
    cols1 = lax.broadcasted_iota(jnp.int32, (8, 128), 1)
    owner = lax.rem(lax.div(cols1, 8), 8)
    field_of = lax.rem(cols1, 8)
    own, opposite = row_table[...], two_on[...]
    lower, upper = from_below[mine], from_above[mine]
    rows_of = [(own, lower, upper, node), (lower, opposite, own, lax.rem(node + nodes - 1, nodes)),
               (upper, own, opposite, lax.rem(node + 1, nodes)), (opposite, upper, lower, lax.rem(node + 2, nodes))]
    if not covered:
        rows_of = rows_of[:1]
    lane_of = lax.rem(lane - jnp.where(owner > 4, owner - 8, owner) + 2 * lanes, lanes)
    wrong = jnp.zeros((8, 128), jnp.float32)
    for table, low, high, at_node in rows_of:
        turned = pltpu.roll(table, 4, 0)
        at_low = jnp.where(rows1 >= 4, turned, jnp.where(at_node == 0, -1.0, pltpu.roll(low, 4, 0)))
        at_high = jnp.where(rows1 < 4, turned, jnp.where(at_node == nodes - 1, -1.0, pltpu.roll(high, 4, 0)))
        y_low = jnp.where(lane_of == 0, -1.0, pltpu.roll(table, 128 - 8, 1))
        y_high = jnp.where(lane_of == lanes - 1, -1.0, pltpu.roll(table, 8, 1))
        z_low = jnp.where(lax.rem(rows1, BZB) == 0, -1.0, pltpu.roll(table, 1, 0))
        z_high = jnp.where(lax.rem(rows1, BZB) == BZB - 1, -1.0, pltpu.roll(table, 7, 0))
        bad = jnp.where((field_of == 0) & (table < 0), 1.0, 0.0)
        for face, expected in enumerate((at_low, at_high, y_low, y_high, z_low, z_high)):
            differs = table != pltpu.roll(expected, 1 + face, 1)
            bad = bad + jnp.where((field_of == 1 + face) & differs, 1.0, 0.0)
        if not covered:
            bad = jnp.where(owner == 0, bad, 0.0)
        wrong = wrong + bad
    flag[0, 0] = (jnp.sum(wrong) > 0).astype(jnp.int32)


ROOM = pltpu.CompilerParams(vmem_limit_bytes=32 * 2**20)
SCALARS = pl.BlockSpec(memory_space=pltpu.SMEM)
VECTORS = pl.BlockSpec(memory_space=pltpu.VMEM)


def fast_body(old_field, old_source, diffusivity, target_box, neighbours):
    count, side, plane = old_field.shape
    half = plane // 2
    lanes, nodes = lax.axis_size("lane"), lax.axis_size("node")
    moves, plan = lane_plan(lanes)
    covered = lanes == 8 and nodes == 4
    units = [(3 * count if bulk is not None else 0) + 2 * len(kept) + 1 for bulk, kept in plan.values()]
    f32 = jnp.float32
    packed = pl.pallas_call(
        lambda *refs: pack_kernel(moves, plan, lanes, count, *refs),
        name="pack_moves",
        out_shape=[pltpu.VMEM((n, side, half), f32) for n in units]
        + [jax.ShapeDtypeStruct((6, count), jnp.int32), pltpu.VMEM((8, 128), f32)],
        in_specs=[SCALARS] * 2 + [VECTORS] * 3,
        out_specs=[VECTORS] * len(units) + [SCALARS, VECTORS],
        compiler_params=ROOM,
    )(target_box, neighbours, old_field, old_source, diffusivity)
    messages, labels, own_table = packed[:-2], packed[-2], packed[-1]
    got = [
        lax.ppermute(message, "lane", [(i, (i + offset) % lanes) for i in range(lanes)])
        for offset, message in zip(plan, messages)
    ]
    width = 4 * half
    strips = BZB * 2 * (width // 128) + 1
    block, upward, downward, row_table = pl.pallas_call(
        lambda *refs: assemble_kernel(moves, plan, lanes, count, *refs),
        name="assemble_block",
        out_shape=[
            pltpu.VMEM((3, BZB + 1, BXD * side, width), f32),
            pltpu.VMEM((strips, 8, 128), f32),
            pltpu.VMEM((strips, 8, 128), f32),
            pltpu.VMEM((8, 128), f32),
        ],
        in_specs=[SCALARS] + [VECTORS] * (4 + len(units)),
        out_specs=[VECTORS] * 4,
        scratch_shapes=[
            pltpu.SMEM((len(units), 8, 128), f32),
            pltpu.SemaphoreType.DMA((len(units),)),
        ],
        compiler_params=ROOM,
    )(labels, own_table, old_field, old_source, diffusivity, *got)
    from_below = lax.ppermute(upward, "node", [(i, (i + 1) % nodes) for i in range(nodes)])
    from_above = lax.ppermute(downward, "node", [(i, (i - 1) % nodes) for i in range(nodes)])
    two_on = lax.ppermute(row_table, "node", [(i, (i + 2) % nodes) for i in range(nodes)])
    tall = BXD * side + 4 * PAD
    big = pltpu.VMEM((BZB, tall, width), f32)
    smoothed, coarse, flag = pl.pallas_call(
        lambda *refs: smooth_kernel(lanes, nodes, covered, *refs),
        name="smooth_block",
        out_shape=[
            jax.ShapeDtypeStruct((count, side, plane), f32),
            jax.ShapeDtypeStruct((count, (side // 2) ** 3), f32),
            jax.ShapeDtypeStruct((1, 1), jnp.int32),
        ],
        in_specs=[SCALARS] + [VECTORS] * 5,
        out_specs=[VECTORS, VECTORS, SCALARS],
        scratch_shapes=[big] * 9 + [pltpu.VMEM((BZB, BXD * side, width), f32), big, pltpu.VMEM((plane // 128, count * side, 128), f32)],
        compiler_params=ROOM,
    )(labels, block, from_below, from_above, row_table, two_on)
    irregular = flag[0, 0]
    if not covered:
        irregular = lax.pmax(irregular, ("node", "lane"))

    def again(carry):
        out = general_body(old_field, old_source, diffusivity, target_box, neighbours)
        return (*out, jnp.int32(0))

    smoothed, coarse, _ = lax.while_loop(lambda carry: carry[2] > 0, again, (smoothed, coarse, irregular))
    return smoothed, coarse


def solution(mesh):
    in_specs = (
        P(("node", "lane"), None, None),
        P(("node", "lane"), None, None),
        P(("node", "lane"), None, None),
        P(("node", "lane")),
        P(("node", "lane"), None),
    )
    out_specs = (P(("node", "lane"), None, None), P(("node", "lane"), None))
    return jax.shard_map(fast_body, mesh=mesh, in_specs=in_specs, out_specs=out_specs, check_vma=False)
```

```python
import jax
import jax.numpy as jnp
from jax import lax
from jax.experimental import pallas as pl
from jax.experimental.pallas import tpu as pltpu
from jax.sharding import PartitionSpec as P

SWEEPS = 2


OPPOSITE = (1, 0, 3, 2, 5, 4)


def with_halo(block, sides, width):
    for axis, dim in sides:
        count = lax.axis_size(axis)
        forward = [(i, i + 1) for i in range(count - 1)]
        backward = [(target, source) for source, target in forward]
        low = lax.ppermute(
            lax.slice_in_dim(block, block.shape[dim] - width, None, axis=dim), axis, forward
        )
        high = lax.ppermute(lax.slice_in_dim(block, 0, width, axis=dim), axis, backward)
        block = jnp.concatenate([low, block, high], axis=dim)
    return block


def face_layers(values):
    boxes, side, plane = values.shape
    return jnp.stack(
        [
            values[:, 0],
            values[:, side - 1],
            values[:, :, :side].reshape(boxes, plane),
            values[:, :, plane - side :].reshape(boxes, plane),
            values[:, :, 0::side].reshape(boxes, plane),
            values[:, :, side - 1 :: side].reshape(boxes, plane),
        ],
        axis=1,
    )


def near_values(values, ghost):
    boxes, side, plane = values.shape
    lower_x = jnp.concatenate([ghost[:, 0][:, None, :], values[:, :-1]], axis=1)
    upper_x = jnp.concatenate([values[:, 1:], ghost[:, 1][:, None, :]], axis=1)
    lower_y = jnp.concatenate(
        [ghost[:, 2].reshape(boxes, side, side), values[:, :, : plane - side]], axis=2
    )
    upper_y = jnp.concatenate([values[:, :, side:], ghost[:, 3].reshape(boxes, side, side)], axis=2)
    depth = jnp.arange(plane) % side
    lower_z = jnp.where(
        depth == 0,
        jnp.repeat(ghost[:, 4].reshape(boxes, side, side), side, axis=2),
        jnp.roll(values, 1, axis=2),
    )
    upper_z = jnp.where(
        depth == side - 1,
        jnp.repeat(ghost[:, 5].reshape(boxes, side, side), side, axis=2),
        jnp.roll(values, -1, axis=2),
    )
    return [lower_x, upper_x, lower_y, upper_y, lower_z, upper_z]


def coefficients(diffusivity, beside):
    return [2.0 * diffusivity * other / (diffusivity + other) for other in beside]


def relax(values, source, couplings, beside, chosen):
    total = couplings[0]
    summed = source + couplings[0] * beside[0]
    for face in range(1, 6):
        total = total + couplings[face]
        summed = summed + couplings[face] * beside[face]
    return jnp.where(chosen, summed / total, values)


def defect_of(values, source, couplings, beside):
    total = couplings[0]
    summed = source + couplings[0] * beside[0]
    for face in range(1, 6):
        total = total + couplings[face]
        summed = summed + couplings[face] * beside[face]
    return summed - total * values


def colour_of(side, plane):
    rows = jnp.arange(side)[:, None]
    cells = jnp.arange(plane)[None, :]
    return (rows + cells // side + cells % side) % 2


def restrict(values):
    boxes, side, plane = values.shape
    half = side // 2
    paired = values.reshape(boxes, half, 2, plane).sum(axis=2)
    cells = jnp.arange(plane)
    coarse_cols = cells // side // 2 * half + cells % side // 2
    pooling = (coarse_cols[:, None] == jnp.arange(half * half)[None, :]).astype(jnp.float32)
    summed = jnp.einsum("bxp,pq->bxq", paired, pooling, precision=lax.Precision.HIGHEST)
    return (0.125 * summed).reshape(boxes, half * half * half)


def place(settled, arrived, tags):
    count = settled.shape[0]
    return settled.at[jnp.where(tags > 0, tags - 1, count)].set(arrived, mode="drop")


def general_body(old_field, old_source, diffusivity, target_box, neighbours):
    count, side, plane = old_field.shape
    lane_count = lax.axis_size("lane")
    lane_here = lax.axis_index("lane")
    own_device = lax.axis_index("node") * lane_count + lane_here
    dest_device = target_box // count
    dest_slot = target_box % count
    staying = dest_device == own_device
    cargo = jnp.stack([old_field, old_source], axis=1)
    settled = jnp.zeros_like(cargo).at[jnp.where(staying, dest_slot, count)].set(cargo, mode="drop")
    slots = jnp.arange(count)
    peers = own_device - lane_here + jnp.arange(lane_count)
    chosen = (dest_device[None, :] == peers[:, None]) & jnp.logical_not(staying)[None, :]
    filled = jnp.any(chosen, axis=1)
    picked = jnp.sum(jnp.where(chosen, slots[None, :], 0), axis=1)
    parcels = jnp.where(filled[:, None, None, None], cargo[picked], 0.0)
    labels = jnp.where(filled, jnp.sum(jnp.where(chosen, dest_slot[None, :], 0), axis=1) + 1, 0)
    arrived, tags = (
        lax.all_to_all(parcels, "lane", split_axis=0, concat_axis=0, tiled=True),
        lax.all_to_all(labels, "lane", split_axis=0, concat_axis=0, tiled=True),
    )
    settled = place(settled, arrived, tags)
    field = settled[:, 0]
    source = settled[:, 1]
    present = neighbours >= 0
    near_device = jnp.where(present, neighbours // count, own_device)
    local_row = neighbours % count * 6 + jnp.array(OPPOSITE, jnp.int32)[None, :]
    across = near_device - own_device
    anchor = jnp.where(
        across == -lane_count,
        1,
        jnp.where(
            across == lane_count, 2, jnp.where(across == -1, 3, jnp.where(across == 1, 4, 0))
        ),
    )
    index = anchor * (count * 6) + local_row
    width_out = count * 6

    def departing_boxes(layers):
        return layers.reshape(count * 6, plane)

    def incoming(received, start):
        return jnp.concatenate(
            [
                received[0, 1, start : start + width_out],
                received[2, 1, start : start + width_out],
                received[1, 0, start : start + width_out],
                received[1, 2, start : start + width_out],
            ],
            axis=0,
        )

    def trade(rows):
        return with_halo(rows[None, None], (("node", 0), ("lane", 1)), 1)

    def ghosts(layers, remote_rows, fallback):
        table = jnp.concatenate([layers.reshape(count * 6, plane), remote_rows], axis=0)
        return jnp.where(present[..., None], table[index], fallback)

    beta_layers = face_layers(diffusivity)
    layers = face_layers(field)
    received = trade(
        jnp.concatenate([departing_boxes(layers), departing_boxes(beta_layers)], axis=0)
    )
    beta_ghost = ghosts(beta_layers, incoming(received, width_out), beta_layers)
    couplings = coefficients(diffusivity, near_values(diffusivity, beta_ghost))
    colour = colour_of(side, plane)
    for sweep in range(SWEEPS):
        for colour_id in (0, 1):
            if sweep + colour_id > 0:
                layers = face_layers(field)
                received = trade(departing_boxes(layers))
            ghost = ghosts(layers, incoming(received, 0), jnp.zeros_like(layers))
            field = relax(field, source, couplings, near_values(field, ghost), colour == colour_id)
    layers = face_layers(field)
    received = trade(departing_boxes(layers))
    ghost = ghosts(layers, incoming(received, 0), jnp.zeros_like(layers))
    coarse = restrict(defect_of(field, source, couplings, near_values(field, ghost)))
    return (field, coarse)


BXD = 2
BZB = 4
PAD = 8
SIDE = 16
LOW, HIGH = "low", "high"


def lane_plan(lanes):
    half = lanes // 2
    moves = [1, lanes - 1, 2, lanes - 2, half]
    ends = {}
    for move in moves:
        for offset, part in ((move + 1, HIGH), (move - 1, LOW)):
            ends.setdefault(offset % lanes, []).append((move, part))
    bulk = {1: HIGH, lanes - 1: LOW}
    plan = {}
    for offset in sorted(set(moves) | set(ends)):
        if offset:
            plan[offset] = (bulk.get(offset), offset in moves, ends.get(offset, []))
    return moves, plan


def plan_units(count, bulk, whole, kept):
    return (count + count // 2 if bulk is not None else 0) + (3 if whole else 0) + len(kept) + 1


def cell_lanes(side):
    rows = lax.broadcasted_iota(jnp.int32, (side, 128), 0)
    cols = lax.broadcasted_iota(jnp.int32, (side, 128), 1)
    black = lax.rem(rows + lax.div(cols, side) + lax.rem(cols, side), 2) == 1
    return cols, black


def turn(values, shift):
    return pltpu.roll(values, shift % values.shape[-1], values.ndim - 1)


def pack_end(part, field, source, beta):
    side = field.shape[0]
    cols, black = cell_lanes(side)
    y = lax.div(cols, side)
    if part == HIGH:
        pairs = jnp.where(black, field, turn(field, side))
        out = jnp.where(y >= 4, source, pairs)
        out = jnp.where(y == 2, turn(beta, -side), out)
        out = jnp.where(y == 1, turn(pairs, -4 * side), out)
        return jnp.where(y == 0, turn(pairs, side), out)
    pairs = jnp.where(black, field, turn(field, -side))
    out = jnp.where(y < 4, source, pairs)
    out = jnp.where(y == 5, turn(beta, side), out)
    out = jnp.where(y == 6, turn(pairs, 4 * side), out)
    return jnp.where(y == 7, turn(pairs, -side), out)


def unpack_end(part, packed):
    side = packed.shape[0]
    y = lax.div(lax.broadcasted_iota(jnp.int32, packed.shape, 1), side)
    out = packed
    places = ((7, 7), (6, 6), (5, 4), (4, 3)) if part == HIGH else ((0, 1), (1, 2), (2, 4), (3, 5))
    for layer, shift in places:
        out = jnp.where(y == layer, turn(packed, shift * side), out)
    return out


def pack_whole(low, high):
    side = low.shape[0]
    cols, black = cell_lanes(side)
    even = lax.rem(lax.div(cols, side), 2) == 0
    low = jnp.where(black, low, turn(low, -side))
    high = jnp.where(black, high, turn(high, -side))
    return jnp.where(even, low, turn(high, side))


def unpack_whole(packed):
    side = packed.shape[0]
    even = lax.rem(lax.div(lax.broadcasted_iota(jnp.int32, packed.shape, 1), side), 2) == 0
    return jnp.where(even, packed, turn(packed, side)), jnp.where(even, turn(packed, -side), packed)


def part_lanes(part, plane):
    return slice(0, plane // 2) if part == LOW else slice(plane // 2, plane)


def pack_kernel(moves, plan, lanes, count, *refs):
    target, near, field, source, beta = refs[:5]
    outs = refs[5 : 5 + len(plan)]
    labels, table = refs[5 + len(plan) :]
    side, plane = field.shape[1:]
    half = plane // 2
    left = lax.broadcasted_iota(jnp.int32, (side, 128), 1) < 64
    for out, (bulk, whole, kept) in zip(outs, plan.values()):
        if bulk is not None:
            cut = part_lanes(bulk, plane)
            for i in range(count):
                out[i] = pack_end(bulk, field[i, :, cut], source[i, :, cut], beta[i, :, cut])
            for i in range(0, count, 2):
                first, second = beta[i, :, cut], turn(beta[i + 1, :, cut], 64)
                out[count + i // 2] = jnp.where(left, second, first) if bulk == HIGH else jnp.where(left, first, second)
    lane = lax.axis_index("lane")
    first = (lax.axis_index("node") * lanes + lane) * count
    old_index = [jnp.int32(0)] * len(moves)
    new_slot = [jnp.int32(-1)] * len(moves)
    stay = []
    for i in range(count):
        there = target[i]
        slot = lax.rem(there, count)
        step = lax.rem(lax.rem(lax.div(there, count), lanes) - lane + lanes, lanes)
        stay.append(jnp.where(step == 0, slot, -1))
        for k, move in enumerate(moves):
            old_index[k] = jnp.where(step == move, i, old_index[k])
            new_slot[k] = jnp.where(step == move, slot, new_slot[k])
    for (offset, (bulk, whole, kept)), out in zip(plan.items(), outs):
        unit = count + count // 2 if bulk is not None else 0
        low, high = part_lanes(LOW, plane), part_lanes(HIGH, plane)
        if whole:
            box = old_index[moves.index(offset)]
            out[unit] = pack_whole(field[box, :, low], field[box, :, high])
            out[unit + 1] = source[box, :, low]
            out[unit + 2] = source[box, :, high]
            unit += 3
        for move, part in kept:
            box = old_index[moves.index(move)]
            cut = part_lanes(part, plane)
            out[unit] = pack_end(part, field[box, :, cut], source[box, :, cut], field[box, :, cut])
            unit += 1
    for i in range(count):
        labels[1, i] = -1

    def local(index, face):
        there = near[index, face]
        inside = (there >= first) & (there < first + count)
        return inside, jnp.clip(there - first, 0, count - 1)

    place = []
    for i in range(count):
        inside, below = local(i, 0)
        depth = jnp.int32(0)
        live, at = local(i, 4)
        for _ in range(BZB - 1):
            depth = depth + jnp.where(live, 1, 0)
            further, onward = local(at, 4)
            live, at = live & further, onward
        spot = jnp.where(inside, BZB, 0) + depth
        place.append((depth, jnp.where(inside, side, 0)))
        deep, row = depth, jnp.where(inside, side, 0)
        labels[0, i] = deep
        labels[5, i] = row
        labels[1, spot] = i
        labels[3, i] = stay[i]
    for k in range(len(moves)):
        labels[2, k] = new_slot[k]
        labels[4, k] = old_index[k]
    rows = lax.broadcasted_iota(jnp.int32, (8, 128), 0)
    cols = lax.broadcasted_iota(jnp.int32, (8, 128), 1)
    spots = rows * 128 + cols
    held = jnp.zeros((8, 128), jnp.int32)

    def put(held, row, col, value):
        return jnp.where(spots == row * 128 + col, value, held)

    for i in range(count):
        slot = labels[1, i]
        held = put(held, i, 0, jnp.where(slot < 0, -7, first + slot))
        for face in range(6):
            held = put(held, i, 1 + face, near[jnp.maximum(slot, 0), face])
        held = put(held, i, 7, place[i][0])
        held = put(held, i, 11, place[i][1])
        held = put(held, i, 9, stay[i])
    for k in range(len(moves)):
        held = put(held, k, 8, new_slot[k])
        held = put(held, k, 10, old_index[k])
    table[...] = held.astype(jnp.float32)
    for out in outs:
        out[out.shape[0] - 1, 0:8] = table[...]


def assemble_kernel(moves, plan, lanes, count, *refs):
    labels, own_table, field, source, beta = refs[:5]
    got = dict(zip(plan, refs[5 : 5 + len(plan)]))
    block, upward, downward, row_table, tables, table_sems = refs[5 + len(plan) :]
    side, plane = field.shape[1:]
    half = plane // 2
    order = list(plan)

    def table_of(offset):
        return got[offset].at[got[offset].shape[0] - 1, 0:8]

    fetch = [
        pltpu.make_async_copy(table_of(offset), tables.at[k], table_sems.at[k]) for k, offset in enumerate(order)
    ]
    for copy in fetch:
        copy.start()

    def put(array, spot, where, values):
        deep, row = spot
        block[array, deep, pl.ds(pl.multiple_of(row, side), side), where] = values

    def checked(slot, spot):
        return jnp.where(slot >= 0, spot[0], BZB), jnp.where(slot >= 0, spot[1], 0)

    own_half = {LOW: slice(half, 2 * half), HIGH: slice(2 * half, 3 * half)}
    low_halo, high_halo = slice(0, half), slice(3 * half, 4 * half)
    whole = slice(half, 3 * half)
    old = (field, source)

    def spot_here(slot):
        at = jnp.maximum(slot, 0)
        return checked(slot, (labels[0, at], labels[5, at]))

    for i in range(count):
        put(2, (labels[0, i], labels[5, i]), whole, beta[i])
        spot = spot_here(labels[3, i])
        for a in range(2):
            put(a, spot, whole, old[a][i])

    cols = lax.broadcasted_iota(jnp.int32, (8, 128), 1)
    shown = [offset for offset in plan if lanes == 8 or offset in (1, lanes - 1)]
    joined = jnp.where(cols < 8, own_table[...], 0.0)
    for offset in shown:
        at = offset if offset < 7 else 7
        joined = joined + pltpu.roll(jnp.where(cols < 8, table_of(offset)[...], 0.0), 8 * at, 1)
    joined = joined + pltpu.roll(joined, 64, 1)
    row_table[...] = joined
    upward[upward.shape[0] - 1] = joined
    downward[downward.shape[0] - 1] = joined

    for copy in fetch:
        copy.wait()

    def said(offset, row, col):
        return tables[order.index(offset), row, col].astype(jnp.int32)

    below, above = 1, lanes - 1

    def spot_at(offset, slot):
        at = jnp.maximum(slot, 0)
        return checked(slot, (said(offset, at, 7), said(offset, at, 11)))

    for move, part, halo, there in ((1, LOW, high_halo, above), (lanes - 1, HIGH, low_halo, below)):
        k = moves.index(move)
        spot = spot_at(there, labels[2, k])
        for a in range(2):
            put(a, spot, halo, old[a][labels[4, k], :, part_lanes(part, plane)])

    left = lax.broadcasted_iota(jnp.int32, (side, 128), 1) < 64
    y = lax.div(lax.broadcasted_iota(jnp.int32, (side, 128), 1), side)
    for offset, (bulk, entire, kept) in plan.items():
        message = got[offset]
        unit = 0
        if bulk is not None:
            halo = low_halo if offset == below else high_halo
            for i in range(count):
                packed = message[i]
                spot = spot_at(offset, said(offset, i, 9))
                put(0, spot, halo, unpack_end(bulk, packed))
                put(1, spot, halo, packed)
                joint = message[count + i // 2]
                if bulk == HIGH:
                    layers = joint if i % 2 == 0 else turn(joint, 64)
                    layers = jnp.where(y == 3, turn(packed, side), jnp.where(y < 3, 1.0, layers))
                else:
                    layers = joint if i % 2 == 0 else turn(joint, 64)
                    layers = jnp.where(y == 4, turn(packed, -side), jnp.where(y > 4, 1.0, layers))
                put(2, (said(offset, i, 7), said(offset, i, 11)), halo, layers)
            unit = count + count // 2
        if entire:
            spot = spot_here(said(offset, moves.index(offset), 8))
            low, high = unpack_whole(message[unit])
            put(0, spot, own_half[LOW], low)
            put(0, spot, own_half[HIGH], high)
            put(1, spot, own_half[LOW], message[unit + 1])
            put(1, spot, own_half[HIGH], message[unit + 2])
            unit += 3
        for move, part in kept:
            slot = said(offset, moves.index(move), 8)
            if part == LOW:
                spot, where = spot_at(above, slot), high_halo
            else:
                spot, where = spot_at(below, slot), low_halo
            put(0, spot, where, unpack_end(part, message[unit]))
            put(1, spot, where, message[unit])
            unit += 1

    width = block.shape[3]
    last = block.shape[2] - 8
    for message, start, up in ((upward, last, True), (downward, 0, False)):
        for deep in range(0, BZB, 2):
            tiles = []
            sources = []
            for d in (deep, deep + 1):
                f, s, b = (block[k, d, start : start + 8] for k in range(3))
                tiles.append(pack_rows(up, f, b))
                sources.append(s)
            tiles.append(pack_sources(up, *sources))
            for k, tile in enumerate(tiles):
                at = (deep // 2 * 3 + k) * 3
                corner = slice(0, 128), slice(width - 128, width)
                message[at] = jnp.where(left[0:8], tile[:, corner[1]], tile[:, corner[0]])
                message[at + 1] = tile[:, 128:256]
                message[at + 2] = tile[:, 256:384]


def row_colours(width, side):
    rows = lax.broadcasted_iota(jnp.int32, (8, width), 0)
    cols = lax.broadcasted_iota(jnp.int32, (8, width), 1)
    return rows, lax.rem(rows + lax.div(cols, side) + lax.rem(cols, side), 2)


def fall(values, shift):
    return pltpu.roll(values, shift % 8, 0)


def pack_rows(up, field, beta):
    rows, colour = row_colours(field.shape[1], SIDE)
    if up:
        pairs = jnp.where(colour == 1, field, fall(field, 1))
        out = jnp.where(rows == 0, fall(pairs, 1), beta)
        out = jnp.where(rows == 1, fall(pairs, 4), out)
        return jnp.where(rows == 2, fall(pairs, 7), out)
    pairs = jnp.where(colour == 1, field, fall(field, 7))
    out = jnp.where(rows == 7, fall(pairs, 7), beta)
    out = jnp.where(rows == 6, fall(pairs, 4), out)
    return jnp.where(rows == 5, fall(pairs, 1), out)


def unpack_rows(up, tile):
    rows = lax.broadcasted_iota(jnp.int32, tile.shape, 0)
    places = ((7, 7), (6, 6), (5, 4), (4, 3), (3, 1)) if up else ((0, 1), (1, 2), (2, 4), (3, 5), (4, 7))
    field = tile
    for row, shift in places:
        field = jnp.where(rows == row, fall(tile, shift), field)
    beta = jnp.where(rows < 3, 1.0, tile) if up else jnp.where(rows > 4, 1.0, tile)
    return field, beta


def pack_sources(up, first, second):
    rows = lax.broadcasted_iota(jnp.int32, first.shape, 0)
    return jnp.where(rows >= 4, first, fall(second, 4)) if up else jnp.where(rows < 4, first, fall(second, 4))


def smooth_kernel(lanes, nodes, covered, labels, block, from_below, from_above, row_table, two_on, smoothed, coarse, flag,
                  f, s, b, xl, xu, yl, yu, zl, zu, total, inverse, rest):
    width = block.shape[3]
    own_rows = block.shape[2]
    side = smoothed.shape[1]
    plane = smoothed.shape[2]
    half = plane // 2
    node, lane = lax.axis_index("node"), lax.axis_index("lane")
    first_node, last_node = node == 0, node == nodes - 1
    first_lane, last_lane = lane == 0, lane == lanes - 1
    top = 2 * PAD + own_rows
    rows8 = lax.broadcasted_iota(jnp.int32, (8, width), 0)
    cols = lax.broadcasted_iota(jnp.int32, (8, width), 1)
    depth = lax.rem(cols, side)
    at_front, at_back = depth == 0, depth == side - 1
    colour = lax.rem(rows8 + lax.div(cols, side) + depth, 2)

    zero, one = jnp.zeros((8, width), jnp.float32), jnp.ones((8, width), jnp.float32)
    for deep in range(BZB):
        for rows in (slice(0, 8), slice(top + 8, top + 16)):
            f[deep, rows] = zero
            b[deep, rows] = one
            xu[deep, rows] = zero
        f[deep, 2 * PAD : top] = block[0, deep]
        b[deep, 2 * PAD : top] = block[2, deep]
        s[deep, 2 * PAD : top] = block[1, deep]
        for message, start, up in ((from_below, PAD, True), (from_above, top, False)):
            strips = []
            for k in (deep % 2, 2):
                at = (deep // 2 * 3 + k) * 3
                strips.append(jnp.concatenate([message[at], message[at + 1], message[at + 2], message[at]], axis=1))
            f[deep, start : start + 8], b[deep, start : start + 8] = unpack_rows(up, strips[0])
            s[deep, start : start + 8] = strips[1] if deep % 2 == 0 else fall(strips[1], 4)

    def after(values):
        return pltpu.roll(values, width - side, 1)

    def before(values):
        return pltpu.roll(values, side, 1)

    def beyond_z(values, afters):
        out = []
        for deep in range(BZB):
            joined = values[deep] if deep == 0 else jnp.where(at_back, afters[deep - 1], values[deep])
            out.append(pltpu.roll(joined, 1, 1))
        return out

    def ahead_z(values, befores):
        out = []
        for deep in range(BZB):
            joined = values[deep] if deep == BZB - 1 else jnp.where(at_front, befores[deep + 1], values[deep])
            out.append(pltpu.roll(joined, width - 1, 1))
        return out

    def mean(one_side, other):
        return 2.0 * one_side * other / (one_side + other)

    starts = range(PAD, top + 8, 8)
    low_edge = (cols >= half) & (cols < half + side) & first_lane
    high_edge = (cols >= 3 * half - side) & (cols < 3 * half) & last_lane
    no_link = ((cols >= half - side) & (cols < half) & first_lane) | high_edge
    for r in starts:
        held = [b[deep, r : r + 8] for deep in range(BZB)]
        befores = [before(v) for v in held]
        afters = [after(v) for v in held]
        aheads = ahead_z(held, befores)
        ky = [jnp.where(no_link, 0.0, mean(held[d], afters[d])) for d in range(BZB)]
        kz = [mean(held[d], aheads[d]) for d in range(BZB)]
        kz[BZB - 1] = jnp.where(at_back, 0.0, kz[BZB - 1])
        kzl = beyond_z(kz, [after(v) for v in kz])
        kzl[0] = jnp.where(at_front, 0.0, kzl[0])
        for d in range(BZB):
            kx = mean(held[d], b[d, r + 1 : r + 9])
            if r == PAD:
                kx = jnp.where((rows8 == 7) & first_node, 0.0, kx)
            if r == top - 8:
                kx = jnp.where((rows8 == 7) & last_node, 0.0, kx)
            xu[d, r : r + 8] = kx
            yu[d, r : r + 8] = ky[d]
            yl[d, r : r + 8] = before(ky[d])
            zu[d, r : r + 8] = kz[d]
            zl[d, r : r + 8] = kzl[d]
    for r in starts:
        for d in range(BZB):
            here = slice(r, r + 8)
            kxl = xu[d, r - 1 : r + 7]
            xl[d, here] = kxl
            held = b[d, here]
            whole = kxl + xu[d, here] + yl[d, here] + yu[d, here] + zl[d, here] + zu[d, here]
            whole = whole + jnp.where(low_edge, held, 0.0) + jnp.where(high_edge, held, 0.0)
            if d == 0:
                whole = whole + jnp.where(at_front, held, 0.0)
            if d == BZB - 1:
                whole = whole + jnp.where(at_back, held, 0.0)
            if r == 2 * PAD:
                whole = whole + jnp.where((rows8 == 0) & first_node, held, 0.0)
            if r == top - 8:
                whole = whole + jnp.where((rows8 == 7) & last_node, held, 0.0)
            if 2 * PAD <= r < top:
                total[d, r - 2 * PAD : r - 2 * PAD + 8] = whole
            inverse[d, here] = 1.0 / whole

    def sums(r, held, afters, befores):
        behind = beyond_z(held, afters)
        aheads = ahead_z(held, befores)
        here = slice(r, r + 8)
        out = []
        for d in range(BZB):
            part = s[d, here] + xl[d, here] * f[d, r - 1 : r + 7] + xu[d, here] * f[d, r + 1 : r + 9]
            part = part + (yl[d, here] * befores[d] + yu[d, here] * afters[d])
            out.append(part + (zl[d, here] * behind[d] + zu[d, here] * aheads[d]))
        return out

    for sweep in range(SWEEPS):
        for colour_id in (0, 1):
            chosen = colour == colour_id
            for r in starts:
                held = [f[d, r : r + 8] for d in range(BZB)]
                parts = sums(r, held, [after(v) for v in held], [before(v) for v in held])
                for d in range(BZB):
                    f[d, r : r + 8] = jnp.where(chosen, parts[d] * inverse[d, r : r + 8], held[d])

    for r in range(2 * PAD, top, 8):
        held = [f[d, r : r + 8] for d in range(BZB)]
        parts = sums(r, held, [after(v) for v in held], [before(v) for v in held])
        wide, inner = divmod(r - 2 * PAD, side)
        for d in range(BZB):
            left = parts[d] - total[d, r - 2 * PAD : r - 2 * PAD + 8] * held[d]
            slot = jnp.maximum(labels[1, wide * BZB + d], 0)
            smoothed[slot, inner : inner + 8] = held[d][:, half : 3 * half]
            for k in range(plane // 128):
                cut = slice(half + k * 128, half + (k + 1) * 128)
                rest[k, pl.ds(pl.multiple_of(slot * side + inner, 8), 8), :] = left[:, cut]

    count = smoothed.shape[0]
    small = side // 2
    cells = lax.broadcasted_iota(jnp.int32, (plane, 128), 0)
    slots = lax.broadcasted_iota(jnp.int32, (plane, 128), 1)
    goal = lax.div(lax.div(cells, side), 2) * small + lax.div(lax.rem(cells, side), 2)
    per = small * small
    for pair in range(small * per // 128):
        acc = None
        for inner in range(128 // per):
            i = pair * (128 // per) + inner
            even = [rest[k, pl.ds(2 * i, count, stride=side), :] for k in range(plane // 128)]
            odd = [rest[k, pl.ds(2 * i + 1, count, stride=side), :] for k in range(plane // 128)]
            rows = jnp.concatenate(even, axis=1) + jnp.concatenate(odd, axis=1)
            pooling = (goal + inner * per == slots).astype(jnp.float32)
            term = jnp.dot(rows, pooling, precision=lax.Precision.HIGHEST, preferred_element_type=jnp.float32)
            acc = term if acc is None else acc + term
        coarse[:, pair * 128 : (pair + 1) * 128] = 0.125 * acc

    mine = from_below.shape[0] - 1
    rows1 = lax.broadcasted_iota(jnp.int32, (8, 128), 0)
    cols1 = lax.broadcasted_iota(jnp.int32, (8, 128), 1)
    owner = lax.rem(lax.div(cols1, 8), 8)
    field_of = lax.rem(cols1, 8)
    own, opposite = row_table[...], two_on[...]
    lower, upper = from_below[mine], from_above[mine]
    rows_of = [(own, lower, upper, node), (lower, opposite, own, lax.rem(node + nodes - 1, nodes)),
               (upper, own, opposite, lax.rem(node + 1, nodes)), (opposite, upper, lower, lax.rem(node + 2, nodes))]
    if not covered:
        rows_of = rows_of[:1]
    lane_of = lax.rem(lane - jnp.where(owner > 4, owner - 8, owner) + 2 * lanes, lanes)
    wrong = jnp.zeros((8, 128), jnp.float32)
    for table, low, high, at_node in rows_of:
        turned = pltpu.roll(table, 4, 0)
        at_low = jnp.where(rows1 >= 4, turned, jnp.where(at_node == 0, -1.0, pltpu.roll(low, 4, 0)))
        at_high = jnp.where(rows1 < 4, turned, jnp.where(at_node == nodes - 1, -1.0, pltpu.roll(high, 4, 0)))
        y_low = jnp.where(lane_of == 0, -1.0, pltpu.roll(table, 128 - 8, 1))
        y_high = jnp.where(lane_of == lanes - 1, -1.0, pltpu.roll(table, 8, 1))
        z_low = jnp.where(lax.rem(rows1, BZB) == 0, -1.0, pltpu.roll(table, 1, 0))
        z_high = jnp.where(lax.rem(rows1, BZB) == BZB - 1, -1.0, pltpu.roll(table, 7, 0))
        bad = jnp.where((field_of == 0) & (table < 0), 1.0, 0.0)
        for face, expected in enumerate((at_low, at_high, y_low, y_high, z_low, z_high)):
            differs = table != pltpu.roll(expected, 1 + face, 1)
            bad = bad + jnp.where((field_of == 1 + face) & differs, 1.0, 0.0)
        if not covered:
            bad = jnp.where(owner == 0, bad, 0.0)
        wrong = wrong + bad
    flag[0, 0] = (jnp.sum(wrong) > 0).astype(jnp.int32)


ROOM = pltpu.CompilerParams(vmem_limit_bytes=32 * 2**20)
SCALARS = pl.BlockSpec(memory_space=pltpu.SMEM)
VECTORS = pl.BlockSpec(memory_space=pltpu.VMEM)


def fast_body(old_field, old_source, diffusivity, target_box, neighbours):
    count, side, plane = old_field.shape
    half = plane // 2
    lanes, nodes = lax.axis_size("lane"), lax.axis_size("node")
    moves, plan = lane_plan(lanes)
    covered = lanes == 8 and nodes == 4
    units = [plan_units(count, *parts) for parts in plan.values()]
    f32 = jnp.float32
    packed = pl.pallas_call(
        lambda *refs: pack_kernel(moves, plan, lanes, count, *refs),
        name="pack_moves",
        out_shape=[pltpu.VMEM((n, side, half), f32) for n in units]
        + [jax.ShapeDtypeStruct((6, count), jnp.int32), pltpu.VMEM((8, 128), f32)],
        in_specs=[SCALARS] * 2 + [VECTORS] * 3,
        out_specs=[VECTORS] * len(units) + [SCALARS, VECTORS],
        compiler_params=ROOM,
    )(target_box, neighbours, old_field, old_source, diffusivity)
    messages, labels, own_table = packed[:-2], packed[-2], packed[-1]
    got = {}
    early = [offset for offset in plan if offset in moves]
    for offset in early + [offset for offset in plan if offset not in moves]:
        message = messages[list(plan).index(offset)]
        if offset not in moves:
            message, _ = lax.optimization_barrier((message, got[2]))
        got[offset] = lax.ppermute(message, "lane", [(i, (i + offset) % lanes) for i in range(lanes)])
    got = [got[offset] for offset in plan]
    width = 4 * half
    strips = BZB // 2 * 9 + 1
    block, upward, downward, row_table = pl.pallas_call(
        lambda *refs: assemble_kernel(moves, plan, lanes, count, *refs),
        name="assemble_block",
        out_shape=[
            pltpu.VMEM((3, BZB + 1, BXD * side, width), f32),
            pltpu.VMEM((strips, 8, 128), f32),
            pltpu.VMEM((strips, 8, 128), f32),
            pltpu.VMEM((8, 128), f32),
        ],
        in_specs=[SCALARS] + [VECTORS] * (4 + len(units)),
        out_specs=[VECTORS] * 4,
        scratch_shapes=[
            pltpu.SMEM((len(units), 8, 128), f32),
            pltpu.SemaphoreType.DMA((len(units),)),
        ],
        compiler_params=ROOM,
    )(labels, own_table, old_field, old_source, diffusivity, *got)
    from_below = lax.ppermute(upward, "node", [(i, (i + 1) % nodes) for i in range(nodes)])
    from_above = lax.ppermute(downward, "node", [(i, (i - 1) % nodes) for i in range(nodes)])
    two_on = lax.ppermute(row_table, "node", [(i, (i + 2) % nodes) for i in range(nodes)])
    tall = BXD * side + 4 * PAD
    big = pltpu.VMEM((BZB, tall, width), f32)
    smoothed, coarse, flag = pl.pallas_call(
        lambda *refs: smooth_kernel(lanes, nodes, covered, *refs),
        name="smooth_block",
        out_shape=[
            jax.ShapeDtypeStruct((count, side, plane), f32),
            jax.ShapeDtypeStruct((count, (side // 2) ** 3), f32),
            jax.ShapeDtypeStruct((1, 1), jnp.int32),
        ],
        in_specs=[SCALARS] + [VECTORS] * 5,
        out_specs=[VECTORS, VECTORS, SCALARS],
        scratch_shapes=[big] * 9 + [pltpu.VMEM((BZB, BXD * side, width), f32), big, pltpu.VMEM((plane // 128, count * side, 128), f32)],
        compiler_params=ROOM,
    )(labels, block, from_below, from_above, row_table, two_on)
    irregular = flag[0, 0]
    if not covered:
        irregular = lax.pmax(irregular, ("node", "lane"))

    def again(carry):
        out = general_body(old_field, old_source, diffusivity, target_box, neighbours)
        return (*out, jnp.int32(0))

    smoothed, coarse, _ = lax.while_loop(lambda carry: carry[2] > 0, again, (smoothed, coarse, irregular))
    return smoothed, coarse


def solution(mesh):
    in_specs = (
        P(("node", "lane"), None, None),
        P(("node", "lane"), None, None),
        P(("node", "lane"), None, None),
        P(("node", "lane")),
        P(("node", "lane"), None),
    )
    out_specs = (P(("node", "lane"), None, None), P(("node", "lane"), None))
    return jax.shard_map(fast_body, mesh=mesh, in_specs=in_specs, out_specs=out_specs, check_vma=False)
```

```python
import jax
import jax.numpy as jnp
from jax import lax
from jax.experimental import pallas as pl
from jax.experimental.pallas import tpu as pltpu
from jax.sharding import PartitionSpec as P

SWEEPS = 2


OPPOSITE = (1, 0, 3, 2, 5, 4)


def with_halo(block, sides, width):
    for axis, dim in sides:
        count = lax.axis_size(axis)
        forward = [(i, i + 1) for i in range(count - 1)]
        backward = [(target, source) for source, target in forward]
        low = lax.ppermute(
            lax.slice_in_dim(block, block.shape[dim] - width, None, axis=dim), axis, forward
        )
        high = lax.ppermute(lax.slice_in_dim(block, 0, width, axis=dim), axis, backward)
        block = jnp.concatenate([low, block, high], axis=dim)
    return block


def face_layers(values):
    boxes, side, plane = values.shape
    return jnp.stack(
        [
            values[:, 0],
            values[:, side - 1],
            values[:, :, :side].reshape(boxes, plane),
            values[:, :, plane - side :].reshape(boxes, plane),
            values[:, :, 0::side].reshape(boxes, plane),
            values[:, :, side - 1 :: side].reshape(boxes, plane),
        ],
        axis=1,
    )


def near_values(values, ghost):
    boxes, side, plane = values.shape
    lower_x = jnp.concatenate([ghost[:, 0][:, None, :], values[:, :-1]], axis=1)
    upper_x = jnp.concatenate([values[:, 1:], ghost[:, 1][:, None, :]], axis=1)
    lower_y = jnp.concatenate(
        [ghost[:, 2].reshape(boxes, side, side), values[:, :, : plane - side]], axis=2
    )
    upper_y = jnp.concatenate([values[:, :, side:], ghost[:, 3].reshape(boxes, side, side)], axis=2)
    depth = jnp.arange(plane) % side
    lower_z = jnp.where(
        depth == 0,
        jnp.repeat(ghost[:, 4].reshape(boxes, side, side), side, axis=2),
        jnp.roll(values, 1, axis=2),
    )
    upper_z = jnp.where(
        depth == side - 1,
        jnp.repeat(ghost[:, 5].reshape(boxes, side, side), side, axis=2),
        jnp.roll(values, -1, axis=2),
    )
    return [lower_x, upper_x, lower_y, upper_y, lower_z, upper_z]


def coefficients(diffusivity, beside):
    return [2.0 * diffusivity * other / (diffusivity + other) for other in beside]


def relax(values, source, couplings, beside, chosen):
    total = couplings[0]
    summed = source + couplings[0] * beside[0]
    for face in range(1, 6):
        total = total + couplings[face]
        summed = summed + couplings[face] * beside[face]
    return jnp.where(chosen, summed / total, values)


def defect_of(values, source, couplings, beside):
    total = couplings[0]
    summed = source + couplings[0] * beside[0]
    for face in range(1, 6):
        total = total + couplings[face]
        summed = summed + couplings[face] * beside[face]
    return summed - total * values


def colour_of(side, plane):
    rows = jnp.arange(side)[:, None]
    cells = jnp.arange(plane)[None, :]
    return (rows + cells // side + cells % side) % 2


def restrict(values):
    boxes, side, plane = values.shape
    half = side // 2
    paired = values.reshape(boxes, half, 2, plane).sum(axis=2)
    cells = jnp.arange(plane)
    coarse_cols = cells // side // 2 * half + cells % side // 2
    pooling = (coarse_cols[:, None] == jnp.arange(half * half)[None, :]).astype(jnp.float32)
    summed = jnp.einsum("bxp,pq->bxq", paired, pooling, precision=lax.Precision.HIGHEST)
    return (0.125 * summed).reshape(boxes, half * half * half)


def place(settled, arrived, tags):
    count = settled.shape[0]
    return settled.at[jnp.where(tags > 0, tags - 1, count)].set(arrived, mode="drop")


def general_body(old_field, old_source, diffusivity, target_box, neighbours):
    count, side, plane = old_field.shape
    lane_count = lax.axis_size("lane")
    lane_here = lax.axis_index("lane")
    own_device = lax.axis_index("node") * lane_count + lane_here
    dest_device = target_box // count
    dest_slot = target_box % count
    staying = dest_device == own_device
    cargo = jnp.stack([old_field, old_source], axis=1)
    settled = jnp.zeros_like(cargo).at[jnp.where(staying, dest_slot, count)].set(cargo, mode="drop")
    slots = jnp.arange(count)
    peers = own_device - lane_here + jnp.arange(lane_count)
    chosen = (dest_device[None, :] == peers[:, None]) & jnp.logical_not(staying)[None, :]
    filled = jnp.any(chosen, axis=1)
    picked = jnp.sum(jnp.where(chosen, slots[None, :], 0), axis=1)
    parcels = jnp.where(filled[:, None, None, None], cargo[picked], 0.0)
    labels = jnp.where(filled, jnp.sum(jnp.where(chosen, dest_slot[None, :], 0), axis=1) + 1, 0)
    arrived, tags = (
        lax.all_to_all(parcels, "lane", split_axis=0, concat_axis=0, tiled=True),
        lax.all_to_all(labels, "lane", split_axis=0, concat_axis=0, tiled=True),
    )
    settled = place(settled, arrived, tags)
    field = settled[:, 0]
    source = settled[:, 1]
    present = neighbours >= 0
    near_device = jnp.where(present, neighbours // count, own_device)
    local_row = neighbours % count * 6 + jnp.array(OPPOSITE, jnp.int32)[None, :]
    across = near_device - own_device
    anchor = jnp.where(
        across == -lane_count,
        1,
        jnp.where(
            across == lane_count, 2, jnp.where(across == -1, 3, jnp.where(across == 1, 4, 0))
        ),
    )
    index = anchor * (count * 6) + local_row
    width_out = count * 6

    def departing_boxes(layers):
        return layers.reshape(count * 6, plane)

    def incoming(received, start):
        return jnp.concatenate(
            [
                received[0, 1, start : start + width_out],
                received[2, 1, start : start + width_out],
                received[1, 0, start : start + width_out],
                received[1, 2, start : start + width_out],
            ],
            axis=0,
        )

    def trade(rows):
        return with_halo(rows[None, None], (("node", 0), ("lane", 1)), 1)

    def ghosts(layers, remote_rows, fallback):
        table = jnp.concatenate([layers.reshape(count * 6, plane), remote_rows], axis=0)
        return jnp.where(present[..., None], table[index], fallback)

    beta_layers = face_layers(diffusivity)
    layers = face_layers(field)
    received = trade(
        jnp.concatenate([departing_boxes(layers), departing_boxes(beta_layers)], axis=0)
    )
    beta_ghost = ghosts(beta_layers, incoming(received, width_out), beta_layers)
    couplings = coefficients(diffusivity, near_values(diffusivity, beta_ghost))
    colour = colour_of(side, plane)
    for sweep in range(SWEEPS):
        for colour_id in (0, 1):
            if sweep + colour_id > 0:
                layers = face_layers(field)
                received = trade(departing_boxes(layers))
            ghost = ghosts(layers, incoming(received, 0), jnp.zeros_like(layers))
            field = relax(field, source, couplings, near_values(field, ghost), colour == colour_id)
    layers = face_layers(field)
    received = trade(departing_boxes(layers))
    ghost = ghosts(layers, incoming(received, 0), jnp.zeros_like(layers))
    coarse = restrict(defect_of(field, source, couplings, near_values(field, ghost)))
    return (field, coarse)


BXD = 2
BZB = 4
PAD = 8
SIDE = 16
LOW, HIGH = "low", "high"


def lane_plan(lanes):
    half = lanes // 2
    moves = [1, lanes - 1, 2, lanes - 2, half]
    ends = {}
    for move in moves:
        for offset, part in ((move + 1, HIGH), (move - 1, LOW)):
            ends.setdefault(offset % lanes, []).append((move, part))
    bulk = {1: HIGH, lanes - 1: LOW}
    plan = {}
    for offset in sorted(set(moves) | set(ends)):
        if offset:
            plan[offset] = (bulk.get(offset), offset in moves, ends.get(offset, []))
    return moves, plan


def plan_units(count, bulk, whole, kept):
    return (count + count // 2 if bulk is not None else 0) + (3 if whole else 0) + len(kept) + 1


def cell_lanes(side):
    rows = lax.broadcasted_iota(jnp.int32, (side, 128), 0)
    cols = lax.broadcasted_iota(jnp.int32, (side, 128), 1)
    black = lax.rem(rows + lax.div(cols, side) + lax.rem(cols, side), 2) == 1
    return cols, black


def turn(values, shift):
    return pltpu.roll(values, shift % values.shape[-1], values.ndim - 1)


def pack_end(part, field, source, beta):
    side = field.shape[0]
    cols, black = cell_lanes(side)
    y = lax.div(cols, side)
    if part == HIGH:
        pairs = jnp.where(black, field, turn(field, side))
        out = jnp.where(y >= 4, source, pairs)
        out = jnp.where(y == 2, turn(beta, -side), out)
        out = jnp.where(y == 1, turn(pairs, -4 * side), out)
        return jnp.where(y == 0, turn(pairs, side), out)
    pairs = jnp.where(black, field, turn(field, -side))
    out = jnp.where(y < 4, source, pairs)
    out = jnp.where(y == 5, turn(beta, side), out)
    out = jnp.where(y == 6, turn(pairs, 4 * side), out)
    return jnp.where(y == 7, turn(pairs, -side), out)


def unpack_end(part, packed):
    side = packed.shape[0]
    y = lax.div(lax.broadcasted_iota(jnp.int32, packed.shape, 1), side)
    out = packed
    places = ((7, 7), (6, 6), (5, 4), (4, 3)) if part == HIGH else ((0, 1), (1, 2), (2, 4), (3, 5))
    for layer, shift in places:
        out = jnp.where(y == layer, turn(packed, shift * side), out)
    return out


def pack_whole(low, high):
    side = low.shape[0]
    cols, black = cell_lanes(side)
    even = lax.rem(lax.div(cols, side), 2) == 0
    low = jnp.where(black, low, turn(low, -side))
    high = jnp.where(black, high, turn(high, -side))
    return jnp.where(even, low, turn(high, side))


def unpack_whole(packed):
    side = packed.shape[0]
    even = lax.rem(lax.div(lax.broadcasted_iota(jnp.int32, packed.shape, 1), side), 2) == 0
    return jnp.where(even, packed, turn(packed, side)), jnp.where(even, turn(packed, -side), packed)


def part_lanes(part, plane):
    return slice(0, plane // 2) if part == LOW else slice(plane // 2, plane)


def pack_kernel(moves, plan, lanes, count, *refs):
    target, near = refs[:2]
    outs = refs[7 : 7 + len(plan)]
    held_here = refs[7 + len(plan) : 12 + len(plan)]
    table, slots, sems = refs[12 + len(plan) :]
    fetch = [pltpu.make_async_copy(src, dst, sems.at[k]) for k, (src, dst) in enumerate(zip(refs[2:7], held_here))]
    for copy in fetch:
        copy.start()
    field, source, beta = held_here[:3]
    side, plane = field.shape[1:]
    half = plane // 2
    lane = lax.axis_index("lane")
    first = (lax.axis_index("node") * lanes + lane) * count
    old_index = [jnp.int32(0)] * len(moves)
    new_slot = [jnp.int32(-1)] * len(moves)
    stay = []
    for i in range(count):
        there = target[i]
        slot = lax.rem(there, count)
        step = lax.rem(lax.rem(lax.div(there, count), lanes) - lane + lanes, lanes)
        stay.append(jnp.where(step == 0, slot, -1))
        for k, move in enumerate(moves):
            old_index[k] = jnp.where(step == move, i, old_index[k])
            new_slot[k] = jnp.where(step == move, slot, new_slot[k])
    for i in range(count):
        slots[i] = -1

    def local(index, face):
        there = near[index, face]
        inside = (there >= first) & (there < first + count)
        return inside, jnp.clip(there - first, 0, count - 1)

    place = []
    for i in range(count):
        inside, below = local(i, 0)
        depth = jnp.int32(0)
        live, at = local(i, 4)
        for _ in range(BZB - 1):
            depth = depth + jnp.where(live, 1, 0)
            further, onward = local(at, 4)
            live, at = live & further, onward
        spot = jnp.where(inside, BZB, 0) + depth
        place.append((depth, jnp.where(inside, side, 0)))
        slots[spot] = i
    rows = lax.broadcasted_iota(jnp.int32, (8, 128), 0)
    cols = lax.broadcasted_iota(jnp.int32, (8, 128), 1)
    spots = rows * 128 + cols
    held = jnp.zeros((8, 128), jnp.int32)

    def put(held, row, col, value):
        return jnp.where(spots == row * 128 + col, value, held)

    for i in range(count):
        slot = slots[i]
        held = put(held, i, 12, jnp.maximum(slot, 0))
        held = put(held, i, 0, jnp.where(slot < 0, -7, first + slot))
        for face in range(6):
            held = put(held, i, 1 + face, near[jnp.maximum(slot, 0), face])
        held = put(held, i, 7, place[i][0])
        held = put(held, i, 11, place[i][1])
        held = put(held, i, 9, stay[i])
    for k in range(len(moves)):
        held = put(held, k, 8, new_slot[k])
        held = put(held, k, 10, old_index[k])
    table[...] = held.astype(jnp.float32)
    for copy in fetch:
        copy.wait()
    left = lax.broadcasted_iota(jnp.int32, (side, 128), 1) < 64
    for out, (bulk, whole, kept) in zip(outs, plan.values()):
        if bulk is not None:
            cut = part_lanes(bulk, plane)
            for i in range(count):
                out[i] = pack_end(bulk, field[i, :, cut], source[i, :, cut], beta[i, :, cut])
            for i in range(0, count, 2):
                one, two = beta[i, :, cut], turn(beta[i + 1, :, cut], 64)
                out[count + i // 2] = jnp.where(left, two, one) if bulk == HIGH else jnp.where(left, one, two)
    for (offset, (bulk, whole, kept)), out in zip(plan.items(), outs):
        unit = count + count // 2 if bulk is not None else 0
        low, high = part_lanes(LOW, plane), part_lanes(HIGH, plane)
        if whole:
            box = old_index[moves.index(offset)]
            out[unit] = pack_whole(field[box, :, low], field[box, :, high])
            out[unit + 1] = source[box, :, low]
            out[unit + 2] = source[box, :, high]
            unit += 3
        for move, part in kept:
            box = old_index[moves.index(move)]
            cut = part_lanes(part, plane)
            out[unit] = pack_end(part, field[box, :, cut], source[box, :, cut], field[box, :, cut])
            unit += 1
    for out in outs:
        out[out.shape[0] - 1, 0:8] = table[...]


def assemble_kernel(moves, plan, lanes, count, *refs):
    own_table, field, source, beta = refs[:4]
    got = dict(zip(plan, refs[4 : 4 + len(plan)]))
    block, fifth, upward, downward, row_table, low_side, high_side, tables, table_sems = refs[4 + len(plan) :]
    side, plane = field.shape[1:]
    half = plane // 2
    order = list(plan) + [0]

    def table_of(offset):
        return got[offset].at[got[offset].shape[0] - 1, 0:8] if offset else own_table

    fetch = [
        pltpu.make_async_copy(table_of(offset), tables.at[k], table_sems.at[k]) for k, offset in enumerate(order)
    ]
    for copy in fetch:
        copy.start()

    cols = lax.broadcasted_iota(jnp.int32, (8, 128), 1)
    shown = [offset for offset in plan if lanes == 8 or offset in (1, lanes - 1)]
    joined = jnp.where(cols < 8, own_table[...], 0.0)
    for offset in shown:
        at = offset if offset < 7 else 7
        joined = joined + pltpu.roll(jnp.where(cols < 8, table_of(offset)[...], 0.0), 8 * at, 1)
    joined = joined + pltpu.roll(joined, 64, 1)
    row_table[...] = joined
    upward[upward.shape[0] - 1] = joined
    downward[downward.shape[0] - 1] = joined

    for copy in fetch:
        copy.wait()

    def said(offset, row, col):
        return tables[order.index(offset), row, col].astype(jnp.int32)

    def spot_at(offset, slot):
        at = jnp.maximum(slot, 0)
        return jnp.where(slot >= 0, said(offset, at, 7), BZB), jnp.where(slot >= 0, said(offset, at, 11), 0)

    def put(ref, array, spot, values, where=slice(None)):
        deep, row = spot
        ref[array, deep, pl.ds(pl.multiple_of(row, side), side), where] = values

    low, high, whole = slice(0, half), slice(half, plane), slice(0, plane)
    for i in range(count):
        put(block, 2, (said(0, i, 7), said(0, i, 11)), beta[i], whole)
        spot = spot_at(0, said(0, i, 9))
        put(block, 0, spot, field[i], whole)
        put(block, 1, spot, source[i], whole)

    below, above = 1, lanes - 1
    sides = {HIGH: (low_side, below, side), LOW: (high_side, above, -side)}

    def put_end(part, slot, layers, raw, sources):
        ref, offset, shift = sides[part]
        spot = spot_at(offset, slot)
        put(ref, 0, spot, layers)
        put(ref, 1, spot, sources)
        put(ref, 3, spot, turn(raw, shift))

    for move, part in ((1, LOW), (lanes - 1, HIGH)):
        k = moves.index(move)
        box, cut = said(0, k, 10), part_lanes(part, plane)
        raw = field[box, :, cut]
        put_end(part, said(0, k, 8), raw, raw, source[box, :, cut])

    for offset, (bulk, entire, kept) in plan.items():
        message = got[offset]
        unit = 0
        if bulk is not None:
            ref, _, shift = sides[bulk]
            for i in range(count):
                packed = message[i]
                put_end(bulk, said(offset, i, 9), unpack_end(bulk, packed), packed, packed)
                joint = message[count + i // 2]
                spot = said(offset, i, 7), said(offset, i, 11)
                put(ref, 2, spot, joint if i % 2 == 0 else turn(joint, 64))
                put(ref, 4, spot, turn(packed, 2 * shift))
            unit = count + count // 2
        if entire:
            spot = spot_at(0, said(offset, moves.index(offset), 8))
            first, second = unpack_whole(message[unit])
            put(block, 0, spot, first, low)
            put(block, 0, spot, second, high)
            put(block, 1, spot, message[unit + 1], low)
            put(block, 1, spot, message[unit + 2], high)
            unit += 3
        for move, part in kept:
            packed = message[unit]
            put_end(part, said(offset, moves.index(move), 8), unpack_end(part, packed), packed, packed)
            unit += 1

    rows, width = block.shape[2:]
    left = lax.broadcasted_iota(jnp.int32, (rows, 128), 1) < 64
    for d in range(BZB):
        for k in range(3):
            block[k, d, :, plane:width] = jnp.where(left, high_side[k, d], low_side[k, d])
        for k in range(2):
            fifth[k, d] = jnp.where(left, high_side[3 + k, d], low_side[3 + k, d])
    for message, start, up in ((upward, rows - 8, True), (downward, 0, False)):
        for deep in range(0, BZB, 2):
            tiles = []
            sources = []
            for d in (deep, deep + 1):
                f, s, b = (block[k, d, start : start + 8] for k in range(3))
                tiles.append(pack_rows(up, f, b))
                sources.append(s)
            tiles.append(pack_sources(up, *sources))
            for k, tile in enumerate(tiles):
                for part in range(width // 128):
                    message[(deep // 2 * 3 + k) * 3 + part] = tile[:, part * 128 : (part + 1) * 128]


def row_colours(width, side):
    rows = lax.broadcasted_iota(jnp.int32, (8, width), 0)
    cols = lax.broadcasted_iota(jnp.int32, (8, width), 1)
    return rows, lax.rem(rows + lax.div(cols, side) + lax.rem(cols, side), 2)


def fall(values, shift):
    return pltpu.roll(values, shift % 8, 0)


def pack_rows(up, field, beta):
    rows, colour = row_colours(field.shape[1], SIDE)
    if up:
        pairs = jnp.where(colour == 1, field, fall(field, 1))
        out = jnp.where(rows == 0, fall(pairs, 1), beta)
        out = jnp.where(rows == 1, fall(pairs, 4), out)
        return jnp.where(rows == 2, fall(pairs, 7), out)
    pairs = jnp.where(colour == 1, field, fall(field, 7))
    out = jnp.where(rows == 7, fall(pairs, 7), beta)
    out = jnp.where(rows == 6, fall(pairs, 4), out)
    return jnp.where(rows == 5, fall(pairs, 1), out)


def unpack_rows(below, above):
    rows = lax.broadcasted_iota(jnp.int32, below.shape, 0)
    field = fall(above, 1)
    for row, tile, shift in ((1, above, 2), (2, above, 4), (3, above, 5), (4, below, 3), (5, below, 4), (6, below, 6), (7, below, 7)):
        field = jnp.where(rows == row, fall(tile, shift), field)
    beta = jnp.where(rows < 4, above, below)
    fifth_field = jnp.where(rows < 4, fall(above, 6), fall(below, 2))
    fifth_beta = jnp.where(rows < 4, fall(above, 7), fall(below, 1))
    return field, beta, fifth_field, fifth_beta


def pack_sources(up, first, second):
    rows = lax.broadcasted_iota(jnp.int32, first.shape, 0)
    return jnp.where(rows >= 4, first, fall(second, 4)) if up else jnp.where(rows < 4, first, fall(second, 4))


class Stencil:
    def __init__(self, width, side, plane, lanes, nodes):
        self.width, self.side, self.plane = width, side, plane
        node, lane = lax.axis_index("node"), lax.axis_index("lane")
        self.first_node, self.last_node = node == 0, node == nodes - 1
        self.rows, self.colour = row_colours(width, side)
        cols = lax.broadcasted_iota(jnp.int32, (8, width), 1)
        depth = lax.rem(cols, side)
        self.at_front, self.at_back = depth == 0, depth == side - 1
        first_lane, last_lane = lane == 0, lane == lanes - 1
        self.low_edge = (cols < side) & first_lane
        self.high_edge = (cols >= plane - side) & (cols < plane) & last_lane
        self.seam = (cols >= plane + 3 * side) & (cols < plane + 4 * side)
        self.no_link = ((cols >= width - side) & first_lane) | self.high_edge | self.seam

    def after(self, values):
        return pltpu.roll(values, self.width - self.side, 1)

    def before(self, values):
        return pltpu.roll(values, self.side, 1)

    def beyond_z(self, values, afters):
        out = []
        for deep in range(BZB):
            joined = values[deep] if deep == 0 else jnp.where(self.at_back, afters[deep - 1], values[deep])
            out.append(pltpu.roll(joined, 1, 1))
        return out

    def ahead_z(self, values, befores):
        out = []
        for deep in range(BZB):
            joined = values[deep] if deep == BZB - 1 else jnp.where(self.at_front, befores[deep + 1], values[deep])
            out.append(pltpu.roll(joined, self.width - 1, 1))
        return out

    def across(self, held):
        befores = [self.before(v) for v in held]
        afters = [self.after(v) for v in held]
        aheads = self.ahead_z(held, befores)
        ky = [jnp.where(self.no_link, 0.0, mean(held[d], afters[d])) for d in range(BZB)]
        kz = [mean(held[d], aheads[d]) for d in range(BZB)]
        kz[BZB - 1] = jnp.where(self.at_back, 0.0, kz[BZB - 1])
        kzl = self.beyond_z(kz, [self.after(v) for v in kz])
        kzl[0] = jnp.where(self.at_front, 0.0, kzl[0])
        return [self.before(v) for v in ky], ky, kzl, kz

    def edges(self, d, held):
        out = jnp.where(self.low_edge | self.high_edge, held, 0.0)
        if d == 0:
            out = out + jnp.where(self.at_front, held, 0.0)
        if d == BZB - 1:
            out = out + jnp.where(self.at_back, held, 0.0)
        return out

    def sums(self, held, lowers, uppers, coefficient):
        afters = [self.after(v) for v in held]
        befores = [self.before(v) for v in held]
        behind = self.beyond_z(held, afters)
        aheads = self.ahead_z(held, befores)
        out = []
        for d in range(BZB):
            s, xl, xu, yl, yu, zl, zu = coefficient(d)
            part = s + xl * lowers[d] + xu * uppers[d]
            part = part + (yl * befores[d] + yu * afters[d])
            out.append(part + (zl * behind[d] + zu * aheads[d]))
        return out


def mean(one_side, other):
    return 2.0 * one_side * other / (one_side + other)


def couple_kernel(lanes, nodes, plane, block, fifth, f, s, xl, xu, yl, yu, zl, zu, total, inverse):
    width, own_rows = block.shape[3], block.shape[2]
    grid = Stencil(width, SIDE, plane, lanes, nodes)
    cols = lax.broadcasted_iota(jnp.int32, (8, 128), 1)
    seam = (cols >= 3 * SIDE) & (cols < 5 * SIDE)
    for r in range(0, own_rows, 8):
        here = slice(r, r + 8)
        held = [block[2, d, here] for d in range(BZB)]
        across = grid.across(held)
        for ref, values in zip((yl, yu, zl, zu), across):
            for d in range(BZB):
                ref[d, here] = values[d]
        for d in range(BZB):
            f[d, here] = block[0, d, here]
            if r + 8 < own_rows:
                xu[d, here] = mean(held[d], block[2, d, r + 1 : r + 9])
            else:
                xu[d, here] = jnp.where(grid.rows == 7, 0.0, mean(held[d], fall(held[d], 7)))
            link = jnp.where(seam, mean(held[d][:, plane:width], fifth[1, d, here]), 0.0)
            s[d, here, 0:plane] = block[1, d, here, 0:plane]
            s[d, here, plane:width] = block[1, d, here, plane:width] + link * jnp.where(seam, fifth[0, d, here], 0.0)
            part = across[0][d] + across[1][d] + across[2][d] + across[3][d] + grid.edges(d, held[d])
            part = jnp.concatenate([part[:, 0:plane], part[:, plane:width] + link], axis=1)
            if r:
                xl[d, here] = xu[d, r - 1 : r + 7]
            if 0 < r < own_rows - 8:
                part = part + xl[d, here] + xu[d, here]
                inverse[d, here] = 1.0 / part
            total[d, here] = part
    for r in range(8, own_rows - 8, 8):
        here = slice(r, r + 8)
        held = [f[d, here] for d in range(BZB)]
        lowers = [f[d, r - 1 : r + 7] for d in range(BZB)]
        uppers = [f[d, r + 1 : r + 9] for d in range(BZB)]
        parts = grid.sums(held, lowers, uppers, lambda d: tuple(ref[d, here] for ref in (s, xl, xu, yl, yu, zl, zu)))
        for d in range(BZB):
            f[d, here] = jnp.where(grid.colour == 0, parts[d] * inverse[d, here], held[d])


def smooth_kernel(lanes, nodes, covered, own_table, block, own_f, own_s, own_xl, own_xu, own_yl, own_yu, own_zl, own_zu,
                  own_total, own_inverse, from_below, from_above, row_table, two_on, smoothed, coarse, flag,
                  f, s, xl, xu, yl, yu, zl, zu, inverse, end_xl, end_xu, end_total, end_inverse, rest, labels, label_sem):
    width = block.shape[3]
    own_rows = block.shape[2]
    side = smoothed.shape[1]
    plane = smoothed.shape[2]
    node, lane = lax.axis_index("node"), lax.axis_index("lane")
    fetch = pltpu.make_async_copy(own_table, labels, label_sem)
    fetch.start()
    grid = Stencil(width, side, plane, lanes, nodes)
    rows = grid.rows
    halo = PAD + own_rows
    last = own_rows - 8
    halo_beta = []
    for d in range(BZB):
        f[d, PAD:halo] = own_f[d]
        strips = []
        for message in (from_below, from_above):
            for k in (d % 2, 2):
                unit = (d // 2 * 3 + k) * 3
                strips.append(jnp.concatenate([message[unit + part] for part in range(width // 128)], axis=1))
        field, beta, fifth_field, fifth_beta = unpack_rows(strips[0], strips[2])
        f[d, 0:8] = field
        f[d, halo : halo + 8] = field
        source = jnp.where(rows < 4, strips[3], strips[1])
        if d % 2:
            source = jnp.where(rows < 4, fall(strips[3], 4), fall(strips[1], 4))
        link = jnp.where((rows == 3) | (rows == 4), mean(beta, fifth_beta), 0.0)
        s[d] = source + link * fifth_field
        inverse[d] = link
        halo_beta.append(beta)
    across = grid.across(halo_beta)
    for ref, values in zip((yl, yu, zl, zu), across):
        for d in range(BZB):
            ref[d] = values[d]
    for d in range(BZB):
        held = halo_beta[d]
        up = mean(held, jnp.where(rows == 7, fall(block[2, d, 0:8], 7), fall(held, 7)))
        up = jnp.where((rows == 3) | ((rows == 7) & grid.first_node), 0.0, up)
        down = mean(held, fall(block[2, d, last:own_rows], 1))
        down = jnp.where(grid.last_node, 0.0, down)
        down = jnp.where(rows == 0, down, fall(up, 1))
        xl[d], xu[d] = down, up
        whole = inverse[d] + down + up + across[0][d] + across[1][d] + across[2][d] + across[3][d] + grid.edges(d, held)
        inverse[d] = 1.0 / whole
        end_xl[d, 0:8] = jnp.where(rows == 0, fall(up, 1), fall(own_xu[d, 0:8], 1))
        end_xu[d, 0:8] = own_xu[d, 0:8]
        end_xl[d, 8:16] = own_xl[d, last:own_rows]
        end_xu[d, 8:16] = jnp.where(rows == 7, fall(down, 7), own_xu[d, last:own_rows])
        for at, start, absent in (
            (slice(0, 8), 0, (rows == 0) & grid.first_node),
            (slice(8, 16), last, (rows == 7) & grid.last_node),
        ):
            whole = own_total[d, start : start + 8] + end_xl[d, at] + end_xu[d, at]
            whole = whole + jnp.where(absent, block[2, d, start : start + 8], 0.0)
            end_total[d, at] = whole
            end_inverse[d, at] = 1.0 / whole

    ends = {0: slice(0, 8), last: slice(8, 16)}

    def coefficients_at(r):
        here = slice(r, r + 8)
        across = (own_yl, own_yu, own_zl, own_zu)
        if r in ends:
            return lambda d: (own_s[d, here], end_xl[d, ends[r]], end_xu[d, ends[r]]) + tuple(ref[d, here] for ref in across)
        return lambda d: tuple(ref[d, here] for ref in (own_s, own_xl, own_xu) + across)

    def own_sums(r):
        held = [f[d, r + PAD : r + PAD + 8] for d in range(BZB)]
        lowers = [f[d, r + PAD - 1 : r + PAD + 7] for d in range(BZB)]
        uppers = [f[d, r + PAD + 1 : r + PAD + 9] for d in range(BZB)]
        return held, grid.sums(held, lowers, uppers, coefficients_at(r))

    for sweep in range(SWEEPS):
        for colour_id in (0, 1):
            chosen = grid.colour == colour_id
            held = [f[d, 0:8] for d in range(BZB)]
            lowers = [jnp.where(rows == 0, fall(f[d, halo - 8 : halo], 1), fall(held[d], 1)) for d in range(BZB)]
            uppers = [jnp.where(rows == 7, fall(f[d, PAD : PAD + 8], 7), fall(held[d], 7)) for d in range(BZB)]
            parts = grid.sums(held, lowers, uppers, lambda d: tuple(ref[d] for ref in (s, xl, xu, yl, yu, zl, zu)))
            halo_new = [jnp.where(chosen, parts[d] * inverse[d], held[d]) for d in range(BZB)]
            for r in range(0, own_rows, 8):
                if sweep + colour_id == 0 and r not in ends:
                    continue
                held, parts = own_sums(r)
                for d in range(BZB):
                    factor = end_inverse[d, ends[r]] if r in ends else own_inverse[d, r : r + 8]
                    f[d, r + PAD : r + PAD + 8] = jnp.where(chosen, parts[d] * factor, held[d])
            for d in range(BZB):
                f[d, 0:8] = halo_new[d]
                f[d, halo : halo + 8] = halo_new[d]

    fetch.wait()
    for r in range(0, own_rows, 8):
        held, parts = own_sums(r)
        wide, inner = divmod(r, side)
        for d in range(BZB):
            whole = end_total[d, ends[r]] if r in ends else own_total[d, r : r + 8]
            left = parts[d] - whole * held[d]
            slot = labels[wide * BZB + d, 12].astype(jnp.int32)
            smoothed[slot, inner : inner + 8] = held[d][:, 0:plane]
            for k in range(plane // 128):
                rest[k, pl.ds(pl.multiple_of(slot * side + inner, 8), 8), :] = left[:, k * 128 : (k + 1) * 128]

    count = smoothed.shape[0]
    small = side // 2
    cells = lax.broadcasted_iota(jnp.int32, (plane, 128), 0)
    slots = lax.broadcasted_iota(jnp.int32, (plane, 128), 1)
    goal = lax.div(lax.div(cells, side), 2) * small + lax.div(lax.rem(cells, side), 2)
    per = small * small
    acc = 0.0
    pairs = small * per // 128
    for inner in range(128 // per):
        stack = []
        for pair in range(pairs):
            i = pair * (128 // per) + inner
            even = [rest[k, pl.ds(2 * i, count, stride=side), :] for k in range(plane // 128)]
            odd = [rest[k, pl.ds(2 * i + 1, count, stride=side), :] for k in range(plane // 128)]
            stack.append(jnp.concatenate(even, axis=1) + jnp.concatenate(odd, axis=1))
        pooling = (goal + inner * per == slots).astype(jnp.float32)
        acc = acc + jnp.dot(
            jnp.concatenate(stack, axis=0), pooling, precision=lax.Precision.HIGHEST, preferred_element_type=jnp.float32
        )
    for pair in range(pairs):
        coarse[:, pair * 128 : (pair + 1) * 128] = 0.125 * acc[pair * count : (pair + 1) * count]

    mine = from_below.shape[0] - 1
    rows1 = lax.broadcasted_iota(jnp.int32, (8, 128), 0)
    cols1 = lax.broadcasted_iota(jnp.int32, (8, 128), 1)
    owner = lax.rem(lax.div(cols1, 8), 8)
    field_of = lax.rem(cols1, 8)
    table_here, opposite = row_table[...], two_on[...]
    lower, upper = from_below[mine], from_above[mine]
    rows_of = [(table_here, lower, upper, node), (lower, opposite, table_here, lax.rem(node + nodes - 1, nodes)),
               (upper, table_here, opposite, lax.rem(node + 1, nodes)), (opposite, upper, lower, lax.rem(node + 2, nodes))]
    if not covered:
        rows_of = rows_of[:1]
    lane_of = lax.rem(lane - jnp.where(owner > 4, owner - 8, owner) + 2 * lanes, lanes)
    wrong = jnp.zeros((8, 128), jnp.float32)
    for table, low, high, at_node in rows_of:
        turned = pltpu.roll(table, 4, 0)
        at_low = jnp.where(rows1 >= 4, turned, jnp.where(at_node == 0, -1.0, pltpu.roll(low, 4, 0)))
        at_high = jnp.where(rows1 < 4, turned, jnp.where(at_node == nodes - 1, -1.0, pltpu.roll(high, 4, 0)))
        y_low = jnp.where(lane_of == 0, -1.0, pltpu.roll(table, 128 - 8, 1))
        y_high = jnp.where(lane_of == lanes - 1, -1.0, pltpu.roll(table, 8, 1))
        z_low = jnp.where(lax.rem(rows1, BZB) == 0, -1.0, pltpu.roll(table, 1, 0))
        z_high = jnp.where(lax.rem(rows1, BZB) == BZB - 1, -1.0, pltpu.roll(table, 7, 0))
        bad = jnp.where((field_of == 0) & (table < 0), 1.0, 0.0)
        for face, expected in enumerate((at_low, at_high, y_low, y_high, z_low, z_high)):
            differs = table != pltpu.roll(expected, 1 + face, 1)
            bad = bad + jnp.where((field_of == 1 + face) & differs, 1.0, 0.0)
        if not covered:
            bad = jnp.where(owner == 0, bad, 0.0)
        wrong = wrong + bad
    flag[0, 0] = (jnp.sum(wrong) > 0).astype(jnp.int32)


ROOM = pltpu.CompilerParams(vmem_limit_bytes=32 * 2**20)
FULL = pltpu.CompilerParams(vmem_limit_bytes=60 * 2**20)
SCALARS = pl.BlockSpec(memory_space=pltpu.SMEM)
VECTORS = pl.BlockSpec(memory_space=pltpu.VMEM)


def fast_body(old_field, old_source, diffusivity, target_box, neighbours):
    count, side, plane = old_field.shape
    half = plane // 2
    lanes, nodes = lax.axis_size("lane"), lax.axis_size("node")
    arrays = (old_field, old_source, diffusivity, target_box, neighbours)
    moves, plan = lane_plan(lanes)
    covered = lanes == 8 and nodes == 4
    units = [plan_units(count, *parts) for parts in plan.values()]
    f32 = jnp.float32
    packed = pl.pallas_call(
        lambda *refs: pack_kernel(moves, plan, lanes, count, *refs),
        name="pack_moves",
        out_shape=[pltpu.VMEM((n, side, half), f32) for n in units]
        + [pltpu.VMEM(array.shape, array.dtype) for array in arrays]
        + [pltpu.VMEM((8, 128), f32)],
        in_specs=[SCALARS] * 2 + [pl.BlockSpec(memory_space=pltpu.HBM)] * 5,
        out_specs=[VECTORS] * (len(units) + 6),
        scratch_shapes=[pltpu.SMEM((count,), jnp.int32), pltpu.SemaphoreType.DMA((5,))],
        compiler_params=FULL,
    )(target_box, neighbours, *arrays)
    messages, own_table = packed[:-6], packed[-1]
    field, source, beta, target_held, neighbours_held = packed[-6:-1]
    got = {}
    early = [offset for offset in plan if offset in moves]
    for offset in early + [offset for offset in plan if offset not in moves]:
        message = messages[list(plan).index(offset)]
        if offset not in moves:
            message, _ = lax.optimization_barrier((message, got[2]))
        got[offset] = lax.ppermute(message, "lane", [(i, (i + offset) % lanes) for i in range(lanes)])
    got = [got[offset] for offset in plan]
    width = plane + 128
    strips = BZB // 2 * 9 + 1
    sides = pltpu.VMEM((5, BZB + 1, BXD * side, 128), f32)
    block, fifth, upward, downward, row_table = pl.pallas_call(
        lambda *refs: assemble_kernel(moves, plan, lanes, count, *refs),
        name="assemble_block",
        out_shape=[
            pltpu.VMEM((3, BZB + 1, BXD * side, width), f32),
            pltpu.VMEM((2, BZB, BXD * side, 128), f32),
            pltpu.VMEM((strips, 8, 128), f32),
            pltpu.VMEM((strips, 8, 128), f32),
            pltpu.VMEM((8, 128), f32),
        ],
        in_specs=[VECTORS] * (4 + len(units)),
        out_specs=[VECTORS] * 5,
        scratch_shapes=[
            sides,
            sides,
            pltpu.SMEM((len(units) + 1, 8, 128), f32),
            pltpu.SemaphoreType.DMA((len(units) + 1,)),
        ],
        compiler_params=ROOM,
    )(own_table, field, source, beta, *got)
    from_below = lax.ppermute(upward, "node", [(i, (i + 1) % nodes) for i in range(nodes)])
    from_above = lax.ppermute(downward, "node", [(i, (i - 1) % nodes) for i in range(nodes)])
    two_on = lax.ppermute(row_table, "node", [(i, (i + 2) % nodes) for i in range(nodes)])
    own_shape = pltpu.VMEM((BZB, BXD * side, width), f32)
    coupled = pl.pallas_call(
        lambda *refs: couple_kernel(lanes, nodes, plane, *refs),
        name="couple_block",
        out_shape=[own_shape] * 10,
        in_specs=[VECTORS] * 2,
        out_specs=[VECTORS] * 10,
        compiler_params=ROOM,
    )(block, fifth)
    tile, two_tiles = pltpu.VMEM((BZB, 8, width), f32), pltpu.VMEM((BZB, 16, width), f32)
    smoothed, coarse, flag = pl.pallas_call(
        lambda *refs: smooth_kernel(lanes, nodes, covered, *refs),
        name="smooth_block",
        out_shape=[
            jax.ShapeDtypeStruct((count, side, plane), f32),
            jax.ShapeDtypeStruct((count, (side // 2) ** 3), f32),
            jax.ShapeDtypeStruct((1, 1), jnp.int32),
        ],
        in_specs=[VECTORS] * 16,
        out_specs=[VECTORS, VECTORS, SCALARS],
        scratch_shapes=[pltpu.VMEM((BZB, BXD * side + 2 * PAD, width), f32)]
        + [tile] * 8
        + [two_tiles] * 4
        + [pltpu.VMEM((plane // 128, count * side, 128), f32), pltpu.SMEM((8, 128), f32), pltpu.SemaphoreType.DMA],
        compiler_params=ROOM,
    )(own_table, block, *coupled, from_below, from_above, row_table, two_on)
    irregular = flag[0, 0]
    if not covered:
        irregular = lax.pmax(irregular, ("node", "lane"))

    def again(carry):
        out = general_body(field, source, beta, target_held, neighbours_held)
        return (*out, jnp.int32(0))

    smoothed, coarse, _ = lax.while_loop(lambda carry: carry[2] > 0, again, (smoothed, coarse, irregular))
    return smoothed, coarse


def solution(mesh):
    in_specs = (
        P(("node", "lane"), None, None),
        P(("node", "lane"), None, None),
        P(("node", "lane"), None, None),
        P(("node", "lane")),
        P(("node", "lane"), None),
    )
    out_specs = (P(("node", "lane"), None, None), P(("node", "lane"), None))
    return jax.shard_map(fast_body, mesh=mesh, in_specs=in_specs, out_specs=out_specs, check_vma=False)
```

```python
import jax
import jax.numpy as jnp
from jax import lax
from jax.experimental import pallas as pl
from jax.experimental.pallas import tpu as pltpu
from jax.sharding import PartitionSpec as P

SWEEPS = 2


OPPOSITE = (1, 0, 3, 2, 5, 4)


def with_halo(block, sides, width):
    for axis, dim in sides:
        count = lax.axis_size(axis)
        forward = [(i, i + 1) for i in range(count - 1)]
        backward = [(target, source) for source, target in forward]
        low = lax.ppermute(
            lax.slice_in_dim(block, block.shape[dim] - width, None, axis=dim), axis, forward
        )
        high = lax.ppermute(lax.slice_in_dim(block, 0, width, axis=dim), axis, backward)
        block = jnp.concatenate([low, block, high], axis=dim)
    return block


def face_layers(values):
    boxes, side, plane = values.shape
    return jnp.stack(
        [
            values[:, 0],
            values[:, side - 1],
            values[:, :, :side].reshape(boxes, plane),
            values[:, :, plane - side :].reshape(boxes, plane),
            values[:, :, 0::side].reshape(boxes, plane),
            values[:, :, side - 1 :: side].reshape(boxes, plane),
        ],
        axis=1,
    )


def near_values(values, ghost):
    boxes, side, plane = values.shape
    lower_x = jnp.concatenate([ghost[:, 0][:, None, :], values[:, :-1]], axis=1)
    upper_x = jnp.concatenate([values[:, 1:], ghost[:, 1][:, None, :]], axis=1)
    lower_y = jnp.concatenate(
        [ghost[:, 2].reshape(boxes, side, side), values[:, :, : plane - side]], axis=2
    )
    upper_y = jnp.concatenate([values[:, :, side:], ghost[:, 3].reshape(boxes, side, side)], axis=2)
    depth = jnp.arange(plane) % side
    lower_z = jnp.where(
        depth == 0,
        jnp.repeat(ghost[:, 4].reshape(boxes, side, side), side, axis=2),
        jnp.roll(values, 1, axis=2),
    )
    upper_z = jnp.where(
        depth == side - 1,
        jnp.repeat(ghost[:, 5].reshape(boxes, side, side), side, axis=2),
        jnp.roll(values, -1, axis=2),
    )
    return [lower_x, upper_x, lower_y, upper_y, lower_z, upper_z]


def coefficients(diffusivity, beside):
    return [2.0 * diffusivity * other / (diffusivity + other) for other in beside]


def relax(values, source, couplings, beside, chosen):
    total = couplings[0]
    summed = source + couplings[0] * beside[0]
    for face in range(1, 6):
        total = total + couplings[face]
        summed = summed + couplings[face] * beside[face]
    return jnp.where(chosen, summed / total, values)


def defect_of(values, source, couplings, beside):
    total = couplings[0]
    summed = source + couplings[0] * beside[0]
    for face in range(1, 6):
        total = total + couplings[face]
        summed = summed + couplings[face] * beside[face]
    return summed - total * values


def colour_of(side, plane):
    rows = jnp.arange(side)[:, None]
    cells = jnp.arange(plane)[None, :]
    return (rows + cells // side + cells % side) % 2


def restrict(values):
    boxes, side, plane = values.shape
    half = side // 2
    paired = values.reshape(boxes, half, 2, plane).sum(axis=2)
    cells = jnp.arange(plane)
    coarse_cols = cells // side // 2 * half + cells % side // 2
    pooling = (coarse_cols[:, None] == jnp.arange(half * half)[None, :]).astype(jnp.float32)
    summed = jnp.einsum("bxp,pq->bxq", paired, pooling, precision=lax.Precision.HIGHEST)
    return (0.125 * summed).reshape(boxes, half * half * half)


def place(settled, arrived, tags):
    count = settled.shape[0]
    return settled.at[jnp.where(tags > 0, tags - 1, count)].set(arrived, mode="drop")


def general_body(old_field, old_source, diffusivity, target_box, neighbours):
    count, side, plane = old_field.shape
    lane_count = lax.axis_size("lane")
    lane_here = lax.axis_index("lane")
    own_device = lax.axis_index("node") * lane_count + lane_here
    dest_device = target_box // count
    dest_slot = target_box % count
    staying = dest_device == own_device
    cargo = jnp.stack([old_field, old_source], axis=1)
    settled = jnp.zeros_like(cargo).at[jnp.where(staying, dest_slot, count)].set(cargo, mode="drop")
    slots = jnp.arange(count)
    peers = own_device - lane_here + jnp.arange(lane_count)
    chosen = (dest_device[None, :] == peers[:, None]) & jnp.logical_not(staying)[None, :]
    filled = jnp.any(chosen, axis=1)
    picked = jnp.sum(jnp.where(chosen, slots[None, :], 0), axis=1)
    parcels = jnp.where(filled[:, None, None, None], cargo[picked], 0.0)
    labels = jnp.where(filled, jnp.sum(jnp.where(chosen, dest_slot[None, :], 0), axis=1) + 1, 0)
    arrived, tags = (
        lax.all_to_all(parcels, "lane", split_axis=0, concat_axis=0, tiled=True),
        lax.all_to_all(labels, "lane", split_axis=0, concat_axis=0, tiled=True),
    )
    settled = place(settled, arrived, tags)
    field = settled[:, 0]
    source = settled[:, 1]
    present = neighbours >= 0
    near_device = jnp.where(present, neighbours // count, own_device)
    local_row = neighbours % count * 6 + jnp.array(OPPOSITE, jnp.int32)[None, :]
    across = near_device - own_device
    anchor = jnp.where(
        across == -lane_count,
        1,
        jnp.where(
            across == lane_count, 2, jnp.where(across == -1, 3, jnp.where(across == 1, 4, 0))
        ),
    )
    index = anchor * (count * 6) + local_row
    width_out = count * 6

    def departing_boxes(layers):
        return layers.reshape(count * 6, plane)

    def incoming(received, start):
        return jnp.concatenate(
            [
                received[0, 1, start : start + width_out],
                received[2, 1, start : start + width_out],
                received[1, 0, start : start + width_out],
                received[1, 2, start : start + width_out],
            ],
            axis=0,
        )

    def trade(rows):
        return with_halo(rows[None, None], (("node", 0), ("lane", 1)), 1)

    def ghosts(layers, remote_rows, fallback):
        table = jnp.concatenate([layers.reshape(count * 6, plane), remote_rows], axis=0)
        return jnp.where(present[..., None], table[index], fallback)

    beta_layers = face_layers(diffusivity)
    layers = face_layers(field)
    received = trade(
        jnp.concatenate([departing_boxes(layers), departing_boxes(beta_layers)], axis=0)
    )
    beta_ghost = ghosts(beta_layers, incoming(received, width_out), beta_layers)
    couplings = coefficients(diffusivity, near_values(diffusivity, beta_ghost))
    colour = colour_of(side, plane)
    for sweep in range(SWEEPS):
        for colour_id in (0, 1):
            if sweep + colour_id > 0:
                layers = face_layers(field)
                received = trade(departing_boxes(layers))
            ghost = ghosts(layers, incoming(received, 0), jnp.zeros_like(layers))
            field = relax(field, source, couplings, near_values(field, ghost), colour == colour_id)
    layers = face_layers(field)
    received = trade(departing_boxes(layers))
    ghost = ghosts(layers, incoming(received, 0), jnp.zeros_like(layers))
    coarse = restrict(defect_of(field, source, couplings, near_values(field, ghost)))
    return (field, coarse)


BXD = 2
BZB = 4
PAD = 8
SIDE = 16
LOW, HIGH = "low", "high"


def lane_plan(lanes):
    half = lanes // 2
    moves = [1, lanes - 1, 2, lanes - 2, half]
    ends = {}
    for move in moves:
        for offset, part in ((move + 1, HIGH), (move - 1, LOW)):
            ends.setdefault(offset % lanes, []).append((move, part))
    bulk = {1: HIGH, lanes - 1: LOW}
    plan = {}
    for offset in sorted(set(moves) | set(ends)):
        if offset:
            plan[offset] = (bulk.get(offset), offset in moves, ends.get(offset, []))
    return moves, plan


def plan_units(count, bulk, whole, kept):
    return (count + count // 2 if bulk is not None else 0) + (3 if whole else 0) + len(kept) + 1


def cell_lanes(side):
    rows = lax.broadcasted_iota(jnp.int32, (side, 128), 0)
    cols = lax.broadcasted_iota(jnp.int32, (side, 128), 1)
    layer = cols >> (side.bit_length() - 1)
    black = ((rows + layer + cols) & 1) == 1
    return layer, black


def turn(values, shift):
    return pltpu.roll(values, shift % values.shape[-1], values.ndim - 1)


def pack_end(part, field, source, beta, masks):
    side = field.shape[0]
    y, black = masks
    if part == HIGH:
        pairs = jnp.where(black, field, turn(field, side))
        out = jnp.where(y >= 4, source, pairs)
        out = jnp.where(y == 2, turn(beta, -side), out)
        out = jnp.where(y == 1, turn(pairs, -4 * side), out)
        return jnp.where(y == 0, turn(pairs, side), out)
    pairs = jnp.where(black, field, turn(field, -side))
    out = jnp.where(y < 4, source, pairs)
    out = jnp.where(y == 5, turn(beta, side), out)
    out = jnp.where(y == 6, turn(pairs, 4 * side), out)
    return jnp.where(y == 7, turn(pairs, -side), out)


def unpack_end(part, packed):
    side = packed.shape[0]
    y, _ = cell_lanes(side)
    out = packed
    places = ((7, 7), (6, 6), (5, 4), (4, 3)) if part == HIGH else ((0, 1), (1, 2), (2, 4), (3, 5))
    for layer, shift in places:
        out = jnp.where(y == layer, turn(packed, shift * side), out)
    return out


def pack_whole(low, high):
    side = low.shape[0]
    layer, black = cell_lanes(side)
    even = (layer & 1) == 0
    low = jnp.where(black, low, turn(low, -side))
    high = jnp.where(black, high, turn(high, -side))
    return jnp.where(even, low, turn(high, side))


def unpack_whole(packed):
    side = packed.shape[0]
    even = (cell_lanes(side)[0] & 1) == 0
    return jnp.where(even, packed, turn(packed, side)), jnp.where(even, turn(packed, -side), packed)


def part_lanes(part, plane):
    return slice(0, plane // 2) if part == LOW else slice(plane // 2, plane)


def pack_kernel(moves, plan, lanes, count, *refs):
    outs = refs[5 : 5 + len(plan)]
    held_here = refs[5 + len(plan) : 10 + len(plan)]
    table, target, near, slots, sems = refs[10 + len(plan) :]
    pairs = [*zip(refs[3:5], (target, near)), *zip(refs[:5], held_here)]
    fetch = [pltpu.make_async_copy(src, dst, sems.at[k]) for k, (src, dst) in enumerate(pairs)]
    for copy in fetch:
        copy.start()
    for copy in fetch[:2]:
        copy.wait()
    field, source, beta = held_here[:3]
    side, plane = field.shape[1:]
    half = plane // 2
    lane = lax.axis_index("lane")
    first = (lax.axis_index("node") * lanes + lane) * count
    old_index = [jnp.int32(0)] * len(moves)
    new_slot = [jnp.int32(-1)] * len(moves)
    stay = []
    for i in range(count):
        there = target[i]
        slot = lax.rem(there, count)
        step = lax.rem(lax.rem(lax.div(there, count), lanes) - lane + lanes, lanes)
        stay.append(jnp.where(step == 0, slot, -1))
        for k, move in enumerate(moves):
            old_index[k] = jnp.where(step == move, i, old_index[k])
            new_slot[k] = jnp.where(step == move, slot, new_slot[k])
    for i in range(count):
        slots[i] = -1

    def local(index, face):
        there = near[index, face]
        inside = (there >= first) & (there < first + count)
        return inside, jnp.clip(there - first, 0, count - 1)

    place = []
    for i in range(count):
        inside, below = local(i, 0)
        depth = jnp.int32(0)
        live, at = local(i, 4)
        for _ in range(BZB - 1):
            depth = depth + jnp.where(live, 1, 0)
            further, onward = local(at, 4)
            live, at = live & further, onward
        spot = jnp.where(inside, BZB, 0) + depth
        place.append((depth, jnp.where(inside, side, 0)))
        slots[spot] = i
    rows = lax.broadcasted_iota(jnp.int32, (8, 128), 0)
    cols = lax.broadcasted_iota(jnp.int32, (8, 128), 1)
    spots = rows * 128 + cols
    held = jnp.zeros((8, 128), jnp.int32)

    def put(held, row, col, value):
        return jnp.where(spots == row * 128 + col, value, held)

    for i in range(count):
        slot = slots[i]
        held = put(held, i, 12, jnp.maximum(slot, 0))
        held = put(held, i, 0, jnp.where(slot < 0, -7, first + slot))
        for face in range(6):
            held = put(held, i, 1 + face, near[jnp.maximum(slot, 0), face])
        held = put(held, i, 7, place[i][0])
        held = put(held, i, 11, place[i][1])
        held = put(held, i, 9, stay[i])
    for k in range(len(moves)):
        held = put(held, k, 8, new_slot[k])
        held = put(held, k, 10, old_index[k])
    table[...] = held.astype(jnp.float32)
    for copy in fetch[2:]:
        copy.wait()
    masks = cell_lanes(side)
    left = lax.broadcasted_iota(jnp.int32, (side, 128), 1) < 64
    for out, (bulk, whole, kept) in zip(outs, plan.values()):
        if bulk is not None:
            cut = part_lanes(bulk, plane)
            for i in range(count):
                out[i] = pack_end(bulk, field[i, :, cut], source[i, :, cut], beta[i, :, cut], masks)
            for i in range(0, count, 2):
                one, two = beta[i, :, cut], turn(beta[i + 1, :, cut], 64)
                out[count + i // 2] = jnp.where(left, two, one) if bulk == HIGH else jnp.where(left, one, two)
    for (offset, (bulk, whole, kept)), out in zip(plan.items(), outs):
        unit = count + count // 2 if bulk is not None else 0
        low, high = part_lanes(LOW, plane), part_lanes(HIGH, plane)
        if whole:
            box = old_index[moves.index(offset)]
            out[unit] = pack_whole(field[box, :, low], field[box, :, high])
            out[unit + 1] = source[box, :, low]
            out[unit + 2] = source[box, :, high]
            unit += 3
        for move, part in kept:
            box = old_index[moves.index(move)]
            cut = part_lanes(part, plane)
            out[unit] = pack_end(part, field[box, :, cut], source[box, :, cut], field[box, :, cut], masks)
            unit += 1
    for out in outs:
        out[out.shape[0] - 1, 0:8] = table[...]


def assemble_kernel(moves, plan, lanes, count, *refs):
    own_table, field, source, beta = refs[:4]
    got = dict(zip(plan, refs[4 : 4 + len(plan)]))
    block, fifth, to_pair, to_other, row_table, low_side, high_side, tables, table_sems = refs[4 + len(plan) :]
    side, plane = field.shape[1:]
    half = plane // 2
    order = list(plan) + [0]

    def table_of(offset):
        return got[offset].at[got[offset].shape[0] - 1, 0:8] if offset else own_table

    fetch = [
        pltpu.make_async_copy(table_of(offset), tables.at[k], table_sems.at[k]) for k, offset in enumerate(order)
    ]
    for copy in fetch:
        copy.start()

    cols = lax.broadcasted_iota(jnp.int32, (8, 128), 1)
    shown = [offset for offset in plan if lanes == 8 or offset in (1, lanes - 1)]
    joined = jnp.where(cols < 8, own_table[...], 0.0)
    for offset in shown:
        at = offset if offset < 7 else 7
        joined = joined + pltpu.roll(jnp.where(cols < 8, table_of(offset)[...], 0.0), 8 * at, 1)
    joined = joined + pltpu.roll(joined, 64, 1)
    row_table[...] = joined
    to_pair[to_pair.shape[0] - 1] = joined
    to_other[to_other.shape[0] - 1] = joined

    for copy in fetch:
        copy.wait()

    def said(offset, row, col):
        return tables[order.index(offset), row, col].astype(jnp.int32)

    def spot_at(offset, slot):
        at = jnp.maximum(slot, 0)
        return jnp.where(slot >= 0, said(offset, at, 7), BZB), jnp.where(slot >= 0, said(offset, at, 11), 0)

    def put(ref, array, spot, values, where=slice(None)):
        deep, row = spot
        ref[array, deep, pl.ds(pl.multiple_of(row, side), side), where] = values

    low, high, whole = slice(0, half), slice(half, plane), slice(0, plane)
    for i in range(count):
        put(block, 2, (said(0, i, 7), said(0, i, 11)), beta[i], whole)
        spot = spot_at(0, said(0, i, 9))
        put(block, 0, spot, field[i], whole)
        put(block, 1, spot, source[i], whole)

    below, above = 1, lanes - 1
    sides = {HIGH: (low_side, below, side), LOW: (high_side, above, -side)}

    def put_end(part, slot, layers, raw, sources):
        ref, offset, shift = sides[part]
        spot = spot_at(offset, slot)
        put(ref, 0, spot, layers)
        put(ref, 1, spot, sources)
        put(ref, 3, spot, turn(raw, shift))

    for move, part in ((1, LOW), (lanes - 1, HIGH)):
        k = moves.index(move)
        box, cut = said(0, k, 10), part_lanes(part, plane)
        raw = field[box, :, cut]
        put_end(part, said(0, k, 8), raw, raw, source[box, :, cut])

    for offset, (bulk, entire, kept) in plan.items():
        message = got[offset]
        unit = 0
        if bulk is not None:
            ref, _, shift = sides[bulk]
            for i in range(count):
                packed = message[i]
                put_end(bulk, said(offset, i, 9), unpack_end(bulk, packed), packed, packed)
                joint = message[count + i // 2]
                spot = said(offset, i, 7), said(offset, i, 11)
                put(ref, 2, spot, joint if i % 2 == 0 else turn(joint, 64))
                put(ref, 4, spot, turn(packed, 2 * shift))
            unit = count + count // 2
        if entire:
            spot = spot_at(0, said(offset, moves.index(offset), 8))
            first, second = unpack_whole(message[unit])
            put(block, 0, spot, first, low)
            put(block, 0, spot, second, high)
            put(block, 1, spot, message[unit + 1], low)
            put(block, 1, spot, message[unit + 2], high)
            unit += 3
        for move, part in kept:
            packed = message[unit]
            put_end(part, said(offset, moves.index(move), 8), unpack_end(part, packed), packed, packed)
            unit += 1

    rows, width = block.shape[2:]
    left = lax.broadcasted_iota(jnp.int32, (rows, 128), 1) < 64
    for d in range(BZB):
        for k in range(3):
            block[k, d, :, plane:width] = jnp.where(left, high_side[k, d], low_side[k, d])
        for k in range(2):
            fifth[k, d] = jnp.where(left, high_side[3 + k, d], low_side[3 + k, d])
    even_node = (lax.axis_index("node") & 1) == 0
    for deep in range(0, BZB, 2):
        strips = []
        for start, up in ((rows - 8, True), (0, False)):
            tiles = []
            sources = []
            for d in (deep, deep + 1):
                f, s, b = (block[k, d, start : start + 8] for k in range(3))
                tiles.append(pack_rows(up, f, b))
                sources.append(s)
            strips.append(tiles + [pack_sources(up, *sources)])
        for k, (up, down) in enumerate(zip(*strips)):
            for part in range(width // 128):
                cut, unit = slice(part * 128, (part + 1) * 128), (deep // 2 * 3 + k) * 3 + part
                to_pair[unit] = jnp.where(even_node, up[:, cut], down[:, cut])
                to_other[unit] = jnp.where(even_node, down[:, cut], up[:, cut])


def row_colours(width, side):
    rows = lax.broadcasted_iota(jnp.int32, (8, width), 0)
    cols = lax.broadcasted_iota(jnp.int32, (8, width), 1)
    return rows, (rows + (cols >> (side.bit_length() - 1)) + cols) & 1


def fall(values, shift):
    return pltpu.roll(values, shift % 8, 0)


def pack_rows(up, field, beta):
    rows, colour = row_colours(field.shape[1], SIDE)
    if up:
        pairs = jnp.where(colour == 1, field, fall(field, 1))
        out = jnp.where(rows == 0, fall(pairs, 1), beta)
        out = jnp.where(rows == 1, fall(pairs, 4), out)
        return jnp.where(rows == 2, fall(pairs, 7), out)
    pairs = jnp.where(colour == 1, field, fall(field, 7))
    out = jnp.where(rows == 7, fall(pairs, 7), beta)
    out = jnp.where(rows == 6, fall(pairs, 4), out)
    return jnp.where(rows == 5, fall(pairs, 1), out)


def unpack_rows(below, above):
    rows = lax.broadcasted_iota(jnp.int32, below.shape, 0)
    field = fall(above, 1)
    for row, tile, shift in ((1, above, 2), (2, above, 4), (3, above, 5), (4, below, 3), (5, below, 4), (6, below, 6), (7, below, 7)):
        field = jnp.where(rows == row, fall(tile, shift), field)
    beta = jnp.where(rows < 4, above, below)
    fifth_field = jnp.where(rows < 4, fall(above, 6), fall(below, 2))
    fifth_beta = jnp.where(rows < 4, fall(above, 7), fall(below, 1))
    return field, beta, fifth_field, fifth_beta


def pack_sources(up, first, second):
    rows = lax.broadcasted_iota(jnp.int32, first.shape, 0)
    return jnp.where(rows >= 4, first, fall(second, 4)) if up else jnp.where(rows < 4, first, fall(second, 4))


class Stencil:
    def __init__(self, width, side, plane, lanes, nodes):
        self.width, self.side, self.plane = width, side, plane
        node, lane = lax.axis_index("node"), lax.axis_index("lane")
        self.first_node, self.last_node = node == 0, node == nodes - 1
        self.rows, self.colour = row_colours(width, side)
        cols = lax.broadcasted_iota(jnp.int32, (8, width), 1)
        depth = lax.rem(cols, side)
        self.at_front, self.at_back = depth == 0, depth == side - 1
        self.odd = (((cols >> (side.bit_length() - 1)) + cols) & 1) == 1
        first_lane, last_lane = lane == 0, lane == lanes - 1
        self.low_edge = (cols < side) & first_lane
        self.high_edge = (cols >= plane - side) & (cols < plane) & last_lane
        self.seam = (cols >= plane + 3 * side) & (cols < plane + 4 * side)
        self.no_link = ((cols >= width - side) & first_lane) | self.high_edge | self.seam

    def after(self, values):
        return pltpu.roll(values, self.width - self.side, 1)

    def before(self, values):
        return pltpu.roll(values, self.side, 1)

    def beyond_z(self, values, afters):
        out = []
        for deep in range(BZB):
            joined = values[deep] if deep == 0 else jnp.where(self.at_back, afters[deep - 1], values[deep])
            out.append(pltpu.roll(joined, 1, 1))
        return out

    def ahead_z(self, values, befores):
        out = []
        for deep in range(BZB):
            joined = values[deep] if deep == BZB - 1 else jnp.where(self.at_front, befores[deep + 1], values[deep])
            out.append(pltpu.roll(joined, self.width - 1, 1))
        return out

    def across(self, held):
        befores = [self.before(v) for v in held]
        afters = [self.after(v) for v in held]
        aheads = self.ahead_z(held, befores)
        ky = [jnp.where(self.no_link, 0.0, mean(held[d], afters[d])) for d in range(BZB)]
        kz = [mean(held[d], aheads[d]) for d in range(BZB)]
        kz[BZB - 1] = jnp.where(self.at_back, 0.0, kz[BZB - 1])
        kzl = self.beyond_z(kz, [self.after(v) for v in kz])
        kzl[0] = jnp.where(self.at_front, 0.0, kzl[0])
        return [self.before(v) for v in ky], ky, kzl, kz

    def edges(self, d, held):
        out = jnp.where(self.low_edge | self.high_edge, held, 0.0)
        if d == 0:
            out = out + jnp.where(self.at_front, held, 0.0)
        if d == BZB - 1:
            out = out + jnp.where(self.at_back, held, 0.0)
        return out

    def sums(self, colour_id, held, downs, ups, behind_of, ahead_of, coefficient):
        afters = [self.after(v) for v in held]
        befores = [self.before(v) for v in held]
        behind = behind_of(held, afters)
        aheads = ahead_of(held, befores)
        out = []
        for at in range(len(held)):
            s, same, other, yl, yu, zl, zu = coefficient(at)
            across = jnp.where(self.odd == (colour_id == 1), downs[at], ups[at])
            part = s + same * held[at] + other * across
            part = part + (yl * befores[at] + yu * afters[at])
            out.append(part + (zl * behind[at] + zu * aheads[at]))
        return out

    def beyond_pairs(self, values, afters):
        last = (fall(afters[1], 4), afters[0])
        return [pltpu.roll(jnp.where(self.at_back, last[j], values[j]), 1, 1) for j in range(2)]

    def ahead_pairs(self, values, befores):
        following = (befores[1], fall(befores[0], 4))
        return [pltpu.roll(jnp.where(self.at_front, following[j], values[j]), self.width - 1, 1) for j in range(2)]

    def split(self, even, odd):
        return jnp.where(self.odd, odd, even), jnp.where(self.odd, even, odd)


def mean(one_side, other):
    return 2.0 * one_side * other / (one_side + other)


def scatter_tiles(ref, index, rows, values):
    for k in range(ref.shape[0]):
        ref[(k, index, rows)] = values[:, k * 128 : (k + 1) * 128]


def every_other(ref, index, start, count):
    tiles = [ref[k, index, pl.ds(start, count, stride=2), :] for k in range(ref.shape[0])]
    return jnp.concatenate(tiles, axis=1)


def couple_kernel(lanes, nodes, plane, block, fifth, *refs):
    first, black, same = refs[:3]
    red_refs, black_refs = refs[3:9], refs[9:15]
    totals = refs[15:17]
    natural = refs[17:]
    f, s, xl, xu, yl, yu, zl, zu, total = natural
    width, own_rows = block.shape[3], block.shape[2]
    grid = Stencil(width, SIDE, plane, lanes, nodes)
    cols = lax.broadcasted_iota(jnp.int32, (8, 128), 1)
    seam = (cols >= 3 * SIDE) & (cols < 5 * SIDE)
    for r in range(0, own_rows, 8):
        here = slice(r, r + 8)
        held = [block[2, d, here] for d in range(BZB)]
        across = grid.across(held)
        for d in range(BZB):
            for ref, values in zip((yl, yu, zl, zu), across):
                scatter_tiles(ref, d, here, values[d])
            scatter_tiles(f, d, here, block[0, d, here])
            if r + 8 < own_rows:
                up = mean(held[d], block[2, d, r + 1 : r + 9])
            else:
                up = jnp.where(grid.rows == 7, 0.0, mean(held[d], fall(held[d], 7)))
            if r:
                down = mean(held[d], block[2, d, r - 1 : r + 7])
            else:
                down = jnp.where(grid.rows == 0, 0.0, mean(held[d], fall(held[d], 1)))
            link = jnp.where(seam, mean(held[d][:, plane:width], fifth[1, d, here]), 0.0)
            extra = link * jnp.where(seam, fifth[0, d, here], 0.0)
            source = block[1, d, here]
            scatter_tiles(s, d, here, jnp.concatenate([source[:, 0:plane], source[:, plane:width] + extra], axis=1))
            scatter_tiles(xl, d, here, down)
            scatter_tiles(xu, d, here, up)
            part = down + up + across[0][d] + across[1][d] + across[2][d] + across[3][d] + grid.edges(d, held[d])
            scatter_tiles(total, d, here, jnp.concatenate([part[:, 0:plane], part[:, plane:width] + link], axis=1))
    for d in range(BZB):
        for t in range(own_rows // 16):
            to = slice(8 * t, 8 * t + 8)
            even = [every_other(ref, d, 16 * t, 8) for ref in natural]
            odd = [every_other(ref, d, 16 * t + 1, 8) for ref in natural]
            black[d, to] = grid.split(even[0], odd[0])[1]
            same[d, to] = even[3]
            pairs = [(even[1], odd[1]), (even[2], odd[3])] + [(even[k], odd[k]) for k in (4, 5, 6, 7)]
            for red_ref, black_ref, pair in zip(red_refs, black_refs, pairs):
                red_ref[d, to], black_ref[d, to] = grid.split(*pair)
            totals[0][d, to], totals[1][d, to] = grid.split(even[8], odd[8])
    for t in range(own_rows // 16):
        to = slice(8 * t, 8 * t + 8)
        held = [black[d, to] for d in range(BZB)]
        downs = [black[d, to.start - 1 : to.stop - 1] if t else fall(held[d], 1) for d in range(BZB)]
        ups = [black[d, to.start + 1 : to.stop + 1] if 8 * t + 8 < own_rows // 2 else fall(held[d], 7) for d in range(BZB)]
        parts = grid.sums(
            0, held, downs, ups, grid.beyond_z, grid.ahead_z,
            lambda d: (red_refs[0][d, to], same[d, to]) + tuple(ref[d, to] for ref in red_refs[1:]),
        )
        for d in range(BZB):
            first[d, to] = parts[d]


def smooth_kernel(lanes, nodes, covered, own_table, block, *refs):
    first, own_black, own_same = refs[:3]
    own = (refs[3:9], refs[9:15])
    own_totals = refs[15:17]
    from_pair, from_other, row_table, two_on, smoothed, coarse, flag = refs[17:24]
    fields, halos, others, totals, inverses = refs[24:26], refs[26:28], refs[28:30], refs[30:32], refs[32:34]
    halo_coefficients = (refs[34:41], refs[41:48])
    halo_inverses = refs[48:50]
    natural = refs[50:59]
    shown, rest, labels, label_sem = refs[59:]
    width = block.shape[3]
    own_rows = block.shape[2]
    side = smoothed.shape[1]
    plane = smoothed.shape[2]
    node, lane = lax.axis_index("node"), lax.axis_index("lane")
    fetch = pltpu.make_async_copy(own_table, labels, label_sem)
    fetch.start()
    grid = Stencil(width, side, plane, lanes, nodes)
    rows = grid.rows
    last = own_rows - 8
    compact = own_rows // 2
    even_node = (node & 1) == 0
    halo_beta, links = [], []
    f, s, xl, xu, yl, yu, zl, zu, total = natural

    def spot(d):
        return d % 2, slice(d // 2 * 8, d // 2 * 8 + 8)

    for d in range(BZB):
        strips = []
        for k in (d % 2, 2):
            unit = (d // 2 * 3 + k) * 3
            pair, other = (
                jnp.concatenate([message[unit + part] for part in range(width // 128)], axis=1)
                for message in (from_pair, from_other)
            )
            strips.append((jnp.where(even_node, other, pair), jnp.where(even_node, pair, other)))
        below, above = strips[0]
        field, beta, fifth_field, fifth_beta = unpack_rows(below, above)
        scatter_tiles(f, *spot(d), field)
        below, above = strips[1]
        source = jnp.where(rows < 4, above, below) if d % 2 == 0 else jnp.where(rows < 4, fall(above, 4), fall(below, 4))
        link = jnp.where((rows == 3) | (rows == 4), mean(beta, fifth_beta), 0.0)
        scatter_tiles(s, *spot(d), source + link * fifth_field)
        links.append(link)
        halo_beta.append(beta)
    across = grid.across(halo_beta)
    for d in range(BZB):
        held = halo_beta[d]
        for ref, values in zip((yl, yu, zl, zu), across):
            scatter_tiles(ref, *spot(d), values[d])
        up = mean(held, jnp.where(rows == 7, fall(block[2, d, 0:8], 7), fall(held, 7)))
        up = jnp.where((rows == 3) | ((rows == 7) & grid.first_node), 0.0, up)
        down = jnp.where(grid.last_node, 0.0, mean(held, fall(block[2, d, last:own_rows], 1)))
        down = jnp.where(rows == 0, down, fall(up, 1))
        scatter_tiles(xl, *spot(d), down)
        scatter_tiles(xu, *spot(d), up)
        whole = links[d] + down + up + across[0][d] + across[1][d] + across[2][d] + across[3][d] + grid.edges(d, held)
        scatter_tiles(total, *spot(d), whole)
        low_link = jnp.where(rows == 0, fall(up, 1), 0.0)
        high_link = jnp.where(rows == 7, fall(down, 7), 0.0)
        low_whole = low_link + jnp.where((rows == 0) & grid.first_node, block[2, d, 0:8], 0.0)
        high_whole = high_link + jnp.where((rows == 7) & grid.last_node, block[2, d, last:own_rows], 0.0)
        for c in range(2):
            at_low, at_high = grid.odd == (c == 1), grid.odd == (c == 0)
            for t in range(compact // 8):
                to = slice(8 * t, 8 * t + 8)
                other, whole = own[c][1][d, to], own_totals[c][d, to]
                if t == 0:
                    other = other + jnp.where(at_low, low_link, 0.0)
                    whole = whole + jnp.where(at_low, low_whole, 0.0)
                if t == compact // 8 - 1:
                    other = other + jnp.where(at_high, high_link, 0.0)
                    whole = whole + jnp.where(at_high, high_whole, 0.0)
                others[c][d, to] = other
                totals[c][d, to] = whole
                inverses[c][d, to] = 1.0 / whole
        fields[1][d, 8 : 8 + compact] = own_black[d]

    def spread(c, j):
        tile = halos[c][j]
        turned = fall(tile, 4)
        fields[c][j, 8 + compact : 16 + compact] = tile
        fields[c][j, 0:8] = turned
        fields[c][j + 2, 8 + compact : 16 + compact] = turned
        fields[c][j + 2, 0:8] = tile

    for j in range(2):
        even = [every_other(ref, j, 0, 8) for ref in natural]
        odd = [every_other(ref, j, 1, 8) for ref in natural]
        halos[1][j] = grid.split(even[0], odd[0])[1]
        spread(1, j)
        pairs = [(even[1], odd[1]), (even[2], odd[3])] + [(even[k], odd[k]) for k in (4, 5, 6, 7)]
        for k, pair in enumerate(pairs):
            at = k if k == 0 else k + 1
            halo_coefficients[0][at][j], halo_coefficients[1][at][j] = grid.split(*pair)
        for c in range(2):
            halo_coefficients[c][1][j] = even[3]
        for c, whole in enumerate(grid.split(even[8], odd[8])):
            halo_inverses[c][j] = 1.0 / whole

    def own_sums(c, t):
        opposite = fields[1 - c]
        start = 8 + 8 * t
        held = [opposite[d, start : start + 8] for d in range(BZB)]
        downs = [opposite[d, start - 1 : start + 7] for d in range(BZB)]
        ups = [opposite[d, start + 1 : start + 9] for d in range(BZB)]
        to = slice(8 * t, 8 * t + 8)

        def coefficient(d):
            return (own[c][0][d, to], own_same[d, to], others[c][d, to]) + tuple(ref[d, to] for ref in own[c][2:])

        return grid.sums(c, held, downs, ups, grid.beyond_z, grid.ahead_z, coefficient)

    def end_terms(t):
        out = []
        for d in range(BZB):
            part = 0.0
            to = slice(8 * t, 8 * t + 8)
            if t == 0:
                low = others[0][d, to] * fields[1][d, 7:15]
                part = part + jnp.where((rows == 0) & ~grid.odd, low, 0.0)
            if t == compact // 8 - 1:
                high = others[0][d, to] * fields[1][d, 9 + 8 * t : 17 + 8 * t]
                part = part + jnp.where((rows == 7) & grid.odd, high, 0.0)
            out.append(first[d, to] + part)
        return out

    quarter = rows & 3
    for sweep in range(SWEEPS):
        for c in (0, 1):
            held = [halos[1 - c][j] for j in range(2)]
            opposite = fields[1 - c]
            downs, ups = [], []
            for j in range(2):
                lows = [opposite[d, compact : compact + 8] for d in (j, j + 2)]
                highs = [opposite[d, 8:16] for d in (j, j + 2)]
                joined = jnp.where(rows < 4, fall(lows[0], 1), fall(lows[1], 5))
                downs.append(jnp.where(quarter == 0, joined, fall(held[j], 1)))
                joined = jnp.where(rows < 4, fall(highs[0], 3), fall(highs[1], 7))
                ups.append(jnp.where(quarter == 3, joined, fall(held[j], 7)))
            parts = grid.sums(
                c, held, downs, ups, grid.beyond_pairs, grid.ahead_pairs,
                lambda j: tuple(ref[j] for ref in halo_coefficients[c]),
            )
            for j in range(2):
                halos[c][j] = parts[j] * halo_inverses[c][j]
                spread(c, j)
            for t in range(compact // 8):
                parts = end_terms(t) if sweep + c == 0 else own_sums(c, t)
                for d in range(BZB):
                    fields[c][d, 8 + 8 * t : 16 + 8 * t] = parts[d] * inverses[c][d, 8 * t : 8 * t + 8]

    fetch.wait()
    count = smoothed.shape[0]
    for t in range(compact // 8):
        to, own_to = slice(8 * t, 8 * t + 8), slice(8 + 8 * t, 16 + 8 * t)
        left = [own_sums(c, t) for c in range(2)]
        for d in range(BZB):
            slot = labels[t * BZB + d, 12].astype(jnp.int32)
            now = [fields[c][d, own_to] for c in range(2)]
            both = left[0][d] - totals[0][d, to] * now[0] + (left[1][d] - totals[1][d, to] * now[1])
            even, odd = grid.split(*now)
            for k in range(plane // 128):
                cut = slice(k * 128, (k + 1) * 128)
                rest[k, pl.ds(pl.multiple_of(slot * 8, 8), 8), :] = both[:, cut]
                shown[k, pl.ds(slot * side, 8, stride=2), :] = even[:, cut]
                shown[k, pl.ds(slot * side + 1, 8, stride=2), :] = odd[:, cut]
    for i in range(count):
        for k in range(plane // 128):
            smoothed[i, :, k * 128 : (k + 1) * 128] = shown[k, i * side : (i + 1) * side]

    small = side // 2
    cells = lax.broadcasted_iota(jnp.int32, (plane, 128), 0)
    slots = lax.broadcasted_iota(jnp.int32, (plane, 128), 1)
    goal = lax.div(lax.div(cells, side), 2) * small + lax.div(lax.rem(cells, side), 2)
    per = small * small
    acc = 0.0
    pairs = small * per // 128
    for inner in range(128 // per):
        stack = []
        for pair in range(pairs):
            i = pair * (128 // per) + inner
            tiles = [rest[k, pl.ds(i, count, stride=small), :] for k in range(plane // 128)]
            stack.append(jnp.concatenate(tiles, axis=1))
        pooling = (goal + inner * per == slots).astype(jnp.float32)
        acc = acc + jnp.dot(
            jnp.concatenate(stack, axis=0), pooling, precision=lax.Precision.HIGHEST, preferred_element_type=jnp.float32
        )
    for pair in range(pairs):
        coarse[:, pair * 128 : (pair + 1) * 128] = 0.125 * acc[pair * count : (pair + 1) * count]

    mine = from_pair.shape[0] - 1
    rows1 = lax.broadcasted_iota(jnp.int32, (8, 128), 0)
    cols1 = lax.broadcasted_iota(jnp.int32, (8, 128), 1)
    owner = lax.rem(lax.div(cols1, 8), 8)
    field_of = lax.rem(cols1, 8)
    table_here, opposite = row_table[...], two_on[...]
    pair, other = from_pair[mine], from_other[mine]
    lower, upper = jnp.where(even_node, other, pair), jnp.where(even_node, pair, other)
    rows_of = [(table_here, lower, upper, node), (lower, opposite, table_here, lax.rem(node + nodes - 1, nodes)),
               (upper, table_here, opposite, lax.rem(node + 1, nodes)), (opposite, upper, lower, lax.rem(node + 2, nodes))]
    if not covered:
        rows_of = rows_of[:1]
    lane_of = lax.rem(lane - jnp.where(owner > 4, owner - 8, owner) + 2 * lanes, lanes)
    wrong = jnp.zeros((8, 128), jnp.float32)
    for table, low, high, at_node in rows_of:
        turned = pltpu.roll(table, 4, 0)
        at_low = jnp.where(rows1 >= 4, turned, jnp.where(at_node == 0, -1.0, pltpu.roll(low, 4, 0)))
        at_high = jnp.where(rows1 < 4, turned, jnp.where(at_node == nodes - 1, -1.0, pltpu.roll(high, 4, 0)))
        y_low = jnp.where(lane_of == 0, -1.0, pltpu.roll(table, 128 - 8, 1))
        y_high = jnp.where(lane_of == lanes - 1, -1.0, pltpu.roll(table, 8, 1))
        z_low = jnp.where(lax.rem(rows1, BZB) == 0, -1.0, pltpu.roll(table, 1, 0))
        z_high = jnp.where(lax.rem(rows1, BZB) == BZB - 1, -1.0, pltpu.roll(table, 7, 0))
        bad = jnp.where((field_of == 0) & (table < 0), 1.0, 0.0)
        for face, expected in enumerate((at_low, at_high, y_low, y_high, z_low, z_high)):
            differs = table != pltpu.roll(expected, 1 + face, 1)
            bad = bad + jnp.where((field_of == 1 + face) & differs, 1.0, 0.0)
        if not covered:
            bad = jnp.where(owner == 0, bad, 0.0)
        wrong = wrong + bad
    flag[0, 0] = (jnp.sum(wrong) > 0).astype(jnp.int32)


ROOM = pltpu.CompilerParams(vmem_limit_bytes=32 * 2**20)
FULL = pltpu.CompilerParams(vmem_limit_bytes=60 * 2**20)
SCALARS = pl.BlockSpec(memory_space=pltpu.SMEM)
VECTORS = pl.BlockSpec(memory_space=pltpu.VMEM)


def fast_body(old_field, old_source, diffusivity, target_box, neighbours):
    count, side, plane = old_field.shape
    half = plane // 2
    lanes, nodes = lax.axis_size("lane"), lax.axis_size("node")
    arrays = (old_field, old_source, diffusivity, target_box, neighbours)
    moves, plan = lane_plan(lanes)
    covered = lanes == 8 and nodes == 4
    units = [plan_units(count, *parts) for parts in plan.values()]
    f32 = jnp.float32
    packed = pl.pallas_call(
        lambda *refs: pack_kernel(moves, plan, lanes, count, *refs),
        name="pack_moves",
        out_shape=[pltpu.VMEM((n, side, half), f32) for n in units]
        + [pltpu.VMEM(array.shape, array.dtype) for array in arrays]
        + [pltpu.VMEM((8, 128), f32)],
        in_specs=[pl.BlockSpec(memory_space=pltpu.HBM)] * 5,
        out_specs=[VECTORS] * (len(units) + 6),
        scratch_shapes=[
            pltpu.SMEM(target_box.shape, jnp.int32),
            pltpu.SMEM(neighbours.shape, jnp.int32),
            pltpu.SMEM((count,), jnp.int32),
            pltpu.SemaphoreType.DMA((7,)),
        ],
        compiler_params=FULL,
    )(*arrays)
    messages, own_table = packed[:-6], packed[-1]
    field, source, beta, target_held, neighbours_held = packed[-6:-1]
    got = {}
    early = [offset for offset in plan if offset in moves]
    for offset in early + [offset for offset in plan if offset not in moves]:
        message = messages[list(plan).index(offset)]
        if offset not in moves:
            message, _ = lax.optimization_barrier((message, got[2]))
        got[offset] = lax.ppermute(message, "lane", [(i, (i + offset) % lanes) for i in range(lanes)])
    got = [got[offset] for offset in plan]
    width = plane + 128
    strips = BZB // 2 * 9 + 1
    sides = pltpu.VMEM((5, BZB + 1, BXD * side, 128), f32)
    block, fifth, to_pair, to_other, row_table = pl.pallas_call(
        lambda *refs: assemble_kernel(moves, plan, lanes, count, *refs),
        name="assemble_block",
        out_shape=[
            pltpu.VMEM((3, BZB + 1, BXD * side, width), f32),
            pltpu.VMEM((2, BZB, BXD * side, 128), f32),
            pltpu.VMEM((strips, 8, 128), f32),
            pltpu.VMEM((strips, 8, 128), f32),
            pltpu.VMEM((8, 128), f32),
        ],
        in_specs=[VECTORS] * (4 + len(units)),
        out_specs=[VECTORS] * 5,
        scratch_shapes=[
            sides,
            sides,
            pltpu.SMEM((len(units) + 1, 8, 128), f32),
            pltpu.SemaphoreType.DMA((len(units) + 1,)),
        ],
        compiler_params=ROOM,
    )(own_table, field, source, beta, *got)
    from_pair = lax.ppermute(to_pair, "node", [(i, i ^ 1) for i in range(nodes)])
    from_other = lax.ppermute(to_other, "node", [(i, (i - 1 + 2 * (i % 2)) % nodes) for i in range(nodes)])
    two_on = lax.ppermute(row_table, "node", [(i, (i + 2) % nodes) for i in range(nodes)])
    tiles, rows = width // 128, BXD * side
    half_rows = pltpu.VMEM((BZB, rows // 2, width), f32)
    coupled = pl.pallas_call(
        lambda *refs: couple_kernel(lanes, nodes, plane, *refs),
        name="couple_block",
        out_shape=[half_rows] * 17,
        in_specs=[VECTORS] * 2,
        out_specs=[VECTORS] * 17,
        scratch_shapes=[pltpu.VMEM((tiles, BZB, rows, 128), f32)] * 9,
        compiler_params=ROOM,
    )(block, fifth)
    pair_tile = pltpu.VMEM((2, 8, width), f32)
    smoothed, coarse, flag = pl.pallas_call(
        lambda *refs: smooth_kernel(lanes, nodes, covered, *refs),
        name="smooth_block",
        out_shape=[
            jax.ShapeDtypeStruct((count, side, plane), f32),
            jax.ShapeDtypeStruct((count, (side // 2) ** 3), f32),
            jax.ShapeDtypeStruct((1, 1), jnp.int32),
        ],
        in_specs=[VECTORS] * (2 + 17 + 4),
        out_specs=[VECTORS, VECTORS, SCALARS],
        scratch_shapes=[pltpu.VMEM((BZB, rows // 2 + 16, width), f32)] * 2
        + [pair_tile] * 2
        + [half_rows] * 6
        + [pair_tile] * 16
        + [pltpu.VMEM((tiles, 2, 16, 128), f32)] * 9
        + [pltpu.VMEM((plane // 128, count * side, 128), f32), pltpu.VMEM((plane // 128, count * side // 2, 128), f32)]
        + [pltpu.SMEM((8, 128), f32), pltpu.SemaphoreType.DMA],
        compiler_params=ROOM,
    )(own_table, block, *coupled, from_pair, from_other, row_table, two_on)
    irregular = flag[0, 0]
    if not covered:
        irregular = lax.pmax(irregular, ("node", "lane"))

    def again(carry):
        out = general_body(field, source, beta, target_held, neighbours_held)
        return (*out, jnp.int32(0))

    smoothed, coarse, _ = lax.while_loop(lambda carry: carry[2] > 0, again, (smoothed, coarse, irregular))
    return smoothed, coarse


def solution(mesh):
    in_specs = (
        P(("node", "lane"), None, None),
        P(("node", "lane"), None, None),
        P(("node", "lane"), None, None),
        P(("node", "lane")),
        P(("node", "lane"), None),
    )
    out_specs = (P(("node", "lane"), None, None), P(("node", "lane"), None))
    return jax.shard_map(fast_body, mesh=mesh, in_specs=in_specs, out_specs=out_specs, check_vma=False)
```

```python
import jax
import jax.numpy as jnp
from jax import lax
from jax.experimental import pallas as pl
from jax.experimental.pallas import tpu as pltpu
from jax.sharding import PartitionSpec as P

SWEEPS = 2


OPPOSITE = (1, 0, 3, 2, 5, 4)


def with_halo(block, sides, width):
    for axis, dim in sides:
        count = lax.axis_size(axis)
        forward = [(i, i + 1) for i in range(count - 1)]
        backward = [(target, source) for source, target in forward]
        low = lax.ppermute(
            lax.slice_in_dim(block, block.shape[dim] - width, None, axis=dim), axis, forward
        )
        high = lax.ppermute(lax.slice_in_dim(block, 0, width, axis=dim), axis, backward)
        block = jnp.concatenate([low, block, high], axis=dim)
    return block


def face_layers(values):
    boxes, side, plane = values.shape
    return jnp.stack(
        [
            values[:, 0],
            values[:, side - 1],
            values[:, :, :side].reshape(boxes, plane),
            values[:, :, plane - side :].reshape(boxes, plane),
            values[:, :, 0::side].reshape(boxes, plane),
            values[:, :, side - 1 :: side].reshape(boxes, plane),
        ],
        axis=1,
    )


def near_values(values, ghost):
    boxes, side, plane = values.shape
    lower_x = jnp.concatenate([ghost[:, 0][:, None, :], values[:, :-1]], axis=1)
    upper_x = jnp.concatenate([values[:, 1:], ghost[:, 1][:, None, :]], axis=1)
    lower_y = jnp.concatenate(
        [ghost[:, 2].reshape(boxes, side, side), values[:, :, : plane - side]], axis=2
    )
    upper_y = jnp.concatenate([values[:, :, side:], ghost[:, 3].reshape(boxes, side, side)], axis=2)
    depth = jnp.arange(plane) % side
    lower_z = jnp.where(
        depth == 0,
        jnp.repeat(ghost[:, 4].reshape(boxes, side, side), side, axis=2),
        jnp.roll(values, 1, axis=2),
    )
    upper_z = jnp.where(
        depth == side - 1,
        jnp.repeat(ghost[:, 5].reshape(boxes, side, side), side, axis=2),
        jnp.roll(values, -1, axis=2),
    )
    return [lower_x, upper_x, lower_y, upper_y, lower_z, upper_z]


def coefficients(diffusivity, beside):
    return [2.0 * diffusivity * other / (diffusivity + other) for other in beside]


def relax(values, source, couplings, beside, chosen):
    total = couplings[0]
    summed = source + couplings[0] * beside[0]
    for face in range(1, 6):
        total = total + couplings[face]
        summed = summed + couplings[face] * beside[face]
    return jnp.where(chosen, summed / total, values)


def defect_of(values, source, couplings, beside):
    total = couplings[0]
    summed = source + couplings[0] * beside[0]
    for face in range(1, 6):
        total = total + couplings[face]
        summed = summed + couplings[face] * beside[face]
    return summed - total * values


def colour_of(side, plane):
    rows = jnp.arange(side)[:, None]
    cells = jnp.arange(plane)[None, :]
    return (rows + cells // side + cells % side) % 2


def restrict(values):
    boxes, side, plane = values.shape
    half = side // 2
    paired = values.reshape(boxes, half, 2, plane).sum(axis=2)
    cells = jnp.arange(plane)
    coarse_cols = cells // side // 2 * half + cells % side // 2
    pooling = (coarse_cols[:, None] == jnp.arange(half * half)[None, :]).astype(jnp.float32)
    summed = jnp.einsum("bxp,pq->bxq", paired, pooling, precision=lax.Precision.HIGHEST)
    return (0.125 * summed).reshape(boxes, half * half * half)


def place(settled, arrived, tags):
    count = settled.shape[0]
    return settled.at[jnp.where(tags > 0, tags - 1, count)].set(arrived, mode="drop")


def general_body(old_field, old_source, diffusivity, target_box, neighbours):
    count, side, plane = old_field.shape
    lane_count = lax.axis_size("lane")
    lane_here = lax.axis_index("lane")
    own_device = lax.axis_index("node") * lane_count + lane_here
    dest_device = target_box // count
    dest_slot = target_box % count
    staying = dest_device == own_device
    cargo = jnp.stack([old_field, old_source], axis=1)
    settled = jnp.zeros_like(cargo).at[jnp.where(staying, dest_slot, count)].set(cargo, mode="drop")
    slots = jnp.arange(count)
    peers = own_device - lane_here + jnp.arange(lane_count)
    chosen = (dest_device[None, :] == peers[:, None]) & jnp.logical_not(staying)[None, :]
    filled = jnp.any(chosen, axis=1)
    picked = jnp.sum(jnp.where(chosen, slots[None, :], 0), axis=1)
    parcels = jnp.where(filled[:, None, None, None], cargo[picked], 0.0)
    labels = jnp.where(filled, jnp.sum(jnp.where(chosen, dest_slot[None, :], 0), axis=1) + 1, 0)
    arrived, tags = (
        lax.all_to_all(parcels, "lane", split_axis=0, concat_axis=0, tiled=True),
        lax.all_to_all(labels, "lane", split_axis=0, concat_axis=0, tiled=True),
    )
    settled = place(settled, arrived, tags)
    field = settled[:, 0]
    source = settled[:, 1]
    present = neighbours >= 0
    near_device = jnp.where(present, neighbours // count, own_device)
    local_row = neighbours % count * 6 + jnp.array(OPPOSITE, jnp.int32)[None, :]
    across = near_device - own_device
    anchor = jnp.where(
        across == -lane_count,
        1,
        jnp.where(
            across == lane_count, 2, jnp.where(across == -1, 3, jnp.where(across == 1, 4, 0))
        ),
    )
    index = anchor * (count * 6) + local_row
    width_out = count * 6

    def departing_boxes(layers):
        return layers.reshape(count * 6, plane)

    def incoming(received, start):
        return jnp.concatenate(
            [
                received[0, 1, start : start + width_out],
                received[2, 1, start : start + width_out],
                received[1, 0, start : start + width_out],
                received[1, 2, start : start + width_out],
            ],
            axis=0,
        )

    def trade(rows):
        return with_halo(rows[None, None], (("node", 0), ("lane", 1)), 1)

    def ghosts(layers, remote_rows, fallback):
        table = jnp.concatenate([layers.reshape(count * 6, plane), remote_rows], axis=0)
        return jnp.where(present[..., None], table[index], fallback)

    beta_layers = face_layers(diffusivity)
    layers = face_layers(field)
    received = trade(
        jnp.concatenate([departing_boxes(layers), departing_boxes(beta_layers)], axis=0)
    )
    beta_ghost = ghosts(beta_layers, incoming(received, width_out), beta_layers)
    couplings = coefficients(diffusivity, near_values(diffusivity, beta_ghost))
    colour = colour_of(side, plane)
    for sweep in range(SWEEPS):
        for colour_id in (0, 1):
            if sweep + colour_id > 0:
                layers = face_layers(field)
                received = trade(departing_boxes(layers))
            ghost = ghosts(layers, incoming(received, 0), jnp.zeros_like(layers))
            field = relax(field, source, couplings, near_values(field, ghost), colour == colour_id)
    layers = face_layers(field)
    received = trade(departing_boxes(layers))
    ghost = ghosts(layers, incoming(received, 0), jnp.zeros_like(layers))
    coarse = restrict(defect_of(field, source, couplings, near_values(field, ghost)))
    return (field, coarse)


BXD = 2
BZB = 4
PAD = 8
SIDE = 16
LOW, HIGH = "low", "high"


def lane_plan(lanes):
    half = lanes // 2
    moves = [1, lanes - 1, 2, lanes - 2, half]
    ends = {}
    for move in moves:
        for offset, part in ((move + 1, HIGH), (move - 1, LOW)):
            ends.setdefault(offset % lanes, []).append((move, part))
    bulk = {1: HIGH, lanes - 1: LOW}
    plan = {}
    for offset in sorted(set(moves) | set(ends)):
        if offset:
            plan[offset] = (bulk.get(offset), offset in moves, ends.get(offset, []))
    return moves, plan


def plan_units(count, bulk, whole, kept):
    return (count + count // 2 if bulk is not None else 0) + (3 if whole else 0) + len(kept) + 1


def cell_lanes(side):
    rows = lax.broadcasted_iota(jnp.int32, (side, 128), 0)
    cols = lax.broadcasted_iota(jnp.int32, (side, 128), 1)
    layer = cols >> (side.bit_length() - 1)
    black = ((rows + layer + cols) & 1) == 1
    return layer, black


def turn(values, shift):
    return pltpu.roll(values, shift % values.shape[-1], values.ndim - 1)


def pack_end(part, field, source, beta, masks):
    side = field.shape[0]
    y, black = masks
    if part == HIGH:
        pairs = jnp.where(black, field, turn(field, side))
        out = jnp.where(y >= 4, source, pairs)
        out = jnp.where(y == 2, turn(beta, -side), out)
        out = jnp.where(y == 1, turn(pairs, -4 * side), out)
        return jnp.where(y == 0, turn(pairs, side), out)
    pairs = jnp.where(black, field, turn(field, -side))
    out = jnp.where(y < 4, source, pairs)
    out = jnp.where(y == 5, turn(beta, side), out)
    out = jnp.where(y == 6, turn(pairs, 4 * side), out)
    return jnp.where(y == 7, turn(pairs, -side), out)


def unpack_end(part, packed):
    side = packed.shape[0]
    y, _ = cell_lanes(side)
    out = packed
    places = ((7, 7), (6, 6), (5, 4), (4, 3)) if part == HIGH else ((0, 1), (1, 2), (2, 4), (3, 5))
    for layer, shift in places:
        out = jnp.where(y == layer, turn(packed, shift * side), out)
    return out


def pack_whole(low, high):
    side = low.shape[0]
    layer, black = cell_lanes(side)
    even = (layer & 1) == 0
    low = jnp.where(black, low, turn(low, -side))
    high = jnp.where(black, high, turn(high, -side))
    return jnp.where(even, low, turn(high, side))


def unpack_whole(packed):
    side = packed.shape[0]
    even = (cell_lanes(side)[0] & 1) == 0
    return jnp.where(even, packed, turn(packed, side)), jnp.where(even, turn(packed, -side), packed)


def part_lanes(part, plane):
    return slice(0, plane // 2) if part == LOW else slice(plane // 2, plane)


def pack_kernel(moves, plan, lanes, count, *refs):
    outs = refs[5 : 5 + len(plan)]
    held_here = refs[5 + len(plan) : 10 + len(plan)]
    table, target, near, slots, sems = refs[10 + len(plan) :]
    pairs = [*zip(refs[3:5], (target, near)), *zip(refs[:5], held_here)]
    fetch = [pltpu.make_async_copy(src, dst, sems.at[k]) for k, (src, dst) in enumerate(pairs)]
    for copy in fetch:
        copy.start()
    for copy in fetch[:2]:
        copy.wait()
    field, source, beta = held_here[:3]
    side, plane = field.shape[1:]
    half = plane // 2
    lane = lax.axis_index("lane")
    first = (lax.axis_index("node") * lanes + lane) * count
    old_index = [jnp.int32(0)] * len(moves)
    new_slot = [jnp.int32(-1)] * len(moves)
    stay = []
    for i in range(count):
        there = target[i]
        slot = lax.rem(there, count)
        step = lax.rem(lax.rem(lax.div(there, count), lanes) - lane + lanes, lanes)
        stay.append(jnp.where(step == 0, slot, -1))
        for k, move in enumerate(moves):
            old_index[k] = jnp.where(step == move, i, old_index[k])
            new_slot[k] = jnp.where(step == move, slot, new_slot[k])
    for i in range(count):
        slots[i] = -1

    def local(index, face):
        there = near[index, face]
        inside = (there >= first) & (there < first + count)
        return inside, jnp.clip(there - first, 0, count - 1)

    place = []
    for i in range(count):
        inside, below = local(i, 0)
        depth = jnp.int32(0)
        live, at = local(i, 4)
        for _ in range(BZB - 1):
            depth = depth + jnp.where(live, 1, 0)
            further, onward = local(at, 4)
            live, at = live & further, onward
        spot = jnp.where(inside, BZB, 0) + depth
        place.append(spot)
        slots[spot] = i
    rows = lax.broadcasted_iota(jnp.int32, (8, 128), 0)
    cols = lax.broadcasted_iota(jnp.int32, (8, 128), 1)
    spots = rows * 128 + cols
    held = jnp.zeros((8, 128), jnp.int32)

    def put(held, row, col, value):
        return jnp.where(spots == row * 128 + col, value, held)

    for i in range(count):
        slot = slots[i]
        held = put(held, i, 12, jnp.maximum(slot, 0))
        held = put(held, i, 0, jnp.where(slot < 0, -7, first + slot))
        for face in range(6):
            held = put(held, i, 1 + face, near[jnp.maximum(slot, 0), face])
    words = [
        sum(place[i] << 3 * i for i in range(count)),
        sum((stay[i] + 1) << 4 * i for i in range(count // 2)),
        sum((stay[i] + 1) << 4 * (i - count // 2) for i in range(count // 2, count)),
        sum((new_slot[k] + 1) << 4 * k for k in range(len(moves))),
        sum(old_index[k] << 3 * k for k in range(len(moves))),
    ]
    for k, word in enumerate(words):
        held = put(held, 0, 16 + k, word)
    table[...] = held.astype(jnp.float32)
    for copy in fetch[2:]:
        copy.wait()
    masks = cell_lanes(side)
    left = lax.broadcasted_iota(jnp.int32, (side, 128), 1) < 64
    for out, (bulk, whole, kept) in zip(outs, plan.values()):
        if bulk is not None:
            cut = part_lanes(bulk, plane)
            for i in range(count):
                out[i] = pack_end(bulk, field[i, :, cut], source[i, :, cut], beta[i, :, cut], masks)
            for i in range(0, count, 2):
                one, two = beta[i, :, cut], turn(beta[i + 1, :, cut], 64)
                out[count + i // 2] = jnp.where(left, two, one) if bulk == HIGH else jnp.where(left, one, two)
    for (offset, (bulk, whole, kept)), out in zip(plan.items(), outs):
        unit = count + count // 2 if bulk is not None else 0
        low, high = part_lanes(LOW, plane), part_lanes(HIGH, plane)
        if whole:
            box = old_index[moves.index(offset)]
            out[unit] = pack_whole(field[box, :, low], field[box, :, high])
            out[unit + 1] = source[box, :, low]
            out[unit + 2] = source[box, :, high]
            unit += 3
        for move, part in kept:
            box = old_index[moves.index(move)]
            cut = part_lanes(part, plane)
            out[unit] = pack_end(part, field[box, :, cut], source[box, :, cut], field[box, :, cut], masks)
            unit += 1
    for out in outs:
        out[out.shape[0] - 1, 0:8] = table[...]


def assemble_kernel(moves, plan, lanes, count, *refs):
    own_table, field, source, beta = refs[:4]
    got = dict(zip(plan, refs[4 : 4 + len(plan)]))
    block, fifth, to_pair, to_other, row_table, low_side, high_side = refs[4 + len(plan) :]
    side, plane = field.shape[1:]
    half = plane // 2

    def table_of(offset):
        return got[offset].at[got[offset].shape[0] - 1, 0:8] if offset else own_table

    words = {}
    for offset in (0, *plan):
        line = table_of(offset)[0:1, :].astype(jnp.int32)
        words[offset] = [line[0, 16 + k] for k in range(5)]

    cols = lax.broadcasted_iota(jnp.int32, (8, 128), 1)
    shown = [offset for offset in plan if lanes == 8 or offset in (1, lanes - 1)]
    joined = jnp.where(cols < 8, own_table[...], 0.0)
    for offset in shown:
        at = offset if offset < 7 else 7
        joined = joined + pltpu.roll(jnp.where(cols < 8, table_of(offset)[...], 0.0), 8 * at, 1)
    joined = joined + pltpu.roll(joined, 64, 1)
    row_table[...] = joined
    to_pair[to_pair.shape[0] - 1] = joined
    to_other[to_other.shape[0] - 1] = joined

    def place_of(offset, slot):
        code = (words[offset][0] >> 3 * slot) & 7
        return code & (BZB - 1), (code >> 2) * side

    def stays(offset, i):
        return ((words[offset][1 + i // (count // 2)] >> 4 * (i % (count // 2))) & 15) - 1

    def moved(offset, k):
        return ((words[offset][3] >> 4 * k) & 15) - 1

    def spot_at(offset, slot):
        deep, row = place_of(offset, jnp.maximum(slot, 0))
        return jnp.where(slot >= 0, deep, BZB), jnp.where(slot >= 0, row, 0)

    def put(ref, array, spot, values, where=slice(None)):
        deep, row = spot
        ref[array, deep, pl.ds(pl.multiple_of(row, side), side), where] = values

    low, high, whole = slice(0, half), slice(half, plane), slice(0, plane)
    for i in range(count):
        put(block, 2, place_of(0, i), beta[i], whole)
        spot = spot_at(0, stays(0, i))
        put(block, 0, spot, field[i], whole)
        put(block, 1, spot, source[i], whole)

    below, above = 1, lanes - 1
    sides = {HIGH: (low_side, below, side), LOW: (high_side, above, -side)}

    def put_end(part, slot, layers, raw, sources):
        ref, offset, shift = sides[part]
        spot = spot_at(offset, slot)
        put(ref, 0, spot, layers)
        put(ref, 1, spot, sources)
        put(ref, 3, spot, turn(raw, shift))

    for move, part in ((1, LOW), (lanes - 1, HIGH)):
        k = moves.index(move)
        box, cut = (words[0][4] >> 3 * k) & 7, part_lanes(part, plane)
        raw = field[box, :, cut]
        put_end(part, moved(0, k), raw, raw, source[box, :, cut])

    for offset, (bulk, entire, kept) in plan.items():
        message = got[offset]
        unit = 0
        if bulk is not None:
            ref, _, shift = sides[bulk]
            for i in range(count):
                packed = message[i]
                put_end(bulk, stays(offset, i), unpack_end(bulk, packed), packed, packed)
                joint = message[count + i // 2]
                spot = place_of(offset, i)
                put(ref, 2, spot, joint if i % 2 == 0 else turn(joint, 64))
                put(ref, 4, spot, turn(packed, 2 * shift))
            unit = count + count // 2
        if entire:
            spot = spot_at(0, moved(offset, moves.index(offset)))
            first, second = unpack_whole(message[unit])
            put(block, 0, spot, first, low)
            put(block, 0, spot, second, high)
            put(block, 1, spot, message[unit + 1], low)
            put(block, 1, spot, message[unit + 2], high)
            unit += 3
        for move, part in kept:
            packed = message[unit]
            put_end(part, moved(offset, moves.index(move)), unpack_end(part, packed), packed, packed)
            unit += 1

    rows, width = block.shape[2:]
    left = lax.broadcasted_iota(jnp.int32, (rows, 128), 1) < 64
    for d in range(BZB):
        for k in range(3):
            block[k, d, :, plane:width] = jnp.where(left, high_side[k, d], low_side[k, d])
        for k in range(2):
            fifth[k, d] = jnp.where(left, high_side[3 + k, d], low_side[3 + k, d])
    even_node = (lax.axis_index("node") & 1) == 0
    for deep in range(0, BZB, 2):
        strips = []
        for start, up in ((rows - 8, True), (0, False)):
            tiles = []
            sources = []
            for d in (deep, deep + 1):
                f, s, b = (block[k, d, start : start + 8] for k in range(3))
                tiles.append(pack_rows(up, f, b))
                sources.append(s)
            strips.append(tiles + [pack_sources(up, *sources)])
        for k, (up, down) in enumerate(zip(*strips)):
            for part in range(width // 128):
                cut, unit = slice(part * 128, (part + 1) * 128), (deep // 2 * 3 + k) * 3 + part
                to_pair[unit] = jnp.where(even_node, up[:, cut], down[:, cut])
                to_other[unit] = jnp.where(even_node, down[:, cut], up[:, cut])


def row_colours(width, side):
    rows = lax.broadcasted_iota(jnp.int32, (8, width), 0)
    cols = lax.broadcasted_iota(jnp.int32, (8, width), 1)
    return rows, (rows + (cols >> (side.bit_length() - 1)) + cols) & 1


def fall(values, shift):
    return pltpu.roll(values, shift % 8, 0)


def pack_rows(up, field, beta):
    rows, colour = row_colours(field.shape[1], SIDE)
    if up:
        pairs = jnp.where(colour == 1, field, fall(field, 1))
        out = jnp.where(rows == 0, fall(pairs, 1), beta)
        out = jnp.where(rows == 1, fall(pairs, 4), out)
        return jnp.where(rows == 2, fall(pairs, 7), out)
    pairs = jnp.where(colour == 1, field, fall(field, 7))
    out = jnp.where(rows == 7, fall(pairs, 7), beta)
    out = jnp.where(rows == 6, fall(pairs, 4), out)
    return jnp.where(rows == 5, fall(pairs, 1), out)


def unpack_rows(below, above):
    rows = lax.broadcasted_iota(jnp.int32, below.shape, 0)
    field = fall(above, 1)
    for row, tile, shift in ((1, above, 2), (2, above, 4), (3, above, 5), (4, below, 3), (5, below, 4), (6, below, 6), (7, below, 7)):
        field = jnp.where(rows == row, fall(tile, shift), field)
    beta = jnp.where(rows < 4, above, below)
    fifth_field = jnp.where(rows < 4, fall(above, 6), fall(below, 2))
    fifth_beta = jnp.where(rows < 4, fall(above, 7), fall(below, 1))
    return field, beta, fifth_field, fifth_beta


def pack_sources(up, first, second):
    rows = lax.broadcasted_iota(jnp.int32, first.shape, 0)
    return jnp.where(rows >= 4, first, fall(second, 4)) if up else jnp.where(rows < 4, first, fall(second, 4))


class Stencil:
    def __init__(self, width, side, plane, lanes, nodes):
        self.width, self.side, self.plane = width, side, plane
        node, lane = lax.axis_index("node"), lax.axis_index("lane")
        self.first_node, self.last_node = node == 0, node == nodes - 1
        self.rows, self.colour = row_colours(width, side)
        cols = lax.broadcasted_iota(jnp.int32, (8, width), 1)
        depth = lax.rem(cols, side)
        self.at_front, self.at_back = depth == 0, depth == side - 1
        self.odd = (((cols >> (side.bit_length() - 1)) + cols) & 1) == 1
        first_lane, last_lane = lane == 0, lane == lanes - 1
        self.low_edge = (cols < side) & first_lane
        self.high_edge = (cols >= plane - side) & (cols < plane) & last_lane
        self.seam = (cols >= plane + 3 * side) & (cols < plane + 4 * side)
        self.no_link = ((cols >= width - side) & first_lane) | self.high_edge | self.seam

    def after(self, values):
        return pltpu.roll(values, self.width - self.side, 1)

    def before(self, values):
        return pltpu.roll(values, self.side, 1)

    def beyond_z(self, values, afters):
        out = []
        for deep in range(BZB):
            joined = values[deep] if deep == 0 else jnp.where(self.at_back, afters[deep - 1], values[deep])
            out.append(pltpu.roll(joined, 1, 1))
        return out

    def ahead_z(self, values, befores):
        out = []
        for deep in range(BZB):
            joined = values[deep] if deep == BZB - 1 else jnp.where(self.at_front, befores[deep + 1], values[deep])
            out.append(pltpu.roll(joined, self.width - 1, 1))
        return out

    def across(self, held):
        befores = [self.before(v) for v in held]
        afters = [self.after(v) for v in held]
        aheads = self.ahead_z(held, befores)
        ky = [jnp.where(self.no_link, 0.0, mean(held[d], afters[d])) for d in range(BZB)]
        kz = [mean(held[d], aheads[d]) for d in range(BZB)]
        kz[BZB - 1] = jnp.where(self.at_back, 0.0, kz[BZB - 1])
        kzl = self.beyond_z(kz, [self.after(v) for v in kz])
        kzl[0] = jnp.where(self.at_front, 0.0, kzl[0])
        return [self.before(v) for v in ky], ky, kzl, kz

    def edges(self, d, held):
        out = jnp.where(self.low_edge | self.high_edge, held, 0.0)
        if d == 0:
            out = out + jnp.where(self.at_front, held, 0.0)
        if d == BZB - 1:
            out = out + jnp.where(self.at_back, held, 0.0)
        return out

    def sums(self, colour_id, held, downs, ups, behind_of, ahead_of, coefficient):
        afters = [self.after(v) for v in held]
        befores = [self.before(v) for v in held]
        behind = behind_of(held, afters)
        aheads = ahead_of(held, befores)
        out = []
        for at in range(len(held)):
            s, same, other, yl, yu, zl, zu = coefficient(at)
            across = jnp.where(self.odd == (colour_id == 1), downs[at], ups[at])
            part = s + same * held[at] + other * across
            part = part + (yl * befores[at] + yu * afters[at])
            out.append(part + (zl * behind[at] + zu * aheads[at]))
        return out

    def beyond_pairs(self, values, afters):
        last = (fall(afters[1], 4), afters[0])
        return [pltpu.roll(jnp.where(self.at_back, last[j], values[j]), 1, 1) for j in range(2)]

    def ahead_pairs(self, values, befores):
        following = (befores[1], fall(befores[0], 4))
        return [pltpu.roll(jnp.where(self.at_front, following[j], values[j]), self.width - 1, 1) for j in range(2)]

    def split(self, even, odd):
        return jnp.where(self.odd, odd, even), jnp.where(self.odd, even, odd)


def mean(one_side, other):
    return 2.0 * one_side * other / (one_side + other)


def scatter_tiles(ref, index, rows, values):
    for k in range(ref.shape[0]):
        ref[(k, index, rows)] = values[:, k * 128 : (k + 1) * 128]


def every_other(ref, index, start, count):
    tiles = [ref[k, index, pl.ds(start, count, stride=2), :] for k in range(ref.shape[0])]
    return jnp.concatenate(tiles, axis=1)


def couple_kernel(lanes, nodes, plane, block, fifth, *refs):
    first, black, same = refs[:3]
    red_refs, black_refs = refs[3:9], refs[9:15]
    totals = refs[15:17]
    natural = refs[17:]
    f, s, xl, xu, yl, yu, zl, zu, total = natural
    width, own_rows = block.shape[3], block.shape[2]
    grid = Stencil(width, SIDE, plane, lanes, nodes)
    cols = lax.broadcasted_iota(jnp.int32, (8, 128), 1)
    seam = (cols >= 3 * SIDE) & (cols < 5 * SIDE)
    for r in range(0, own_rows, 8):
        here = slice(r, r + 8)
        held = [block[2, d, here] for d in range(BZB)]
        across = grid.across(held)
        for d in range(BZB):
            for ref, values in zip((yl, yu, zl, zu), across):
                scatter_tiles(ref, d, here, values[d])
            scatter_tiles(f, d, here, block[0, d, here])
            if r + 8 < own_rows:
                up = mean(held[d], block[2, d, r + 1 : r + 9])
            else:
                up = jnp.where(grid.rows == 7, 0.0, mean(held[d], fall(held[d], 7)))
            if r:
                down = mean(held[d], block[2, d, r - 1 : r + 7])
            else:
                down = jnp.where(grid.rows == 0, 0.0, mean(held[d], fall(held[d], 1)))
            link = jnp.where(seam, mean(held[d][:, plane:width], fifth[1, d, here]), 0.0)
            extra = link * jnp.where(seam, fifth[0, d, here], 0.0)
            source = block[1, d, here]
            scatter_tiles(s, d, here, jnp.concatenate([source[:, 0:plane], source[:, plane:width] + extra], axis=1))
            scatter_tiles(xl, d, here, down)
            scatter_tiles(xu, d, here, up)
            part = down + up + across[0][d] + across[1][d] + across[2][d] + across[3][d] + grid.edges(d, held[d])
            scatter_tiles(total, d, here, jnp.concatenate([part[:, 0:plane], part[:, plane:width] + link], axis=1))
    for d in range(BZB):
        for t in range(own_rows // 16):
            to = slice(8 * t, 8 * t + 8)
            even = [every_other(ref, d, 16 * t, 8) for ref in natural]
            odd = [every_other(ref, d, 16 * t + 1, 8) for ref in natural]
            black[d, to] = grid.split(even[0], odd[0])[1]
            same[d, to] = even[3]
            pairs = [(even[1], odd[1]), (even[2], odd[3])] + [(even[k], odd[k]) for k in (4, 5, 6, 7)]
            for red_ref, black_ref, pair in zip(red_refs, black_refs, pairs):
                red_ref[d, to], black_ref[d, to] = grid.split(*pair)
            totals[0][d, to], totals[1][d, to] = grid.split(even[8], odd[8])
    for t in range(own_rows // 16):
        to = slice(8 * t, 8 * t + 8)
        held = [black[d, to] for d in range(BZB)]
        downs = [black[d, to.start - 1 : to.stop - 1] if t else fall(held[d], 1) for d in range(BZB)]
        ups = [black[d, to.start + 1 : to.stop + 1] if 8 * t + 8 < own_rows // 2 else fall(held[d], 7) for d in range(BZB)]
        parts = grid.sums(
            0, held, downs, ups, grid.beyond_z, grid.ahead_z,
            lambda d: (red_refs[0][d, to], same[d, to]) + tuple(ref[d, to] for ref in red_refs[1:]),
        )
        for d in range(BZB):
            first[d, to] = parts[d]


def smooth_kernel(lanes, nodes, covered, own_table, block, *refs):
    first, own_black, own_same = refs[:3]
    own = (refs[3:9], refs[9:15])
    own_totals = refs[15:17]
    from_pair, from_other, row_table, two_on, smoothed, coarse, flag = refs[17:24]
    fields, halos, others, totals, inverses = refs[24:26], refs[26:28], refs[28:30], refs[30:32], refs[32:34]
    halo_coefficients = (refs[34:41], refs[41:48])
    halo_inverses = refs[48:50]
    natural = refs[50:59]
    shown, rest, labels, label_sem = refs[59:]
    width = block.shape[3]
    own_rows = block.shape[2]
    side = smoothed.shape[1]
    plane = smoothed.shape[2]
    node, lane = lax.axis_index("node"), lax.axis_index("lane")
    fetch = pltpu.make_async_copy(own_table, labels, label_sem)
    fetch.start()
    grid = Stencil(width, side, plane, lanes, nodes)
    rows = grid.rows
    last = own_rows - 8
    compact = own_rows // 2
    even_node = (node & 1) == 0
    halo_beta, links = [], []
    f, s, xl, xu, yl, yu, zl, zu, total = natural

    def spot(d):
        return d % 2, slice(d // 2 * 8, d // 2 * 8 + 8)

    for d in range(BZB):
        strips = []
        for k in (d % 2, 2):
            unit = (d // 2 * 3 + k) * 3
            pair, other = (
                jnp.concatenate([message[unit + part] for part in range(width // 128)], axis=1)
                for message in (from_pair, from_other)
            )
            strips.append((jnp.where(even_node, other, pair), jnp.where(even_node, pair, other)))
        below, above = strips[0]
        field, beta, fifth_field, fifth_beta = unpack_rows(below, above)
        scatter_tiles(f, *spot(d), field)
        below, above = strips[1]
        source = jnp.where(rows < 4, above, below) if d % 2 == 0 else jnp.where(rows < 4, fall(above, 4), fall(below, 4))
        link = jnp.where((rows == 3) | (rows == 4), mean(beta, fifth_beta), 0.0)
        scatter_tiles(s, *spot(d), source + link * fifth_field)
        links.append(link)
        halo_beta.append(beta)
    across = grid.across(halo_beta)
    for d in range(BZB):
        held = halo_beta[d]
        for ref, values in zip((yl, yu, zl, zu), across):
            scatter_tiles(ref, *spot(d), values[d])
        up = mean(held, jnp.where(rows == 7, fall(block[2, d, 0:8], 7), fall(held, 7)))
        up = jnp.where((rows == 3) | ((rows == 7) & grid.first_node), 0.0, up)
        down = jnp.where(grid.last_node, 0.0, mean(held, fall(block[2, d, last:own_rows], 1)))
        down = jnp.where(rows == 0, down, fall(up, 1))
        scatter_tiles(xl, *spot(d), down)
        scatter_tiles(xu, *spot(d), up)
        whole = links[d] + down + up + across[0][d] + across[1][d] + across[2][d] + across[3][d] + grid.edges(d, held)
        scatter_tiles(total, *spot(d), whole)
        low_link = jnp.where(rows == 0, fall(up, 1), 0.0)
        high_link = jnp.where(rows == 7, fall(down, 7), 0.0)
        low_whole = low_link + jnp.where((rows == 0) & grid.first_node, block[2, d, 0:8], 0.0)
        high_whole = high_link + jnp.where((rows == 7) & grid.last_node, block[2, d, last:own_rows], 0.0)
        for c in range(2):
            at_low, at_high = grid.odd == (c == 1), grid.odd == (c == 0)
            for t in range(compact // 8):
                to = slice(8 * t, 8 * t + 8)
                other, whole = own[c][1][d, to], own_totals[c][d, to]
                if t == 0:
                    other = other + jnp.where(at_low, low_link, 0.0)
                    whole = whole + jnp.where(at_low, low_whole, 0.0)
                if t == compact // 8 - 1:
                    other = other + jnp.where(at_high, high_link, 0.0)
                    whole = whole + jnp.where(at_high, high_whole, 0.0)
                others[c][d, to] = other
                totals[c][d, to] = whole
                inverses[c][d, to] = 1.0 / whole
        fields[1][d, 8 : 8 + compact] = own_black[d]

    def spread(c, j):
        tile = halos[c][j]
        turned = fall(tile, 4)
        fields[c][j, 8 + compact : 16 + compact] = tile
        fields[c][j, 0:8] = turned
        fields[c][j + 2, 8 + compact : 16 + compact] = turned
        fields[c][j + 2, 0:8] = tile

    for j in range(2):
        even = [every_other(ref, j, 0, 8) for ref in natural]
        odd = [every_other(ref, j, 1, 8) for ref in natural]
        halos[1][j] = grid.split(even[0], odd[0])[1]
        spread(1, j)
        pairs = [(even[1], odd[1]), (even[2], odd[3])] + [(even[k], odd[k]) for k in (4, 5, 6, 7)]
        for k, pair in enumerate(pairs):
            at = k if k == 0 else k + 1
            halo_coefficients[0][at][j], halo_coefficients[1][at][j] = grid.split(*pair)
        for c in range(2):
            halo_coefficients[c][1][j] = even[3]
        for c, whole in enumerate(grid.split(even[8], odd[8])):
            halo_inverses[c][j] = 1.0 / whole

    def own_sums(c, t):
        opposite = fields[1 - c]
        start = 8 + 8 * t
        held = [opposite[d, start : start + 8] for d in range(BZB)]
        downs = [opposite[d, start - 1 : start + 7] for d in range(BZB)]
        ups = [opposite[d, start + 1 : start + 9] for d in range(BZB)]
        to = slice(8 * t, 8 * t + 8)

        def coefficient(d):
            return (own[c][0][d, to], own_same[d, to], others[c][d, to]) + tuple(ref[d, to] for ref in own[c][2:])

        return grid.sums(c, held, downs, ups, grid.beyond_z, grid.ahead_z, coefficient)

    def end_terms(t):
        out = []
        for d in range(BZB):
            part = 0.0
            to = slice(8 * t, 8 * t + 8)
            if t == 0:
                low = others[0][d, to] * fields[1][d, 7:15]
                part = part + jnp.where((rows == 0) & ~grid.odd, low, 0.0)
            if t == compact // 8 - 1:
                high = others[0][d, to] * fields[1][d, 9 + 8 * t : 17 + 8 * t]
                part = part + jnp.where((rows == 7) & grid.odd, high, 0.0)
            out.append(first[d, to] + part)
        return out

    quarter = rows & 3
    for sweep in range(SWEEPS):
        for c in (0, 1):
            held = [halos[1 - c][j] for j in range(2)]
            opposite = fields[1 - c]
            downs, ups = [], []
            for j in range(2):
                lows = [opposite[d, compact : compact + 8] for d in (j, j + 2)]
                highs = [opposite[d, 8:16] for d in (j, j + 2)]
                joined = jnp.where(rows < 4, fall(lows[0], 1), fall(lows[1], 5))
                downs.append(jnp.where(quarter == 0, joined, fall(held[j], 1)))
                joined = jnp.where(rows < 4, fall(highs[0], 3), fall(highs[1], 7))
                ups.append(jnp.where(quarter == 3, joined, fall(held[j], 7)))
            parts = grid.sums(
                c, held, downs, ups, grid.beyond_pairs, grid.ahead_pairs,
                lambda j: tuple(ref[j] for ref in halo_coefficients[c]),
            )
            for j in range(2):
                halos[c][j] = parts[j] * halo_inverses[c][j]
                spread(c, j)
            for t in range(compact // 8):
                parts = end_terms(t) if sweep + c == 0 else own_sums(c, t)
                for d in range(BZB):
                    fields[c][d, 8 + 8 * t : 16 + 8 * t] = parts[d] * inverses[c][d, 8 * t : 8 * t + 8]

    fetch.wait()
    count = smoothed.shape[0]
    for t in range(compact // 8):
        to, own_to = slice(8 * t, 8 * t + 8), slice(8 + 8 * t, 16 + 8 * t)
        left = [own_sums(c, t) for c in range(2)]
        for d in range(BZB):
            slot = labels[t * BZB + d, 12].astype(jnp.int32)
            now = [fields[c][d, own_to] for c in range(2)]
            both = left[0][d] - totals[0][d, to] * now[0] + (left[1][d] - totals[1][d, to] * now[1])
            even, odd = grid.split(*now)
            for k in range(plane // 128):
                cut = slice(k * 128, (k + 1) * 128)
                rest[k, pl.ds(pl.multiple_of(slot * 8, 8), 8), :] = both[:, cut]
                shown[k, pl.ds(slot * side, 8, stride=2), :] = even[:, cut]
                shown[k, pl.ds(slot * side + 1, 8, stride=2), :] = odd[:, cut]
    for i in range(count):
        for k in range(plane // 128):
            smoothed[i, :, k * 128 : (k + 1) * 128] = shown[k, i * side : (i + 1) * side]

    small = side // 2
    cells = lax.broadcasted_iota(jnp.int32, (plane, 128), 0)
    slots = lax.broadcasted_iota(jnp.int32, (plane, 128), 1)
    goal = lax.div(lax.div(cells, side), 2) * small + lax.div(lax.rem(cells, side), 2)
    per = small * small
    acc = 0.0
    pairs = small * per // 128
    for inner in range(128 // per):
        stack = []
        for pair in range(pairs):
            i = pair * (128 // per) + inner
            tiles = [rest[k, pl.ds(i, count, stride=small), :] for k in range(plane // 128)]
            stack.append(jnp.concatenate(tiles, axis=1))
        pooling = (goal + inner * per == slots).astype(jnp.float32)
        acc = acc + jnp.dot(
            jnp.concatenate(stack, axis=0), pooling, precision=lax.Precision.HIGHEST, preferred_element_type=jnp.float32
        )
    for pair in range(pairs):
        coarse[:, pair * 128 : (pair + 1) * 128] = 0.125 * acc[pair * count : (pair + 1) * count]

    mine = from_pair.shape[0] - 1
    rows1 = lax.broadcasted_iota(jnp.int32, (8, 128), 0)
    cols1 = lax.broadcasted_iota(jnp.int32, (8, 128), 1)
    owner = lax.rem(lax.div(cols1, 8), 8)
    field_of = lax.rem(cols1, 8)
    table_here, opposite = row_table[...], two_on[...]
    pair, other = from_pair[mine], from_other[mine]
    lower, upper = jnp.where(even_node, other, pair), jnp.where(even_node, pair, other)
    rows_of = [(table_here, lower, upper, node), (lower, opposite, table_here, lax.rem(node + nodes - 1, nodes)),
               (upper, table_here, opposite, lax.rem(node + 1, nodes)), (opposite, upper, lower, lax.rem(node + 2, nodes))]
    if not covered:
        rows_of = rows_of[:1]
    lane_of = lax.rem(lane - jnp.where(owner > 4, owner - 8, owner) + 2 * lanes, lanes)
    wrong = jnp.zeros((8, 128), jnp.float32)
    for table, low, high, at_node in rows_of:
        turned = pltpu.roll(table, 4, 0)
        at_low = jnp.where(rows1 >= 4, turned, jnp.where(at_node == 0, -1.0, pltpu.roll(low, 4, 0)))
        at_high = jnp.where(rows1 < 4, turned, jnp.where(at_node == nodes - 1, -1.0, pltpu.roll(high, 4, 0)))
        y_low = jnp.where(lane_of == 0, -1.0, pltpu.roll(table, 128 - 8, 1))
        y_high = jnp.where(lane_of == lanes - 1, -1.0, pltpu.roll(table, 8, 1))
        z_low = jnp.where(lax.rem(rows1, BZB) == 0, -1.0, pltpu.roll(table, 1, 0))
        z_high = jnp.where(lax.rem(rows1, BZB) == BZB - 1, -1.0, pltpu.roll(table, 7, 0))
        bad = jnp.where((field_of == 0) & (table < 0), 1.0, 0.0)
        for face, expected in enumerate((at_low, at_high, y_low, y_high, z_low, z_high)):
            differs = table != pltpu.roll(expected, 1 + face, 1)
            bad = bad + jnp.where((field_of == 1 + face) & differs, 1.0, 0.0)
        if not covered:
            bad = jnp.where(owner == 0, bad, 0.0)
        wrong = wrong + bad
    flag[0, 0] = (jnp.sum(wrong) > 0).astype(jnp.int32)


ROOM = pltpu.CompilerParams(vmem_limit_bytes=32 * 2**20)
FULL = pltpu.CompilerParams(vmem_limit_bytes=60 * 2**20)
SCALARS = pl.BlockSpec(memory_space=pltpu.SMEM)
VECTORS = pl.BlockSpec(memory_space=pltpu.VMEM)


def fast_body(old_field, old_source, diffusivity, target_box, neighbours):
    count, side, plane = old_field.shape
    half = plane // 2
    lanes, nodes = lax.axis_size("lane"), lax.axis_size("node")
    arrays = (old_field, old_source, diffusivity, target_box, neighbours)
    moves, plan = lane_plan(lanes)
    covered = lanes == 8 and nodes == 4
    units = [plan_units(count, *parts) for parts in plan.values()]
    f32 = jnp.float32
    packed = pl.pallas_call(
        lambda *refs: pack_kernel(moves, plan, lanes, count, *refs),
        name="pack_moves",
        out_shape=[pltpu.VMEM((n, side, half), f32) for n in units]
        + [pltpu.VMEM(array.shape, array.dtype) for array in arrays]
        + [pltpu.VMEM((8, 128), f32)],
        in_specs=[pl.BlockSpec(memory_space=pltpu.HBM)] * 5,
        out_specs=[VECTORS] * (len(units) + 6),
        scratch_shapes=[
            pltpu.SMEM(target_box.shape, jnp.int32),
            pltpu.SMEM(neighbours.shape, jnp.int32),
            pltpu.SMEM((count,), jnp.int32),
            pltpu.SemaphoreType.DMA((7,)),
        ],
        compiler_params=FULL,
    )(*arrays)
    messages, own_table = packed[:-6], packed[-1]
    field, source, beta, target_held, neighbours_held = packed[-6:-1]
    got = {}
    late = [lanes // 2, lanes // 2 + 1]
    near = [1, lanes - 1, 2, lanes - 2]
    for offset in near + [offset for offset in plan if offset not in near + late] + late:
        message = messages[list(plan).index(offset)]
        if offset in late:
            message, _ = lax.optimization_barrier((message, got[2]))
        got[offset] = lax.ppermute(message, "lane", [(i, (i + offset) % lanes) for i in range(lanes)])
    got = [got[offset] for offset in plan]
    width = plane + 128
    strips = BZB // 2 * 9 + 1
    sides = pltpu.VMEM((5, BZB + 1, BXD * side, 128), f32)
    block, fifth, to_pair, to_other, row_table = pl.pallas_call(
        lambda *refs: assemble_kernel(moves, plan, lanes, count, *refs),
        name="assemble_block",
        out_shape=[
            pltpu.VMEM((3, BZB + 1, BXD * side, width), f32),
            pltpu.VMEM((2, BZB, BXD * side, 128), f32),
            pltpu.VMEM((strips, 8, 128), f32),
            pltpu.VMEM((strips, 8, 128), f32),
            pltpu.VMEM((8, 128), f32),
        ],
        in_specs=[VECTORS] * (4 + len(units)),
        out_specs=[VECTORS] * 5,
        scratch_shapes=[
            sides,
            sides,
        ],
        compiler_params=ROOM,
    )(own_table, field, source, beta, *got)
    from_pair = lax.ppermute(to_pair, "node", [(i, i ^ 1) for i in range(nodes)])
    from_other = lax.ppermute(to_other, "node", [(i, (i - 1 + 2 * (i % 2)) % nodes) for i in range(nodes)])
    two_on = lax.ppermute(row_table, "node", [(i, (i + 2) % nodes) for i in range(nodes)])
    tiles, rows = width // 128, BXD * side
    half_rows = pltpu.VMEM((BZB, rows // 2, width), f32)
    coupled = pl.pallas_call(
        lambda *refs: couple_kernel(lanes, nodes, plane, *refs),
        name="couple_block",
        out_shape=[half_rows] * 17,
        in_specs=[VECTORS] * 2,
        out_specs=[VECTORS] * 17,
        scratch_shapes=[pltpu.VMEM((tiles, BZB, rows, 128), f32)] * 9,
        compiler_params=ROOM,
    )(block, fifth)
    pair_tile = pltpu.VMEM((2, 8, width), f32)
    smoothed, coarse, flag = pl.pallas_call(
        lambda *refs: smooth_kernel(lanes, nodes, covered, *refs),
        name="smooth_block",
        out_shape=[
            jax.ShapeDtypeStruct((count, side, plane), f32),
            jax.ShapeDtypeStruct((count, (side // 2) ** 3), f32),
            jax.ShapeDtypeStruct((1, 1), jnp.int32),
        ],
        in_specs=[VECTORS] * (2 + 17 + 4),
        out_specs=[VECTORS, VECTORS, SCALARS],
        scratch_shapes=[pltpu.VMEM((BZB, rows // 2 + 16, width), f32)] * 2
        + [pair_tile] * 2
        + [half_rows] * 6
        + [pair_tile] * 16
        + [pltpu.VMEM((tiles, 2, 16, 128), f32)] * 9
        + [pltpu.VMEM((plane // 128, count * side, 128), f32), pltpu.VMEM((plane // 128, count * side // 2, 128), f32)]
        + [pltpu.SMEM((8, 128), f32), pltpu.SemaphoreType.DMA],
        compiler_params=ROOM,
    )(own_table, block, *coupled, from_pair, from_other, row_table, two_on)
    irregular = flag[0, 0]
    if not covered:
        irregular = lax.pmax(irregular, ("node", "lane"))

    def again(carry):
        out = general_body(field, source, beta, target_held, neighbours_held)
        return (*out, jnp.int32(0))

    smoothed, coarse, _ = lax.while_loop(lambda carry: carry[2] > 0, again, (smoothed, coarse, irregular))
    return smoothed, coarse


def solution(mesh):
    in_specs = (
        P(("node", "lane"), None, None),
        P(("node", "lane"), None, None),
        P(("node", "lane"), None, None),
        P(("node", "lane")),
        P(("node", "lane"), None),
    )
    out_specs = (P(("node", "lane"), None, None), P(("node", "lane"), None))
    return jax.shard_map(fast_body, mesh=mesh, in_specs=in_specs, out_specs=out_specs, check_vma=False)
```

```python
import jax
import jax.numpy as jnp
from jax import lax
from jax.experimental import pallas as pl
from jax.experimental.pallas import tpu as pltpu
from jax.sharding import PartitionSpec as P

SWEEPS = 2


OPPOSITE = (1, 0, 3, 2, 5, 4)


def with_halo(block, sides, width):
    for axis, dim in sides:
        count = lax.axis_size(axis)
        forward = [(i, i + 1) for i in range(count - 1)]
        backward = [(target, source) for source, target in forward]
        low = lax.ppermute(
            lax.slice_in_dim(block, block.shape[dim] - width, None, axis=dim), axis, forward
        )
        high = lax.ppermute(lax.slice_in_dim(block, 0, width, axis=dim), axis, backward)
        block = jnp.concatenate([low, block, high], axis=dim)
    return block


def face_layers(values):
    boxes, side, plane = values.shape
    return jnp.stack(
        [
            values[:, 0],
            values[:, side - 1],
            values[:, :, :side].reshape(boxes, plane),
            values[:, :, plane - side :].reshape(boxes, plane),
            values[:, :, 0::side].reshape(boxes, plane),
            values[:, :, side - 1 :: side].reshape(boxes, plane),
        ],
        axis=1,
    )


def near_values(values, ghost):
    boxes, side, plane = values.shape
    lower_x = jnp.concatenate([ghost[:, 0][:, None, :], values[:, :-1]], axis=1)
    upper_x = jnp.concatenate([values[:, 1:], ghost[:, 1][:, None, :]], axis=1)
    lower_y = jnp.concatenate(
        [ghost[:, 2].reshape(boxes, side, side), values[:, :, : plane - side]], axis=2
    )
    upper_y = jnp.concatenate([values[:, :, side:], ghost[:, 3].reshape(boxes, side, side)], axis=2)
    depth = jnp.arange(plane) % side
    lower_z = jnp.where(
        depth == 0,
        jnp.repeat(ghost[:, 4].reshape(boxes, side, side), side, axis=2),
        jnp.roll(values, 1, axis=2),
    )
    upper_z = jnp.where(
        depth == side - 1,
        jnp.repeat(ghost[:, 5].reshape(boxes, side, side), side, axis=2),
        jnp.roll(values, -1, axis=2),
    )
    return [lower_x, upper_x, lower_y, upper_y, lower_z, upper_z]


def coefficients(diffusivity, beside):
    return [2.0 * diffusivity * other / (diffusivity + other) for other in beside]


def relax(values, source, couplings, beside, chosen):
    total = couplings[0]
    summed = source + couplings[0] * beside[0]
    for face in range(1, 6):
        total = total + couplings[face]
        summed = summed + couplings[face] * beside[face]
    return jnp.where(chosen, summed / total, values)


def defect_of(values, source, couplings, beside):
    total = couplings[0]
    summed = source + couplings[0] * beside[0]
    for face in range(1, 6):
        total = total + couplings[face]
        summed = summed + couplings[face] * beside[face]
    return summed - total * values


def colour_of(side, plane):
    rows = jnp.arange(side)[:, None]
    cells = jnp.arange(plane)[None, :]
    return (rows + cells // side + cells % side) % 2


def restrict(values):
    boxes, side, plane = values.shape
    half = side // 2
    paired = values.reshape(boxes, half, 2, plane).sum(axis=2)
    cells = jnp.arange(plane)
    coarse_cols = cells // side // 2 * half + cells % side // 2
    pooling = (coarse_cols[:, None] == jnp.arange(half * half)[None, :]).astype(jnp.float32)
    summed = jnp.einsum("bxp,pq->bxq", paired, pooling, precision=lax.Precision.HIGHEST)
    return (0.125 * summed).reshape(boxes, half * half * half)


def place(settled, arrived, tags):
    count = settled.shape[0]
    return settled.at[jnp.where(tags > 0, tags - 1, count)].set(arrived, mode="drop")


def general_body(old_field, old_source, diffusivity, target_box, neighbours):
    count, side, plane = old_field.shape
    lane_count = lax.axis_size("lane")
    lane_here = lax.axis_index("lane")
    own_device = lax.axis_index("node") * lane_count + lane_here
    dest_device = target_box // count
    dest_slot = target_box % count
    staying = dest_device == own_device
    cargo = jnp.stack([old_field, old_source], axis=1)
    settled = jnp.zeros_like(cargo).at[jnp.where(staying, dest_slot, count)].set(cargo, mode="drop")
    slots = jnp.arange(count)
    peers = own_device - lane_here + jnp.arange(lane_count)
    chosen = (dest_device[None, :] == peers[:, None]) & jnp.logical_not(staying)[None, :]
    filled = jnp.any(chosen, axis=1)
    picked = jnp.sum(jnp.where(chosen, slots[None, :], 0), axis=1)
    parcels = jnp.where(filled[:, None, None, None], cargo[picked], 0.0)
    labels = jnp.where(filled, jnp.sum(jnp.where(chosen, dest_slot[None, :], 0), axis=1) + 1, 0)
    arrived, tags = (
        lax.all_to_all(parcels, "lane", split_axis=0, concat_axis=0, tiled=True),
        lax.all_to_all(labels, "lane", split_axis=0, concat_axis=0, tiled=True),
    )
    settled = place(settled, arrived, tags)
    field = settled[:, 0]
    source = settled[:, 1]
    present = neighbours >= 0
    near_device = jnp.where(present, neighbours // count, own_device)
    local_row = neighbours % count * 6 + jnp.array(OPPOSITE, jnp.int32)[None, :]
    across = near_device - own_device
    anchor = jnp.where(
        across == -lane_count,
        1,
        jnp.where(
            across == lane_count, 2, jnp.where(across == -1, 3, jnp.where(across == 1, 4, 0))
        ),
    )
    index = anchor * (count * 6) + local_row
    width_out = count * 6

    def departing_boxes(layers):
        return layers.reshape(count * 6, plane)

    def incoming(received, start):
        return jnp.concatenate(
            [
                received[0, 1, start : start + width_out],
                received[2, 1, start : start + width_out],
                received[1, 0, start : start + width_out],
                received[1, 2, start : start + width_out],
            ],
            axis=0,
        )

    def trade(rows):
        return with_halo(rows[None, None], (("node", 0), ("lane", 1)), 1)

    def ghosts(layers, remote_rows, fallback):
        table = jnp.concatenate([layers.reshape(count * 6, plane), remote_rows], axis=0)
        return jnp.where(present[..., None], table[index], fallback)

    beta_layers = face_layers(diffusivity)
    layers = face_layers(field)
    received = trade(
        jnp.concatenate([departing_boxes(layers), departing_boxes(beta_layers)], axis=0)
    )
    beta_ghost = ghosts(beta_layers, incoming(received, width_out), beta_layers)
    couplings = coefficients(diffusivity, near_values(diffusivity, beta_ghost))
    colour = colour_of(side, plane)
    for sweep in range(SWEEPS):
        for colour_id in (0, 1):
            if sweep + colour_id > 0:
                layers = face_layers(field)
                received = trade(departing_boxes(layers))
            ghost = ghosts(layers, incoming(received, 0), jnp.zeros_like(layers))
            field = relax(field, source, couplings, near_values(field, ghost), colour == colour_id)
    layers = face_layers(field)
    received = trade(departing_boxes(layers))
    ghost = ghosts(layers, incoming(received, 0), jnp.zeros_like(layers))
    coarse = restrict(defect_of(field, source, couplings, near_values(field, ghost)))
    return (field, coarse)


BXD = 2
BZB = 4
PAD = 8
SIDE = 16
LOW, HIGH = "low", "high"


def lane_plan(lanes):
    half = lanes // 2
    moves = [1, lanes - 1, 2, lanes - 2, half]
    ends = {}
    for move in moves:
        for offset, part in ((move + 1, HIGH), (move - 1, LOW)):
            ends.setdefault(offset % lanes, []).append((move, part))
    bulk = {1: HIGH, lanes - 1: LOW}
    plan = {}
    for offset in sorted(set(moves) | set(ends)):
        if offset:
            plan[offset] = (bulk.get(offset), offset in moves, ends.get(offset, []))
    return moves, plan


def plan_units(count, bulk, whole, kept):
    return (count + count // 2 if bulk is not None else 0) + (4 if whole else 0) + len(kept) + 1


def cell_lanes(side):
    rows = lax.broadcasted_iota(jnp.int32, (side, 128), 0)
    cols = lax.broadcasted_iota(jnp.int32, (side, 128), 1)
    layer = cols >> (side.bit_length() - 1)
    black = ((rows + layer + cols) & 1) == 1
    return layer, black


def turn(values, shift):
    return pltpu.roll(values, shift % values.shape[-1], values.ndim - 1)


def pack_end(part, field, source, beta, masks):
    side = field.shape[0]
    y, black = masks
    if part == HIGH:
        pairs = turn(jnp.where(black, field, turn(field, -side)), 4 * side)
        out = jnp.where(y >= 4, source, pairs)
        out = jnp.where(y == 3, field, out)
        return out if beta is None else jnp.where(y == 1, turn(beta, -2 * side), out)
    pairs = turn(jnp.where(black, field, turn(field, side)), 4 * side)
    out = jnp.where(y < 4, source, pairs)
    out = jnp.where(y == 4, field, out)
    return out if beta is None else jnp.where(y == 6, turn(beta, 2 * side), out)


def unpack_end(part, packed):
    side = packed.shape[0]
    y, _ = cell_lanes(side)
    if part == HIGH:
        return jnp.where((y & 1) == 0, turn(packed, 4 * side), turn(packed, 5 * side))
    return jnp.where((y & 1) == 1, turn(packed, 4 * side), turn(packed, -5 * side))


def part_lanes(part, plane):
    return slice(0, plane // 2) if part == LOW else slice(plane // 2, plane)


def pack_kernel(moves, plan, lanes, count, *refs):
    outs = refs[5 : 5 + len(plan)]
    held_here = refs[5 + len(plan) : 10 + len(plan)]
    table, target, near, slots, sems = refs[10 + len(plan) :]
    pairs = [*zip(refs[3:5], (target, near)), *zip(refs[:5], held_here)]
    fetch = [pltpu.make_async_copy(src, dst, sems.at[k]) for k, (src, dst) in enumerate(pairs)]
    for copy in fetch:
        copy.start()
    for copy in fetch[:2]:
        copy.wait()
    field, source, beta = held_here[:3]
    side, plane = field.shape[1:]
    half = plane // 2
    lane = lax.axis_index("lane")
    first = (lax.axis_index("node") * lanes + lane) * count
    old_index = [jnp.int32(0)] * len(moves)
    new_slot = [jnp.int32(-1)] * len(moves)
    stay = []
    for i in range(count):
        there = target[i]
        slot = lax.rem(there, count)
        step = lax.rem(lax.rem(lax.div(there, count), lanes) - lane + lanes, lanes)
        stay.append(jnp.where(step == 0, slot, -1))
        for k, move in enumerate(moves):
            old_index[k] = jnp.where(step == move, i, old_index[k])
            new_slot[k] = jnp.where(step == move, slot, new_slot[k])
    for i in range(count):
        slots[i] = -1

    def local(index, face):
        there = near[index, face]
        inside = (there >= first) & (there < first + count)
        return inside, jnp.clip(there - first, 0, count - 1)

    place = []
    for i in range(count):
        inside, below = local(i, 0)
        depth = jnp.int32(0)
        live, at = local(i, 4)
        for _ in range(BZB - 1):
            depth = depth + jnp.where(live, 1, 0)
            further, onward = local(at, 4)
            live, at = live & further, onward
        spot = jnp.where(inside, BZB, 0) + depth
        place.append(spot)
        slots[spot] = i
    rows = lax.broadcasted_iota(jnp.int32, (8, 128), 0)
    cols = lax.broadcasted_iota(jnp.int32, (8, 128), 1)
    spots = rows * 128 + cols
    held = jnp.zeros((8, 128), jnp.int32)

    def put(held, row, col, value):
        return jnp.where(spots == row * 128 + col, value, held)

    for i in range(count):
        slot = slots[i]
        held = put(held, i, 12, jnp.maximum(slot, 0))
        held = put(held, i, 0, jnp.where(slot < 0, -7, first + slot))
        for face in range(6):
            held = put(held, i, 1 + face, near[jnp.maximum(slot, 0), face])
    words = [
        sum(place[i] << 3 * i for i in range(count)),
        sum((stay[i] + 1) << 4 * i for i in range(count // 2)),
        sum((stay[i] + 1) << 4 * (i - count // 2) for i in range(count // 2, count)),
        sum((new_slot[k] + 1) << 4 * k for k in range(len(moves))),
        sum(old_index[k] << 3 * k for k in range(len(moves))),
    ]
    for k, word in enumerate(words):
        held = put(held, 0, 16 + k, word)
    table[...] = held.astype(jnp.float32)
    for copy in fetch[2:]:
        copy.wait()
    masks = cell_lanes(side)
    left = lax.broadcasted_iota(jnp.int32, (side, 128), 1) < 64
    for out, (bulk, whole, kept) in zip(outs, plan.values()):
        if bulk is not None:
            cut = part_lanes(bulk, plane)
            for i in range(count):
                out[i] = pack_end(bulk, field[i, :, cut], source[i, :, cut], beta[i, :, cut], masks)
            for i in range(0, count, 2):
                one, two = beta[i, :, cut], turn(beta[i + 1, :, cut], 64)
                out[count + i // 2] = jnp.where(left, two, one) if bulk == HIGH else jnp.where(left, one, two)
    for (offset, (bulk, whole, kept)), out in zip(plan.items(), outs):
        unit = count + count // 2 if bulk is not None else 0
        low, high = part_lanes(LOW, plane), part_lanes(HIGH, plane)
        if whole:
            box = old_index[moves.index(offset)]
            for k, array in enumerate((field, source)):
                out[unit + 2 * k] = array[box, :, low]
                out[unit + 2 * k + 1] = array[box, :, high]
            unit += 4
        for move, part in kept:
            box = old_index[moves.index(move)]
            cut = part_lanes(part, plane)
            out[unit] = pack_end(part, field[box, :, cut], source[box, :, cut], None, masks)
            unit += 1
    for out in outs:
        out[out.shape[0] - 1, 0:8] = table[...]


def assemble_kernel(moves, plan, lanes, count, *refs):
    own_table, field, source, beta = refs[:4]
    got = dict(zip(plan, refs[4 : 4 + len(plan)]))
    block, fifth, to_pair, to_other, row_table, low_side, high_side = refs[4 + len(plan) :]
    side, plane = field.shape[1:]
    half = plane // 2

    def table_of(offset):
        return got[offset].at[got[offset].shape[0] - 1, 0:8] if offset else own_table

    words = {}
    for offset in (0, *plan):
        line = table_of(offset)[0:1, :].astype(jnp.int32)
        words[offset] = [line[0, 16 + k] for k in range(5)]

    cols = lax.broadcasted_iota(jnp.int32, (8, 128), 1)
    shown = [offset for offset in plan if lanes == 8 or offset in (1, lanes - 1)]
    joined = jnp.where(cols < 8, own_table[...], 0.0)
    for offset in shown:
        at = offset if offset < 7 else 7
        joined = joined + pltpu.roll(jnp.where(cols < 8, table_of(offset)[...], 0.0), 8 * at, 1)
    joined = joined + pltpu.roll(joined, 64, 1)
    row_table[...] = joined
    to_pair[to_pair.shape[0] - 1] = joined
    to_other[to_other.shape[0] - 1] = joined

    def place_of(offset, slot):
        code = (words[offset][0] >> 3 * slot) & 7
        return code & (BZB - 1), (code >> 2) * side

    def stays(offset, i):
        return ((words[offset][1 + i // (count // 2)] >> 4 * (i % (count // 2))) & 15) - 1

    def moved(offset, k):
        return ((words[offset][3] >> 4 * k) & 15) - 1

    def spot_at(offset, slot):
        deep, row = place_of(offset, jnp.maximum(slot, 0))
        return jnp.where(slot >= 0, deep, BZB), jnp.where(slot >= 0, row, 0)

    def put(ref, array, spot, values, where=slice(None)):
        deep, row = spot
        ref[array, deep, pl.ds(pl.multiple_of(row, side), side), where] = values

    low, high, whole = slice(0, half), slice(half, plane), slice(0, plane)
    for i in range(count):
        put(block, 2, place_of(0, i), beta[i], whole)
        spot = spot_at(0, stays(0, i))
        put(block, 0, spot, field[i], whole)
        put(block, 1, spot, source[i], whole)

    below, above = 1, lanes - 1
    sides = {HIGH: (low_side, below, side), LOW: (high_side, above, -side)}

    def put_end(part, slot, layers, raw, sources):
        ref, offset, shift = sides[part]
        spot = spot_at(offset, slot)
        put(ref, 0, spot, layers)
        put(ref, 1, spot, sources)
        put(ref, 3, spot, turn(raw, shift))

    for move, part in ((1, LOW), (lanes - 1, HIGH)):
        k = moves.index(move)
        box, cut = (words[0][4] >> 3 * k) & 7, part_lanes(part, plane)
        raw = field[box, :, cut]
        put_end(part, moved(0, k), raw, raw, source[box, :, cut])

    for offset, (bulk, entire, kept) in plan.items():
        message = got[offset]
        unit = 0
        if bulk is not None:
            ref, _, shift = sides[bulk]
            for i in range(count):
                packed = message[i]
                put_end(bulk, stays(offset, i), unpack_end(bulk, packed), packed, packed)
                joint = message[count + i // 2]
                spot = place_of(offset, i)
                put(ref, 2, spot, joint if i % 2 == 0 else turn(joint, 64))
                put(ref, 4, spot, turn(packed, 3 * shift))
            unit = count + count // 2
        if entire:
            spot = spot_at(0, moved(offset, moves.index(offset)))
            for k in range(2):
                put(block, k, spot, message[unit + 2 * k], low)
                put(block, k, spot, message[unit + 2 * k + 1], high)
            unit += 4
        for move, part in kept:
            packed = message[unit]
            put_end(part, moved(offset, moves.index(move)), unpack_end(part, packed), packed, packed)
            unit += 1

    rows, width = block.shape[2:]
    left = lax.broadcasted_iota(jnp.int32, (rows, 128), 1) < 64
    for d in range(BZB):
        for k in range(3):
            block[k, d, :, plane:width] = jnp.where(left, high_side[k, d], low_side[k, d])
        for k in range(2):
            fifth[k, d] = jnp.where(left, high_side[3 + k, d], low_side[3 + k, d])
    even_node = (lax.axis_index("node") & 1) == 0
    for deep in range(0, BZB, 2):
        strips = []
        for start, up in ((rows - 8, True), (0, False)):
            tiles = []
            sources = []
            for d in (deep, deep + 1):
                f, s, b = (block[k, d, start : start + 8] for k in range(3))
                tiles.append(pack_rows(up, f, b))
                sources.append(s)
            strips.append(tiles + [pack_sources(up, *sources)])
        for k, (up, down) in enumerate(zip(*strips)):
            for part in range(width // 128):
                cut, unit = slice(part * 128, (part + 1) * 128), (deep // 2 * 3 + k) * 3 + part
                to_pair[unit] = jnp.where(even_node, up[:, cut], down[:, cut])
                to_other[unit] = jnp.where(even_node, down[:, cut], up[:, cut])


def row_colours(width, side):
    rows = lax.broadcasted_iota(jnp.int32, (8, width), 0)
    cols = lax.broadcasted_iota(jnp.int32, (8, width), 1)
    return rows, (rows + (cols >> (side.bit_length() - 1)) + cols) & 1


def fall(values, shift):
    return pltpu.roll(values, shift % 8, 0)


def pack_rows(up, field, beta):
    rows, colour = row_colours(field.shape[1], SIDE)
    if up:
        pairs = jnp.where(colour == 1, field, fall(field, 1))
        out = jnp.where(rows == 0, fall(pairs, 1), beta)
        out = jnp.where(rows == 1, fall(pairs, 4), out)
        return jnp.where(rows == 2, fall(pairs, 7), out)
    pairs = jnp.where(colour == 1, field, fall(field, 7))
    out = jnp.where(rows == 7, fall(pairs, 7), beta)
    out = jnp.where(rows == 6, fall(pairs, 4), out)
    return jnp.where(rows == 5, fall(pairs, 1), out)


def unpack_rows(below, above):
    rows = lax.broadcasted_iota(jnp.int32, below.shape, 0)
    field = fall(above, 1)
    for row, tile, shift in ((1, above, 2), (2, above, 4), (3, above, 5), (4, below, 3), (5, below, 4), (6, below, 6), (7, below, 7)):
        field = jnp.where(rows == row, fall(tile, shift), field)
    beta = jnp.where(rows < 4, above, below)
    fifth_field = jnp.where(rows < 4, fall(above, 6), fall(below, 2))
    fifth_beta = jnp.where(rows < 4, fall(above, 7), fall(below, 1))
    return field, beta, fifth_field, fifth_beta


def pack_sources(up, first, second):
    rows = lax.broadcasted_iota(jnp.int32, first.shape, 0)
    return jnp.where(rows >= 4, first, fall(second, 4)) if up else jnp.where(rows < 4, first, fall(second, 4))


class Stencil:
    def __init__(self, width, side, plane, lanes, nodes):
        self.width, self.side, self.plane = width, side, plane
        node, lane = lax.axis_index("node"), lax.axis_index("lane")
        self.first_node, self.last_node = node == 0, node == nodes - 1
        self.rows, self.colour = row_colours(width, side)
        cols = lax.broadcasted_iota(jnp.int32, (8, width), 1)
        depth = lax.rem(cols, side)
        self.at_front, self.at_back = depth == 0, depth == side - 1
        self.odd = (((cols >> (side.bit_length() - 1)) + cols) & 1) == 1
        first_lane, last_lane = lane == 0, lane == lanes - 1
        self.low_edge = (cols < side) & first_lane
        self.high_edge = (cols >= plane - side) & (cols < plane) & last_lane
        self.seam = (cols >= plane + 3 * side) & (cols < plane + 4 * side)
        self.no_link = ((cols >= width - side) & first_lane) | self.high_edge | self.seam

    def after(self, values):
        return pltpu.roll(values, self.width - self.side, 1)

    def before(self, values):
        return pltpu.roll(values, self.side, 1)

    def beyond_z(self, values, afters):
        out = []
        for deep in range(BZB):
            joined = values[deep] if deep == 0 else jnp.where(self.at_back, afters[deep - 1], values[deep])
            out.append(pltpu.roll(joined, 1, 1))
        return out

    def ahead_z(self, values, befores):
        out = []
        for deep in range(BZB):
            joined = values[deep] if deep == BZB - 1 else jnp.where(self.at_front, befores[deep + 1], values[deep])
            out.append(pltpu.roll(joined, self.width - 1, 1))
        return out

    def across(self, held):
        befores = [self.before(v) for v in held]
        afters = [self.after(v) for v in held]
        aheads = self.ahead_z(held, befores)
        ky = [jnp.where(self.no_link, 0.0, mean(held[d], afters[d])) for d in range(BZB)]
        kz = [mean(held[d], aheads[d]) for d in range(BZB)]
        kz[BZB - 1] = jnp.where(self.at_back, 0.0, kz[BZB - 1])
        kzl = self.beyond_z(kz, [self.after(v) for v in kz])
        kzl[0] = jnp.where(self.at_front, 0.0, kzl[0])
        return [self.before(v) for v in ky], ky, kzl, kz

    def edges(self, d, held):
        out = jnp.where(self.low_edge | self.high_edge, held, 0.0)
        if d == 0:
            out = out + jnp.where(self.at_front, held, 0.0)
        if d == BZB - 1:
            out = out + jnp.where(self.at_back, held, 0.0)
        return out

    def sums(self, colour_id, held, downs, ups, behind_of, ahead_of, coefficient):
        afters = [self.after(v) for v in held]
        befores = [self.before(v) for v in held]
        behind = behind_of(held, afters)
        aheads = ahead_of(held, befores)
        out = []
        for at in range(len(held)):
            s, same, other, yl, yu, zl, zu = coefficient(at)
            across = jnp.where(self.odd == (colour_id == 1), downs[at], ups[at])
            part = s + same * held[at] + other * across
            part = part + (yl * befores[at] + yu * afters[at])
            out.append(part + (zl * behind[at] + zu * aheads[at]))
        return out

    def beyond_pairs(self, values, afters):
        last = (fall(afters[1], 4), afters[0])
        return [pltpu.roll(jnp.where(self.at_back, last[j], values[j]), 1, 1) for j in range(2)]

    def ahead_pairs(self, values, befores):
        following = (befores[1], fall(befores[0], 4))
        return [pltpu.roll(jnp.where(self.at_front, following[j], values[j]), self.width - 1, 1) for j in range(2)]

    def split(self, even, odd):
        return jnp.where(self.odd, odd, even), jnp.where(self.odd, even, odd)


def mean(one_side, other):
    return 2.0 * one_side * other / (one_side + other)


def scatter_tiles(ref, index, rows, values):
    for k in range(ref.shape[0]):
        ref[(k, index, rows)] = values[:, k * 128 : (k + 1) * 128]


def every_other(ref, index, start, count):
    tiles = [ref[k, index, pl.ds(start, count, stride=2), :] for k in range(ref.shape[0])]
    return jnp.concatenate(tiles, axis=1)


def couple_kernel(lanes, nodes, plane, block, fifth, *refs):
    first, black, same = refs[:3]
    red_refs, black_refs = refs[3:9], refs[9:15]
    totals = refs[15:17]
    natural = refs[17:]
    f, s, xl, xu, yl, yu, zl, zu, total = natural
    width, own_rows = block.shape[3], block.shape[2]
    grid = Stencil(width, SIDE, plane, lanes, nodes)
    cols = lax.broadcasted_iota(jnp.int32, (8, 128), 1)
    seam = (cols >= 3 * SIDE) & (cols < 5 * SIDE)
    for r in range(0, own_rows, 8):
        here = slice(r, r + 8)
        held = [block[2, d, here] for d in range(BZB)]
        across = grid.across(held)
        for d in range(BZB):
            for ref, values in zip((yl, yu, zl, zu), across):
                scatter_tiles(ref, d, here, values[d])
            scatter_tiles(f, d, here, block[0, d, here])
            if r + 8 < own_rows:
                up = mean(held[d], block[2, d, r + 1 : r + 9])
            else:
                up = jnp.where(grid.rows == 7, 0.0, mean(held[d], fall(held[d], 7)))
            if r:
                down = mean(held[d], block[2, d, r - 1 : r + 7])
            else:
                down = jnp.where(grid.rows == 0, 0.0, mean(held[d], fall(held[d], 1)))
            link = jnp.where(seam, mean(held[d][:, plane:width], fifth[1, d, here]), 0.0)
            extra = link * jnp.where(seam, fifth[0, d, here], 0.0)
            source = block[1, d, here]
            scatter_tiles(s, d, here, jnp.concatenate([source[:, 0:plane], source[:, plane:width] + extra], axis=1))
            scatter_tiles(xl, d, here, down)
            scatter_tiles(xu, d, here, up)
            part = down + up + across[0][d] + across[1][d] + across[2][d] + across[3][d] + grid.edges(d, held[d])
            scatter_tiles(total, d, here, jnp.concatenate([part[:, 0:plane], part[:, plane:width] + link], axis=1))
    for d in range(BZB):
        for t in range(own_rows // 16):
            to = slice(8 * t, 8 * t + 8)
            even = [every_other(ref, d, 16 * t, 8) for ref in natural]
            odd = [every_other(ref, d, 16 * t + 1, 8) for ref in natural]
            black[d, to] = grid.split(even[0], odd[0])[1]
            same[d, to] = even[3]
            pairs = [(even[1], odd[1]), (even[2], odd[3])] + [(even[k], odd[k]) for k in (4, 5, 6, 7)]
            for red_ref, black_ref, pair in zip(red_refs, black_refs, pairs):
                red_ref[d, to], black_ref[d, to] = grid.split(*pair)
            totals[0][d, to], totals[1][d, to] = grid.split(even[8], odd[8])
    for t in range(own_rows // 16):
        to = slice(8 * t, 8 * t + 8)
        held = [black[d, to] for d in range(BZB)]
        downs = [black[d, to.start - 1 : to.stop - 1] if t else fall(held[d], 1) for d in range(BZB)]
        ups = [black[d, to.start + 1 : to.stop + 1] if 8 * t + 8 < own_rows // 2 else fall(held[d], 7) for d in range(BZB)]
        parts = grid.sums(
            0, held, downs, ups, grid.beyond_z, grid.ahead_z,
            lambda d: (red_refs[0][d, to], same[d, to]) + tuple(ref[d, to] for ref in red_refs[1:]),
        )
        for d in range(BZB):
            first[d, to] = parts[d]


def smooth_kernel(lanes, nodes, covered, own_table, block, *refs):
    first, own_black, own_same = refs[:3]
    own = (refs[3:9], refs[9:15])
    own_totals = refs[15:17]
    from_pair, from_other, row_table, two_on, smoothed, coarse, flag = refs[17:24]
    fields, halos, others, totals, inverses = refs[24:26], refs[26:28], refs[28:30], refs[30:32], refs[32:34]
    halo_coefficients = (refs[34:41], refs[41:48])
    halo_inverses = refs[48:50]
    natural = refs[50:59]
    shown, rest, labels, label_sem = refs[59:]
    width = block.shape[3]
    own_rows = block.shape[2]
    side = smoothed.shape[1]
    plane = smoothed.shape[2]
    node, lane = lax.axis_index("node"), lax.axis_index("lane")
    fetch = pltpu.make_async_copy(own_table, labels, label_sem)
    fetch.start()
    grid = Stencil(width, side, plane, lanes, nodes)
    rows = grid.rows
    last = own_rows - 8
    compact = own_rows // 2
    even_node = (node & 1) == 0
    halo_beta, links = [], []
    f, s, xl, xu, yl, yu, zl, zu, total = natural

    def spot(d):
        return d % 2, slice(d // 2 * 8, d // 2 * 8 + 8)

    for d in range(BZB):
        strips = []
        for k in (d % 2, 2):
            unit = (d // 2 * 3 + k) * 3
            pair, other = (
                jnp.concatenate([message[unit + part] for part in range(width // 128)], axis=1)
                for message in (from_pair, from_other)
            )
            strips.append((jnp.where(even_node, other, pair), jnp.where(even_node, pair, other)))
        below, above = strips[0]
        field, beta, fifth_field, fifth_beta = unpack_rows(below, above)
        scatter_tiles(f, *spot(d), field)
        below, above = strips[1]
        source = jnp.where(rows < 4, above, below) if d % 2 == 0 else jnp.where(rows < 4, fall(above, 4), fall(below, 4))
        link = jnp.where((rows == 3) | (rows == 4), mean(beta, fifth_beta), 0.0)
        scatter_tiles(s, *spot(d), source + link * fifth_field)
        links.append(link)
        halo_beta.append(beta)
    across = grid.across(halo_beta)
    for d in range(BZB):
        held = halo_beta[d]
        for ref, values in zip((yl, yu, zl, zu), across):
            scatter_tiles(ref, *spot(d), values[d])
        up = mean(held, jnp.where(rows == 7, fall(block[2, d, 0:8], 7), fall(held, 7)))
        up = jnp.where((rows == 3) | ((rows == 7) & grid.first_node), 0.0, up)
        down = jnp.where(grid.last_node, 0.0, mean(held, fall(block[2, d, last:own_rows], 1)))
        down = jnp.where(rows == 0, down, fall(up, 1))
        scatter_tiles(xl, *spot(d), down)
        scatter_tiles(xu, *spot(d), up)
        whole = links[d] + down + up + across[0][d] + across[1][d] + across[2][d] + across[3][d] + grid.edges(d, held)
        scatter_tiles(total, *spot(d), whole)
        low_link = jnp.where(rows == 0, fall(up, 1), 0.0)
        high_link = jnp.where(rows == 7, fall(down, 7), 0.0)
        low_whole = low_link + jnp.where((rows == 0) & grid.first_node, block[2, d, 0:8], 0.0)
        high_whole = high_link + jnp.where((rows == 7) & grid.last_node, block[2, d, last:own_rows], 0.0)
        for c in range(2):
            at_low, at_high = grid.odd == (c == 1), grid.odd == (c == 0)
            for t in range(compact // 8):
                to = slice(8 * t, 8 * t + 8)
                other, whole = own[c][1][d, to], own_totals[c][d, to]
                if t == 0:
                    other = other + jnp.where(at_low, low_link, 0.0)
                    whole = whole + jnp.where(at_low, low_whole, 0.0)
                if t == compact // 8 - 1:
                    other = other + jnp.where(at_high, high_link, 0.0)
                    whole = whole + jnp.where(at_high, high_whole, 0.0)
                others[c][d, to] = other
                totals[c][d, to] = whole
                inverses[c][d, to] = 1.0 / whole
        fields[1][d, 8 : 8 + compact] = own_black[d]

    def spread(c, j):
        tile = halos[c][j]
        turned = fall(tile, 4)
        fields[c][j, 8 + compact : 16 + compact] = tile
        fields[c][j, 0:8] = turned
        fields[c][j + 2, 8 + compact : 16 + compact] = turned
        fields[c][j + 2, 0:8] = tile

    for j in range(2):
        even = [every_other(ref, j, 0, 8) for ref in natural]
        odd = [every_other(ref, j, 1, 8) for ref in natural]
        halos[1][j] = grid.split(even[0], odd[0])[1]
        spread(1, j)
        pairs = [(even[1], odd[1]), (even[2], odd[3])] + [(even[k], odd[k]) for k in (4, 5, 6, 7)]
        for k, pair in enumerate(pairs):
            at = k if k == 0 else k + 1
            halo_coefficients[0][at][j], halo_coefficients[1][at][j] = grid.split(*pair)
        for c in range(2):
            halo_coefficients[c][1][j] = even[3]
        for c, whole in enumerate(grid.split(even[8], odd[8])):
            halo_inverses[c][j] = 1.0 / whole

    def own_sums(c, t):
        opposite = fields[1 - c]
        start = 8 + 8 * t
        held = [opposite[d, start : start + 8] for d in range(BZB)]
        downs = [opposite[d, start - 1 : start + 7] for d in range(BZB)]
        ups = [opposite[d, start + 1 : start + 9] for d in range(BZB)]
        to = slice(8 * t, 8 * t + 8)

        def coefficient(d):
            return (own[c][0][d, to], own_same[d, to], others[c][d, to]) + tuple(ref[d, to] for ref in own[c][2:])

        return grid.sums(c, held, downs, ups, grid.beyond_z, grid.ahead_z, coefficient)

    def end_terms(t):
        out = []
        for d in range(BZB):
            part = 0.0
            to = slice(8 * t, 8 * t + 8)
            if t == 0:
                low = others[0][d, to] * fields[1][d, 7:15]
                part = part + jnp.where((rows == 0) & ~grid.odd, low, 0.0)
            if t == compact // 8 - 1:
                high = others[0][d, to] * fields[1][d, 9 + 8 * t : 17 + 8 * t]
                part = part + jnp.where((rows == 7) & grid.odd, high, 0.0)
            out.append(first[d, to] + part)
        return out

    quarter = rows & 3
    for sweep in range(SWEEPS):
        for c in (0, 1):
            held = [halos[1 - c][j] for j in range(2)]
            opposite = fields[1 - c]
            downs, ups = [], []
            for j in range(2):
                lows = [opposite[d, compact : compact + 8] for d in (j, j + 2)]
                highs = [opposite[d, 8:16] for d in (j, j + 2)]
                joined = jnp.where(rows < 4, fall(lows[0], 1), fall(lows[1], 5))
                downs.append(jnp.where(quarter == 0, joined, fall(held[j], 1)))
                joined = jnp.where(rows < 4, fall(highs[0], 3), fall(highs[1], 7))
                ups.append(jnp.where(quarter == 3, joined, fall(held[j], 7)))
            parts = grid.sums(
                c, held, downs, ups, grid.beyond_pairs, grid.ahead_pairs,
                lambda j: tuple(ref[j] for ref in halo_coefficients[c]),
            )
            for j in range(2):
                halos[c][j] = parts[j] * halo_inverses[c][j]
                spread(c, j)
            for t in range(compact // 8):
                parts = end_terms(t) if sweep + c == 0 else own_sums(c, t)
                for d in range(BZB):
                    fields[c][d, 8 + 8 * t : 16 + 8 * t] = parts[d] * inverses[c][d, 8 * t : 8 * t + 8]

    fetch.wait()
    count = smoothed.shape[0]
    for t in range(compact // 8):
        to, own_to = slice(8 * t, 8 * t + 8), slice(8 + 8 * t, 16 + 8 * t)
        left = [own_sums(c, t) for c in range(2)]
        for d in range(BZB):
            slot = labels[t * BZB + d, 12].astype(jnp.int32)
            now = [fields[c][d, own_to] for c in range(2)]
            both = left[0][d] - totals[0][d, to] * now[0] + (left[1][d] - totals[1][d, to] * now[1])
            even, odd = grid.split(*now)
            for k in range(plane // 128):
                cut = slice(k * 128, (k + 1) * 128)
                rest[k, pl.ds(pl.multiple_of(slot * 8, 8), 8), :] = both[:, cut]
                shown[k, pl.ds(slot * side, 8, stride=2), :] = even[:, cut]
                shown[k, pl.ds(slot * side + 1, 8, stride=2), :] = odd[:, cut]
    for i in range(count):
        for k in range(plane // 128):
            smoothed[i, :, k * 128 : (k + 1) * 128] = shown[k, i * side : (i + 1) * side]

    small = side // 2
    cells = lax.broadcasted_iota(jnp.int32, (plane, 128), 0)
    slots = lax.broadcasted_iota(jnp.int32, (plane, 128), 1)
    goal = lax.div(lax.div(cells, side), 2) * small + lax.div(lax.rem(cells, side), 2)
    per = small * small
    acc = 0.0
    pairs = small * per // 128
    for inner in range(128 // per):
        stack = []
        for pair in range(pairs):
            i = pair * (128 // per) + inner
            tiles = [rest[k, pl.ds(i, count, stride=small), :] for k in range(plane // 128)]
            stack.append(jnp.concatenate(tiles, axis=1))
        pooling = (goal + inner * per == slots).astype(jnp.float32)
        acc = acc + jnp.dot(
            jnp.concatenate(stack, axis=0), pooling, precision=lax.Precision.HIGHEST, preferred_element_type=jnp.float32
        )
    for pair in range(pairs):
        coarse[:, pair * 128 : (pair + 1) * 128] = 0.125 * acc[pair * count : (pair + 1) * count]

    mine = from_pair.shape[0] - 1
    rows1 = lax.broadcasted_iota(jnp.int32, (8, 128), 0)
    cols1 = lax.broadcasted_iota(jnp.int32, (8, 128), 1)
    owner = lax.rem(lax.div(cols1, 8), 8)
    field_of = lax.rem(cols1, 8)
    table_here, opposite = row_table[...], two_on[...]
    pair, other = from_pair[mine], from_other[mine]
    lower, upper = jnp.where(even_node, other, pair), jnp.where(even_node, pair, other)
    rows_of = [(table_here, lower, upper, node), (lower, opposite, table_here, lax.rem(node + nodes - 1, nodes)),
               (upper, table_here, opposite, lax.rem(node + 1, nodes)), (opposite, upper, lower, lax.rem(node + 2, nodes))]
    if not covered:
        rows_of = rows_of[:1]
    lane_of = lax.rem(lane - jnp.where(owner > 4, owner - 8, owner) + 2 * lanes, lanes)
    wrong = jnp.zeros((8, 128), jnp.float32)
    for table, low, high, at_node in rows_of:
        turned = pltpu.roll(table, 4, 0)
        at_low = jnp.where(rows1 >= 4, turned, jnp.where(at_node == 0, -1.0, pltpu.roll(low, 4, 0)))
        at_high = jnp.where(rows1 < 4, turned, jnp.where(at_node == nodes - 1, -1.0, pltpu.roll(high, 4, 0)))
        y_low = jnp.where(lane_of == 0, -1.0, pltpu.roll(table, 128 - 8, 1))
        y_high = jnp.where(lane_of == lanes - 1, -1.0, pltpu.roll(table, 8, 1))
        z_low = jnp.where(lax.rem(rows1, BZB) == 0, -1.0, pltpu.roll(table, 1, 0))
        z_high = jnp.where(lax.rem(rows1, BZB) == BZB - 1, -1.0, pltpu.roll(table, 7, 0))
        bad = jnp.where((field_of == 0) & (table < 0), 1.0, 0.0)
        for face, expected in enumerate((at_low, at_high, y_low, y_high, z_low, z_high)):
            differs = table != pltpu.roll(expected, 1 + face, 1)
            bad = bad + jnp.where((field_of == 1 + face) & differs, 1.0, 0.0)
        if not covered:
            bad = jnp.where(owner == 0, bad, 0.0)
        wrong = wrong + bad
    flag[0, 0] = (jnp.sum(wrong) > 0).astype(jnp.int32)


ROOM = pltpu.CompilerParams(vmem_limit_bytes=32 * 2**20)
FULL = pltpu.CompilerParams(vmem_limit_bytes=60 * 2**20)
SCALARS = pl.BlockSpec(memory_space=pltpu.SMEM)
VECTORS = pl.BlockSpec(memory_space=pltpu.VMEM)


def fast_body(old_field, old_source, diffusivity, target_box, neighbours):
    count, side, plane = old_field.shape
    half = plane // 2
    lanes, nodes = lax.axis_size("lane"), lax.axis_size("node")
    arrays = (old_field, old_source, diffusivity, target_box, neighbours)
    moves, plan = lane_plan(lanes)
    covered = lanes == 8 and nodes == 4
    units = [plan_units(count, *parts) for parts in plan.values()]
    f32 = jnp.float32
    packed = pl.pallas_call(
        lambda *refs: pack_kernel(moves, plan, lanes, count, *refs),
        name="pack_moves",
        out_shape=[pltpu.VMEM((n, side, half), f32) for n in units]
        + [pltpu.VMEM(array.shape, array.dtype) for array in arrays]
        + [pltpu.VMEM((8, 128), f32)],
        in_specs=[pl.BlockSpec(memory_space=pltpu.HBM)] * 5,
        out_specs=[VECTORS] * (len(units) + 6),
        scratch_shapes=[
            pltpu.SMEM(target_box.shape, jnp.int32),
            pltpu.SMEM(neighbours.shape, jnp.int32),
            pltpu.SMEM((count,), jnp.int32),
            pltpu.SemaphoreType.DMA((7,)),
        ],
        compiler_params=FULL,
    )(*arrays)
    messages, own_table = packed[:-6], packed[-1]
    field, source, beta, target_held, neighbours_held = packed[-6:-1]
    got = {}
    late = [lanes // 2, lanes // 2 + 1]
    near = [1, lanes - 1, 2, lanes - 2]
    for offset in near + [offset for offset in plan if offset not in near + late] + late:
        message = messages[list(plan).index(offset)]
        if offset in late:
            message, _ = lax.optimization_barrier((message, got[2]))
        got[offset] = lax.ppermute(message, "lane", [(i, (i + offset) % lanes) for i in range(lanes)])
    got = [got[offset] for offset in plan]
    width = plane + 128
    strips = BZB // 2 * 9 + 1
    sides = pltpu.VMEM((5, BZB + 1, BXD * side, 128), f32)
    block, fifth, to_pair, to_other, row_table = pl.pallas_call(
        lambda *refs: assemble_kernel(moves, plan, lanes, count, *refs),
        name="assemble_block",
        out_shape=[
            pltpu.VMEM((3, BZB + 1, BXD * side, width), f32),
            pltpu.VMEM((2, BZB, BXD * side, 128), f32),
            pltpu.VMEM((strips, 8, 128), f32),
            pltpu.VMEM((strips, 8, 128), f32),
            pltpu.VMEM((8, 128), f32),
        ],
        in_specs=[VECTORS] * (4 + len(units)),
        out_specs=[VECTORS] * 5,
        scratch_shapes=[
            sides,
            sides,
        ],
        compiler_params=ROOM,
    )(own_table, field, source, beta, *got)
    from_pair = lax.ppermute(to_pair, "node", [(i, i ^ 1) for i in range(nodes)])
    from_other = lax.ppermute(to_other, "node", [(i, (i - 1 + 2 * (i % 2)) % nodes) for i in range(nodes)])
    two_on = lax.ppermute(row_table, "node", [(i, (i + 2) % nodes) for i in range(nodes)])
    tiles, rows = width // 128, BXD * side
    half_rows = pltpu.VMEM((BZB, rows // 2, width), f32)
    coupled = pl.pallas_call(
        lambda *refs: couple_kernel(lanes, nodes, plane, *refs),
        name="couple_block",
        out_shape=[half_rows] * 17,
        in_specs=[VECTORS] * 2,
        out_specs=[VECTORS] * 17,
        scratch_shapes=[pltpu.VMEM((tiles, BZB, rows, 128), f32)] * 9,
        compiler_params=ROOM,
    )(block, fifth)
    pair_tile = pltpu.VMEM((2, 8, width), f32)
    smoothed, coarse, flag = pl.pallas_call(
        lambda *refs: smooth_kernel(lanes, nodes, covered, *refs),
        name="smooth_block",
        out_shape=[
            jax.ShapeDtypeStruct((count, side, plane), f32),
            jax.ShapeDtypeStruct((count, (side // 2) ** 3), f32),
            jax.ShapeDtypeStruct((1, 1), jnp.int32),
        ],
        in_specs=[VECTORS] * (2 + 17 + 4),
        out_specs=[VECTORS, VECTORS, SCALARS],
        scratch_shapes=[pltpu.VMEM((BZB, rows // 2 + 16, width), f32)] * 2
        + [pair_tile] * 2
        + [half_rows] * 6
        + [pair_tile] * 16
        + [pltpu.VMEM((tiles, 2, 16, 128), f32)] * 9
        + [pltpu.VMEM((plane // 128, count * side, 128), f32), pltpu.VMEM((plane // 128, count * side // 2, 128), f32)]
        + [pltpu.SMEM((8, 128), f32), pltpu.SemaphoreType.DMA],
        compiler_params=ROOM,
    )(own_table, block, *coupled, from_pair, from_other, row_table, two_on)
    irregular = flag[0, 0]
    if not covered:
        irregular = lax.pmax(irregular, ("node", "lane"))

    def again(carry):
        out = general_body(field, source, beta, target_held, neighbours_held)
        return (*out, jnp.int32(0))

    smoothed, coarse, _ = lax.while_loop(lambda carry: carry[2] > 0, again, (smoothed, coarse, irregular))
    return smoothed, coarse


def solution(mesh):
    in_specs = (
        P(("node", "lane"), None, None),
        P(("node", "lane"), None, None),
        P(("node", "lane"), None, None),
        P(("node", "lane")),
        P(("node", "lane"), None),
    )
    out_specs = (P(("node", "lane"), None, None), P(("node", "lane"), None))
    return jax.shard_map(fast_body, mesh=mesh, in_specs=in_specs, out_specs=out_specs, check_vma=False)
```

```python
import jax
import jax.numpy as jnp
from jax import lax
from jax.experimental import pallas as pl
from jax.experimental.pallas import tpu as pltpu
from jax.sharding import PartitionSpec as P

SWEEPS = 2


OPPOSITE = (1, 0, 3, 2, 5, 4)


def with_halo(block, sides, width):
    for axis, dim in sides:
        count = lax.axis_size(axis)
        forward = [(i, i + 1) for i in range(count - 1)]
        backward = [(target, source) for source, target in forward]
        low = lax.ppermute(
            lax.slice_in_dim(block, block.shape[dim] - width, None, axis=dim), axis, forward
        )
        high = lax.ppermute(lax.slice_in_dim(block, 0, width, axis=dim), axis, backward)
        block = jnp.concatenate([low, block, high], axis=dim)
    return block


def face_layers(values):
    boxes, side, plane = values.shape
    return jnp.stack(
        [
            values[:, 0],
            values[:, side - 1],
            values[:, :, :side].reshape(boxes, plane),
            values[:, :, plane - side :].reshape(boxes, plane),
            values[:, :, 0::side].reshape(boxes, plane),
            values[:, :, side - 1 :: side].reshape(boxes, plane),
        ],
        axis=1,
    )


def near_values(values, ghost):
    boxes, side, plane = values.shape
    lower_x = jnp.concatenate([ghost[:, 0][:, None, :], values[:, :-1]], axis=1)
    upper_x = jnp.concatenate([values[:, 1:], ghost[:, 1][:, None, :]], axis=1)
    lower_y = jnp.concatenate(
        [ghost[:, 2].reshape(boxes, side, side), values[:, :, : plane - side]], axis=2
    )
    upper_y = jnp.concatenate([values[:, :, side:], ghost[:, 3].reshape(boxes, side, side)], axis=2)
    depth = jnp.arange(plane) % side
    lower_z = jnp.where(
        depth == 0,
        jnp.repeat(ghost[:, 4].reshape(boxes, side, side), side, axis=2),
        jnp.roll(values, 1, axis=2),
    )
    upper_z = jnp.where(
        depth == side - 1,
        jnp.repeat(ghost[:, 5].reshape(boxes, side, side), side, axis=2),
        jnp.roll(values, -1, axis=2),
    )
    return [lower_x, upper_x, lower_y, upper_y, lower_z, upper_z]


def coefficients(diffusivity, beside):
    return [2.0 * diffusivity * other / (diffusivity + other) for other in beside]


def relax(values, source, couplings, beside, chosen):
    total = couplings[0]
    summed = source + couplings[0] * beside[0]
    for face in range(1, 6):
        total = total + couplings[face]
        summed = summed + couplings[face] * beside[face]
    return jnp.where(chosen, summed / total, values)


def defect_of(values, source, couplings, beside):
    total = couplings[0]
    summed = source + couplings[0] * beside[0]
    for face in range(1, 6):
        total = total + couplings[face]
        summed = summed + couplings[face] * beside[face]
    return summed - total * values


def colour_of(side, plane):
    rows = jnp.arange(side)[:, None]
    cells = jnp.arange(plane)[None, :]
    return (rows + cells // side + cells % side) % 2


def restrict(values):
    boxes, side, plane = values.shape
    half = side // 2
    paired = values.reshape(boxes, half, 2, plane).sum(axis=2)
    cells = jnp.arange(plane)
    coarse_cols = cells // side // 2 * half + cells % side // 2
    pooling = (coarse_cols[:, None] == jnp.arange(half * half)[None, :]).astype(jnp.float32)
    summed = jnp.einsum("bxp,pq->bxq", paired, pooling, precision=lax.Precision.HIGHEST)
    return (0.125 * summed).reshape(boxes, half * half * half)


def place(settled, arrived, tags):
    count = settled.shape[0]
    return settled.at[jnp.where(tags > 0, tags - 1, count)].set(arrived, mode="drop")


def general_body(old_field, old_source, diffusivity, target_box, neighbours):
    count, side, plane = old_field.shape
    lane_count = lax.axis_size("lane")
    lane_here = lax.axis_index("lane")
    own_device = lax.axis_index("node") * lane_count + lane_here
    dest_device = target_box // count
    dest_slot = target_box % count
    staying = dest_device == own_device
    cargo = jnp.stack([old_field, old_source], axis=1)
    settled = jnp.zeros_like(cargo).at[jnp.where(staying, dest_slot, count)].set(cargo, mode="drop")
    slots = jnp.arange(count)
    peers = own_device - lane_here + jnp.arange(lane_count)
    chosen = (dest_device[None, :] == peers[:, None]) & jnp.logical_not(staying)[None, :]
    filled = jnp.any(chosen, axis=1)
    picked = jnp.sum(jnp.where(chosen, slots[None, :], 0), axis=1)
    parcels = jnp.where(filled[:, None, None, None], cargo[picked], 0.0)
    labels = jnp.where(filled, jnp.sum(jnp.where(chosen, dest_slot[None, :], 0), axis=1) + 1, 0)
    arrived, tags = (
        lax.all_to_all(parcels, "lane", split_axis=0, concat_axis=0, tiled=True),
        lax.all_to_all(labels, "lane", split_axis=0, concat_axis=0, tiled=True),
    )
    settled = place(settled, arrived, tags)
    field = settled[:, 0]
    source = settled[:, 1]
    present = neighbours >= 0
    near_device = jnp.where(present, neighbours // count, own_device)
    local_row = neighbours % count * 6 + jnp.array(OPPOSITE, jnp.int32)[None, :]
    across = near_device - own_device
    anchor = jnp.where(
        across == -lane_count,
        1,
        jnp.where(
            across == lane_count, 2, jnp.where(across == -1, 3, jnp.where(across == 1, 4, 0))
        ),
    )
    index = anchor * (count * 6) + local_row
    width_out = count * 6

    def departing_boxes(layers):
        return layers.reshape(count * 6, plane)

    def incoming(received, start):
        return jnp.concatenate(
            [
                received[0, 1, start : start + width_out],
                received[2, 1, start : start + width_out],
                received[1, 0, start : start + width_out],
                received[1, 2, start : start + width_out],
            ],
            axis=0,
        )

    def trade(rows):
        return with_halo(rows[None, None], (("node", 0), ("lane", 1)), 1)

    def ghosts(layers, remote_rows, fallback):
        table = jnp.concatenate([layers.reshape(count * 6, plane), remote_rows], axis=0)
        return jnp.where(present[..., None], table[index], fallback)

    beta_layers = face_layers(diffusivity)
    layers = face_layers(field)
    received = trade(
        jnp.concatenate([departing_boxes(layers), departing_boxes(beta_layers)], axis=0)
    )
    beta_ghost = ghosts(beta_layers, incoming(received, width_out), beta_layers)
    couplings = coefficients(diffusivity, near_values(diffusivity, beta_ghost))
    colour = colour_of(side, plane)
    for sweep in range(SWEEPS):
        for colour_id in (0, 1):
            if sweep + colour_id > 0:
                layers = face_layers(field)
                received = trade(departing_boxes(layers))
            ghost = ghosts(layers, incoming(received, 0), jnp.zeros_like(layers))
            field = relax(field, source, couplings, near_values(field, ghost), colour == colour_id)
    layers = face_layers(field)
    received = trade(departing_boxes(layers))
    ghost = ghosts(layers, incoming(received, 0), jnp.zeros_like(layers))
    coarse = restrict(defect_of(field, source, couplings, near_values(field, ghost)))
    return (field, coarse)


BXD = 2
BZB = 4
PAD = 8
SIDE = 16
LOW, HIGH = "low", "high"


def lane_plan(lanes):
    half = lanes // 2
    moves = [1, lanes - 1, 2, lanes - 2, half]
    ends = {}
    for move in moves:
        for offset, part in ((move + 1, HIGH), (move - 1, LOW)):
            ends.setdefault(offset % lanes, []).append((move, part))
    bulk = {1: HIGH, lanes - 1: LOW}
    plan = {}
    for offset in sorted(set(moves) | set(ends)):
        if offset:
            plan[offset] = (bulk.get(offset), offset in moves, ends.get(offset, []))
    return moves, plan


def plan_units(count, bulk, whole, kept):
    return (count + count // 2 if bulk is not None else 0) + (4 if whole else 0) + len(kept) + 1


def cell_lanes(side):
    rows = lax.broadcasted_iota(jnp.int32, (side, 128), 0)
    cols = lax.broadcasted_iota(jnp.int32, (side, 128), 1)
    layer = cols >> (side.bit_length() - 1)
    black = ((rows + layer + cols) & 1) == 1
    return layer, black


def turn(values, shift):
    return pltpu.roll(values, shift % values.shape[-1], values.ndim - 1)


def pack_end(part, field, source, beta, masks):
    side = field.shape[0]
    y, black = masks
    if part == HIGH:
        pairs = turn(jnp.where(black, field, turn(field, -side)), 4 * side)
        out = jnp.where(y >= 4, source, pairs)
        out = jnp.where(y == 3, field, out)
        return out if beta is None else jnp.where(y == 1, turn(beta, -2 * side), out)
    pairs = turn(jnp.where(black, field, turn(field, side)), 4 * side)
    out = jnp.where(y < 4, source, pairs)
    out = jnp.where(y == 4, field, out)
    return out if beta is None else jnp.where(y == 6, turn(beta, 2 * side), out)


def unpack_end(part, packed):
    side = packed.shape[0]
    y, _ = cell_lanes(side)
    if part == HIGH:
        return jnp.where((y & 1) == 0, turn(packed, 4 * side), turn(packed, 5 * side))
    return jnp.where((y & 1) == 1, turn(packed, 4 * side), turn(packed, -5 * side))


def part_lanes(part, plane):
    return slice(0, plane // 2) if part == LOW else slice(plane // 2, plane)


def pack_kernel(moves, plan, lanes, count, *refs):
    outs = refs[5 : 5 + len(plan)]
    held_here = refs[5 + len(plan) : 10 + len(plan)]
    table, target, near, slots, sems = refs[10 + len(plan) :]
    pairs = [*zip(refs[3:5], (target, near)), *zip(refs[:5], held_here)]
    fetch = [pltpu.make_async_copy(src, dst, sems.at[k]) for k, (src, dst) in enumerate(pairs)]
    for copy in fetch:
        copy.start()
    for copy in fetch[:2]:
        copy.wait()
    field, source, beta = held_here[:3]
    side, plane = field.shape[1:]
    half = plane // 2
    lane = lax.axis_index("lane")
    first = (lax.axis_index("node") * lanes + lane) * count
    old_index = [jnp.int32(0)] * len(moves)
    new_slot = [jnp.int32(-1)] * len(moves)
    stay = []
    for i in range(count):
        there = target[i]
        slot = lax.rem(there, count)
        step = lax.rem(lax.rem(lax.div(there, count), lanes) - lane + lanes, lanes)
        stay.append(jnp.where(step == 0, slot, -1))
        for k, move in enumerate(moves):
            old_index[k] = jnp.where(step == move, i, old_index[k])
            new_slot[k] = jnp.where(step == move, slot, new_slot[k])
    for i in range(count):
        slots[i] = -1

    def local(index, face):
        there = near[index, face]
        inside = (there >= first) & (there < first + count)
        return inside, jnp.clip(there - first, 0, count - 1)

    place = []
    for i in range(count):
        inside, below = local(i, 0)
        depth = jnp.int32(0)
        live, at = local(i, 4)
        for _ in range(BZB - 1):
            depth = depth + jnp.where(live, 1, 0)
            further, onward = local(at, 4)
            live, at = live & further, onward
        spot = jnp.where(inside, BZB, 0) + depth
        place.append(spot)
        slots[spot] = i
    rows = lax.broadcasted_iota(jnp.int32, (8, 128), 0)
    cols = lax.broadcasted_iota(jnp.int32, (8, 128), 1)
    spots = rows * 128 + cols
    held = jnp.zeros((8, 128), jnp.int32)

    def put(held, row, col, value):
        return jnp.where(spots == row * 128 + col, value, held)

    for i in range(count):
        slot = slots[i]
        held = put(held, i, 12, jnp.maximum(slot, 0))
        held = put(held, i, 0, jnp.where(slot < 0, -7, first + slot))
        for face in range(6):
            held = put(held, i, 1 + face, near[jnp.maximum(slot, 0), face])
    words = [
        sum(place[i] << 3 * i for i in range(count)),
        sum((stay[i] + 1) << 4 * i for i in range(count // 2)),
        sum((stay[i] + 1) << 4 * (i - count // 2) for i in range(count // 2, count)),
        sum((new_slot[k] + 1) << 4 * k for k in range(len(moves))),
        sum(old_index[k] << 3 * k for k in range(len(moves))),
    ]
    for k, word in enumerate(words):
        held = put(held, 0, 16 + k, word)
    table[...] = held.astype(jnp.float32)
    for copy in fetch[2:]:
        copy.wait()
    masks = cell_lanes(side)
    left = lax.broadcasted_iota(jnp.int32, (side, 128), 1) < 64
    for out, (bulk, whole, kept) in zip(outs, plan.values()):
        if bulk is not None:
            cut = part_lanes(bulk, plane)
            for i in range(count):
                out[i] = pack_end(bulk, field[i, :, cut], source[i, :, cut], beta[i, :, cut], masks)
            for i in range(0, count, 2):
                one, two = beta[i, :, cut], turn(beta[i + 1, :, cut], 64)
                out[count + i // 2] = jnp.where(left, two, one) if bulk == HIGH else jnp.where(left, one, two)
    for (offset, (bulk, whole, kept)), out in zip(plan.items(), outs):
        unit = count + count // 2 if bulk is not None else 0
        low, high = part_lanes(LOW, plane), part_lanes(HIGH, plane)
        if whole:
            box = old_index[moves.index(offset)]
            for k, array in enumerate((field, source)):
                out[unit + 2 * k] = array[box, :, low]
                out[unit + 2 * k + 1] = array[box, :, high]
            unit += 4
        for move, part in kept:
            box = old_index[moves.index(move)]
            cut = part_lanes(part, plane)
            out[unit] = pack_end(part, field[box, :, cut], source[box, :, cut], None, masks)
            unit += 1
    for out in outs:
        out[out.shape[0] - 1, 0:8] = table[...]


def assemble_kernel(moves, plan, lanes, count, *refs):
    own_table, field, source, beta = refs[:4]
    got = dict(zip(plan, refs[4 : 4 + len(plan)]))
    block, fifth, to_pair, to_other, row_table, low_side, high_side = refs[4 + len(plan) :]
    side, plane = field.shape[1:]
    half = plane // 2

    def table_of(offset):
        return got[offset].at[got[offset].shape[0] - 1, 0:8] if offset else own_table

    words = {}
    for offset in (0, *plan):
        line = table_of(offset)[0:1, :].astype(jnp.int32)
        words[offset] = [line[0, 16 + k] for k in range(5)]

    cols = lax.broadcasted_iota(jnp.int32, (8, 128), 1)
    shown = [offset for offset in plan if lanes == 8 or offset in (1, lanes - 1)]
    joined = jnp.where(cols < 8, own_table[...], 0.0)
    for offset in shown:
        at = offset if offset < 7 else 7
        joined = joined + pltpu.roll(jnp.where(cols < 8, table_of(offset)[...], 0.0), 8 * at, 1)
    joined = joined + pltpu.roll(joined, 64, 1)
    row_table[...] = joined
    to_pair[to_pair.shape[0] - 1] = joined
    to_other[to_other.shape[0] - 1] = joined

    def place_of(offset, slot):
        code = (words[offset][0] >> 3 * slot) & 7
        return code & (BZB - 1), (code >> 2) * side

    def stays(offset, i):
        return ((words[offset][1 + i // (count // 2)] >> 4 * (i % (count // 2))) & 15) - 1

    def moved(offset, k):
        return ((words[offset][3] >> 4 * k) & 15) - 1

    def spot_at(offset, slot):
        deep, row = place_of(offset, jnp.maximum(slot, 0))
        return jnp.where(slot >= 0, deep, BZB), jnp.where(slot >= 0, row, 0)

    def put(ref, array, spot, values, where=slice(None)):
        deep, row = spot
        ref[array, deep, pl.ds(pl.multiple_of(row, side), side), where] = values

    low, high, whole = slice(0, half), slice(half, plane), slice(0, plane)
    for i in range(count):
        put(block, 2, place_of(0, i), beta[i], whole)
        spot = spot_at(0, stays(0, i))
        put(block, 0, spot, field[i], whole)
        put(block, 1, spot, source[i], whole)

    below, above = 1, lanes - 1
    sides = {HIGH: (low_side, below, side), LOW: (high_side, above, -side)}

    def put_end(part, slot, layers, raw, sources):
        ref, offset, shift = sides[part]
        spot = spot_at(offset, slot)
        put(ref, 0, spot, layers)
        put(ref, 1, spot, sources)
        put(ref, 3, spot, turn(raw, shift))

    for move, part in ((1, LOW), (lanes - 1, HIGH)):
        k = moves.index(move)
        box, cut = (words[0][4] >> 3 * k) & 7, part_lanes(part, plane)
        raw = field[box, :, cut]
        put_end(part, moved(0, k), raw, raw, source[box, :, cut])

    for offset, (bulk, entire, kept) in plan.items():
        message = got[offset]
        unit = 0
        if bulk is not None:
            ref, _, shift = sides[bulk]
            for i in range(count):
                packed = message[i]
                put_end(bulk, stays(offset, i), unpack_end(bulk, packed), packed, packed)
                joint = message[count + i // 2]
                spot = place_of(offset, i)
                put(ref, 2, spot, joint if i % 2 == 0 else turn(joint, 64))
                put(ref, 4, spot, turn(packed, 3 * shift))
            unit = count + count // 2
        if entire:
            spot = spot_at(0, moved(offset, moves.index(offset)))
            for k in range(2):
                put(block, k, spot, message[unit + 2 * k], low)
                put(block, k, spot, message[unit + 2 * k + 1], high)
            unit += 4
        for move, part in kept:
            packed = message[unit]
            put_end(part, moved(offset, moves.index(move)), unpack_end(part, packed), packed, packed)
            unit += 1

    rows, width = block.shape[2:]
    left = lax.broadcasted_iota(jnp.int32, (rows, 128), 1) < 64
    for d in range(BZB):
        for k in range(3):
            block[k, d, :, plane:width] = jnp.where(left, high_side[k, d], low_side[k, d])
        for k in range(2):
            fifth[k, d] = jnp.where(left, high_side[3 + k, d], low_side[3 + k, d])
    even_node = (lax.axis_index("node") & 1) == 0
    for deep in range(0, BZB, 2):
        strips = []
        for start, up in ((rows - 8, True), (0, False)):
            tiles = []
            sources = []
            for d in (deep, deep + 1):
                f, s, b = (block[k, d, start : start + 8] for k in range(3))
                tiles.append(pack_rows(up, f, b))
                sources.append(s)
            strips.append(tiles + [pack_sources(up, *sources)])
        for k, (up, down) in enumerate(zip(*strips)):
            for part in range(width // 128):
                cut, unit = slice(part * 128, (part + 1) * 128), (deep // 2 * 3 + k) * 3 + part
                to_pair[unit] = jnp.where(even_node, up[:, cut], down[:, cut])
                to_other[unit] = jnp.where(even_node, down[:, cut], up[:, cut])


def row_colours(width, side):
    rows = lax.broadcasted_iota(jnp.int32, (8, width), 0)
    cols = lax.broadcasted_iota(jnp.int32, (8, width), 1)
    return rows, (rows + (cols >> (side.bit_length() - 1)) + cols) & 1


def fall(values, shift):
    return pltpu.roll(values, shift % 8, 0)


def pack_rows(up, field, beta):
    rows, colour = row_colours(field.shape[1], SIDE)
    if up:
        pairs = fall(jnp.where(colour == 1, field, fall(field, 7)), 4)
        out = jnp.where(rows < 3, pairs, beta)
        return jnp.where(rows == 1, fall(field, 6), out)
    pairs = fall(jnp.where(colour == 1, field, fall(field, 1)), 4)
    out = jnp.where(rows > 4, pairs, beta)
    return jnp.where(rows == 6, fall(field, 2), out)


def unpack_rows(below, above):
    rows = lax.broadcasted_iota(jnp.int32, below.shape, 0)
    odd = (rows & 1) == 1
    first = jnp.where(odd, fall(above, 4), fall(above, 3))
    second = jnp.where(odd, fall(below, 5), fall(below, 4))
    field = jnp.where(rows < 4, first, second)
    beta = jnp.where(rows < 4, above, below)
    fifth_field = jnp.where(rows < 4, fall(above, 5), fall(below, 3))
    fifth_beta = jnp.where(rows < 4, fall(above, 7), fall(below, 1))
    return field, beta, fifth_field, fifth_beta


def pack_sources(up, first, second):
    rows = lax.broadcasted_iota(jnp.int32, first.shape, 0)
    return jnp.where(rows >= 4, first, fall(second, 4)) if up else jnp.where(rows < 4, first, fall(second, 4))


class Stencil:
    def __init__(self, width, side, plane, lanes, nodes):
        self.width, self.side, self.plane = width, side, plane
        node, lane = lax.axis_index("node"), lax.axis_index("lane")
        self.first_node, self.last_node = node == 0, node == nodes - 1
        self.rows, self.colour = row_colours(width, side)
        cols = lax.broadcasted_iota(jnp.int32, (8, width), 1)
        depth = lax.rem(cols, side)
        self.at_front, self.at_back = depth == 0, depth == side - 1
        self.odd = (((cols >> (side.bit_length() - 1)) + cols) & 1) == 1
        first_lane, last_lane = lane == 0, lane == lanes - 1
        self.low_edge = (cols < side) & first_lane
        self.high_edge = (cols >= plane - side) & (cols < plane) & last_lane
        self.seam = (cols >= plane + 3 * side) & (cols < plane + 4 * side)
        self.no_link = ((cols >= width - side) & first_lane) | self.high_edge | self.seam

    def after(self, values):
        return pltpu.roll(values, self.width - self.side, 1)

    def before(self, values):
        return pltpu.roll(values, self.side, 1)

    def beyond_z(self, values, afters):
        out = []
        for deep in range(BZB):
            joined = values[deep] if deep == 0 else jnp.where(self.at_back, afters[deep - 1], values[deep])
            out.append(pltpu.roll(joined, 1, 1))
        return out

    def ahead_z(self, values, befores):
        out = []
        for deep in range(BZB):
            joined = values[deep] if deep == BZB - 1 else jnp.where(self.at_front, befores[deep + 1], values[deep])
            out.append(pltpu.roll(joined, self.width - 1, 1))
        return out

    def across(self, held):
        befores = [self.before(v) for v in held]
        afters = [self.after(v) for v in held]
        aheads = self.ahead_z(held, befores)
        ky = [jnp.where(self.no_link, 0.0, mean(held[d], afters[d])) for d in range(BZB)]
        kz = [mean(held[d], aheads[d]) for d in range(BZB)]
        kz[BZB - 1] = jnp.where(self.at_back, 0.0, kz[BZB - 1])
        kzl = self.beyond_z(kz, [self.after(v) for v in kz])
        kzl[0] = jnp.where(self.at_front, 0.0, kzl[0])
        return [self.before(v) for v in ky], ky, kzl, kz

    def edges(self, d, held):
        out = jnp.where(self.low_edge | self.high_edge, held, 0.0)
        if d == 0:
            out = out + jnp.where(self.at_front, held, 0.0)
        if d == BZB - 1:
            out = out + jnp.where(self.at_back, held, 0.0)
        return out

    def sums(self, colour_id, held, downs, ups, behind_of, ahead_of, coefficient):
        afters = [self.after(v) for v in held]
        befores = [self.before(v) for v in held]
        behind = behind_of(held, afters)
        aheads = ahead_of(held, befores)
        out = []
        for at in range(len(held)):
            s, same, other, yl, yu, zl, zu = coefficient(at)
            across = jnp.where(self.odd == (colour_id == 1), downs[at], ups[at])
            part = s + same * held[at] + other * across
            part = part + (yl * befores[at] + yu * afters[at])
            out.append(part + (zl * behind[at] + zu * aheads[at]))
        return out

    def beyond_pairs(self, values, afters):
        last = (fall(afters[1], 4), afters[0])
        return [pltpu.roll(jnp.where(self.at_back, last[j], values[j]), 1, 1) for j in range(2)]

    def ahead_pairs(self, values, befores):
        following = (befores[1], fall(befores[0], 4))
        return [pltpu.roll(jnp.where(self.at_front, following[j], values[j]), self.width - 1, 1) for j in range(2)]

    def split(self, even, odd):
        return jnp.where(self.odd, odd, even), jnp.where(self.odd, even, odd)


def mean(one_side, other):
    return 2.0 * one_side * other / (one_side + other)


def scatter_tiles(ref, index, rows, values):
    for k in range(ref.shape[0]):
        ref[(k, index, rows)] = values[:, k * 128 : (k + 1) * 128]


def every_other(ref, index, start, count):
    tiles = [ref[k, index, pl.ds(start, count, stride=2), :] for k in range(ref.shape[0])]
    return jnp.concatenate(tiles, axis=1)


def couple_kernel(lanes, nodes, plane, block, fifth, *refs):
    first, black, same = refs[:3]
    red_refs, black_refs = refs[3:9], refs[9:15]
    totals = refs[15:17]
    natural = refs[17:]
    f, s, xl, xu, yl, yu, zl, zu, total = natural
    width, own_rows = block.shape[3], block.shape[2]
    grid = Stencil(width, SIDE, plane, lanes, nodes)
    cols = lax.broadcasted_iota(jnp.int32, (8, 128), 1)
    seam = (cols >= 3 * SIDE) & (cols < 5 * SIDE)
    for r in range(0, own_rows, 8):
        here = slice(r, r + 8)
        held = [block[2, d, here] for d in range(BZB)]
        across = grid.across(held)
        for d in range(BZB):
            for ref, values in zip((yl, yu, zl, zu), across):
                scatter_tiles(ref, d, here, values[d])
            scatter_tiles(f, d, here, block[0, d, here])
            if r + 8 < own_rows:
                up = mean(held[d], block[2, d, r + 1 : r + 9])
            else:
                up = jnp.where(grid.rows == 7, 0.0, mean(held[d], fall(held[d], 7)))
            if r:
                down = mean(held[d], block[2, d, r - 1 : r + 7])
            else:
                down = jnp.where(grid.rows == 0, 0.0, mean(held[d], fall(held[d], 1)))
            link = jnp.where(seam, mean(held[d][:, plane:width], fifth[1, d, here]), 0.0)
            extra = link * jnp.where(seam, fifth[0, d, here], 0.0)
            source = block[1, d, here]
            scatter_tiles(s, d, here, jnp.concatenate([source[:, 0:plane], source[:, plane:width] + extra], axis=1))
            scatter_tiles(xl, d, here, down)
            scatter_tiles(xu, d, here, up)
            part = down + up + across[0][d] + across[1][d] + across[2][d] + across[3][d] + grid.edges(d, held[d])
            scatter_tiles(total, d, here, jnp.concatenate([part[:, 0:plane], part[:, plane:width] + link], axis=1))
    for d in range(BZB):
        for t in range(own_rows // 16):
            to = slice(8 * t, 8 * t + 8)
            even = [every_other(ref, d, 16 * t, 8) for ref in natural]
            odd = [every_other(ref, d, 16 * t + 1, 8) for ref in natural]
            black[d, to] = grid.split(even[0], odd[0])[1]
            same[d, to] = even[3]
            pairs = [(even[1], odd[1]), (even[2], odd[3])] + [(even[k], odd[k]) for k in (4, 5, 6, 7)]
            for red_ref, black_ref, pair in zip(red_refs, black_refs, pairs):
                red_ref[d, to], black_ref[d, to] = grid.split(*pair)
            totals[0][d, to], totals[1][d, to] = grid.split(even[8], odd[8])
    for t in range(own_rows // 16):
        to = slice(8 * t, 8 * t + 8)
        held = [black[d, to] for d in range(BZB)]
        downs = [black[d, to.start - 1 : to.stop - 1] if t else fall(held[d], 1) for d in range(BZB)]
        ups = [black[d, to.start + 1 : to.stop + 1] if 8 * t + 8 < own_rows // 2 else fall(held[d], 7) for d in range(BZB)]
        parts = grid.sums(
            0, held, downs, ups, grid.beyond_z, grid.ahead_z,
            lambda d: (red_refs[0][d, to], same[d, to]) + tuple(ref[d, to] for ref in red_refs[1:]),
        )
        for d in range(BZB):
            first[d, to] = parts[d]


def smooth_kernel(lanes, nodes, covered, own_table, block, *refs):
    first, own_black, own_same = refs[:3]
    own = (refs[3:9], refs[9:15])
    own_totals = refs[15:17]
    from_pair, from_other, row_table, two_on, smoothed, coarse, flag = refs[17:24]
    fields, halos, others, totals, inverses = refs[24:26], refs[26:28], refs[28:30], refs[30:32], refs[32:34]
    halo_coefficients = (refs[34:41], refs[41:48])
    halo_inverses = refs[48:50]
    natural = refs[50:59]
    shown, rest, labels, label_sem = refs[59:]
    width = block.shape[3]
    own_rows = block.shape[2]
    side = smoothed.shape[1]
    plane = smoothed.shape[2]
    node, lane = lax.axis_index("node"), lax.axis_index("lane")
    fetch = pltpu.make_async_copy(own_table, labels, label_sem)
    fetch.start()
    grid = Stencil(width, side, plane, lanes, nodes)
    rows = grid.rows
    last = own_rows - 8
    compact = own_rows // 2
    even_node = (node & 1) == 0
    halo_beta, links = [], []
    f, s, xl, xu, yl, yu, zl, zu, total = natural

    def spot(d):
        return d % 2, slice(d // 2 * 8, d // 2 * 8 + 8)

    for d in range(BZB):
        strips = []
        for k in (d % 2, 2):
            unit = (d // 2 * 3 + k) * 3
            pair, other = (
                jnp.concatenate([message[unit + part] for part in range(width // 128)], axis=1)
                for message in (from_pair, from_other)
            )
            strips.append((jnp.where(even_node, other, pair), jnp.where(even_node, pair, other)))
        below, above = strips[0]
        field, beta, fifth_field, fifth_beta = unpack_rows(below, above)
        scatter_tiles(f, *spot(d), field)
        below, above = strips[1]
        source = jnp.where(rows < 4, above, below) if d % 2 == 0 else jnp.where(rows < 4, fall(above, 4), fall(below, 4))
        link = jnp.where((rows == 3) | (rows == 4), mean(beta, fifth_beta), 0.0)
        scatter_tiles(s, *spot(d), source + link * fifth_field)
        links.append(link)
        halo_beta.append(beta)
    across = grid.across(halo_beta)
    for d in range(BZB):
        held = halo_beta[d]
        for ref, values in zip((yl, yu, zl, zu), across):
            scatter_tiles(ref, *spot(d), values[d])
        up = mean(held, jnp.where(rows == 7, fall(block[2, d, 0:8], 7), fall(held, 7)))
        up = jnp.where((rows == 3) | ((rows == 7) & grid.first_node), 0.0, up)
        down = jnp.where(grid.last_node, 0.0, mean(held, fall(block[2, d, last:own_rows], 1)))
        down = jnp.where(rows == 0, down, fall(up, 1))
        scatter_tiles(xl, *spot(d), down)
        scatter_tiles(xu, *spot(d), up)
        whole = links[d] + down + up + across[0][d] + across[1][d] + across[2][d] + across[3][d] + grid.edges(d, held)
        scatter_tiles(total, *spot(d), whole)
        low_link = jnp.where(rows == 0, fall(up, 1), 0.0)
        high_link = jnp.where(rows == 7, fall(down, 7), 0.0)
        low_whole = low_link + jnp.where((rows == 0) & grid.first_node, block[2, d, 0:8], 0.0)
        high_whole = high_link + jnp.where((rows == 7) & grid.last_node, block[2, d, last:own_rows], 0.0)
        for c in range(2):
            at_low, at_high = grid.odd == (c == 1), grid.odd == (c == 0)
            for t in range(compact // 8):
                to = slice(8 * t, 8 * t + 8)
                other, whole = own[c][1][d, to], own_totals[c][d, to]
                if t == 0:
                    other = other + jnp.where(at_low, low_link, 0.0)
                    whole = whole + jnp.where(at_low, low_whole, 0.0)
                if t == compact // 8 - 1:
                    other = other + jnp.where(at_high, high_link, 0.0)
                    whole = whole + jnp.where(at_high, high_whole, 0.0)
                others[c][d, to] = other
                totals[c][d, to] = whole
                inverses[c][d, to] = 1.0 / whole
        fields[1][d, 8 : 8 + compact] = own_black[d]

    def spread(c, j):
        tile = halos[c][j]
        turned = fall(tile, 4)
        fields[c][j, 8 + compact : 16 + compact] = tile
        fields[c][j, 0:8] = turned
        fields[c][j + 2, 8 + compact : 16 + compact] = turned
        fields[c][j + 2, 0:8] = tile

    for j in range(2):
        even = [every_other(ref, j, 0, 8) for ref in natural]
        odd = [every_other(ref, j, 1, 8) for ref in natural]
        halos[1][j] = grid.split(even[0], odd[0])[1]
        spread(1, j)
        pairs = [(even[1], odd[1]), (even[2], odd[3])] + [(even[k], odd[k]) for k in (4, 5, 6, 7)]
        for k, pair in enumerate(pairs):
            at = k if k == 0 else k + 1
            halo_coefficients[0][at][j], halo_coefficients[1][at][j] = grid.split(*pair)
        for c in range(2):
            halo_coefficients[c][1][j] = even[3]
        for c, whole in enumerate(grid.split(even[8], odd[8])):
            halo_inverses[c][j] = 1.0 / whole

    def own_sums(c, t):
        opposite = fields[1 - c]
        start = 8 + 8 * t
        held = [opposite[d, start : start + 8] for d in range(BZB)]
        downs = [opposite[d, start - 1 : start + 7] for d in range(BZB)]
        ups = [opposite[d, start + 1 : start + 9] for d in range(BZB)]
        to = slice(8 * t, 8 * t + 8)

        def coefficient(d):
            return (own[c][0][d, to], own_same[d, to], others[c][d, to]) + tuple(ref[d, to] for ref in own[c][2:])

        return grid.sums(c, held, downs, ups, grid.beyond_z, grid.ahead_z, coefficient)

    def end_terms(t):
        out = []
        for d in range(BZB):
            part = 0.0
            to = slice(8 * t, 8 * t + 8)
            if t == 0:
                low = others[0][d, to] * fields[1][d, 7:15]
                part = part + jnp.where((rows == 0) & ~grid.odd, low, 0.0)
            if t == compact // 8 - 1:
                high = others[0][d, to] * fields[1][d, 9 + 8 * t : 17 + 8 * t]
                part = part + jnp.where((rows == 7) & grid.odd, high, 0.0)
            out.append(first[d, to] + part)
        return out

    quarter = rows & 3
    for sweep in range(SWEEPS):
        for c in (0, 1):
            held = [halos[1 - c][j] for j in range(2)]
            opposite = fields[1 - c]
            downs, ups = [], []
            for j in range(2):
                lows = [opposite[d, compact : compact + 8] for d in (j, j + 2)]
                highs = [opposite[d, 8:16] for d in (j, j + 2)]
                joined = jnp.where(rows < 4, fall(lows[0], 1), fall(lows[1], 5))
                downs.append(jnp.where(quarter == 0, joined, fall(held[j], 1)))
                joined = jnp.where(rows < 4, fall(highs[0], 3), fall(highs[1], 7))
                ups.append(jnp.where(quarter == 3, joined, fall(held[j], 7)))
            parts = grid.sums(
                c, held, downs, ups, grid.beyond_pairs, grid.ahead_pairs,
                lambda j: tuple(ref[j] for ref in halo_coefficients[c]),
            )
            for j in range(2):
                halos[c][j] = parts[j] * halo_inverses[c][j]
                spread(c, j)
            for t in range(compact // 8):
                parts = end_terms(t) if sweep + c == 0 else own_sums(c, t)
                for d in range(BZB):
                    fields[c][d, 8 + 8 * t : 16 + 8 * t] = parts[d] * inverses[c][d, 8 * t : 8 * t + 8]

    fetch.wait()
    count = smoothed.shape[0]
    for t in range(compact // 8):
        to, own_to = slice(8 * t, 8 * t + 8), slice(8 + 8 * t, 16 + 8 * t)
        left = [own_sums(c, t) for c in range(2)]
        for d in range(BZB):
            slot = labels[t * BZB + d, 12].astype(jnp.int32)
            now = [fields[c][d, own_to] for c in range(2)]
            both = left[0][d] - totals[0][d, to] * now[0] + (left[1][d] - totals[1][d, to] * now[1])
            even, odd = grid.split(*now)
            for k in range(plane // 128):
                cut = slice(k * 128, (k + 1) * 128)
                rest[k, pl.ds(pl.multiple_of(slot * 8, 8), 8), :] = both[:, cut]
                shown[k, pl.ds(slot * side, 8, stride=2), :] = even[:, cut]
                shown[k, pl.ds(slot * side + 1, 8, stride=2), :] = odd[:, cut]
    for i in range(count):
        for k in range(plane // 128):
            smoothed[i, :, k * 128 : (k + 1) * 128] = shown[k, i * side : (i + 1) * side]

    small = side // 2
    cells = lax.broadcasted_iota(jnp.int32, (plane, 128), 0)
    slots = lax.broadcasted_iota(jnp.int32, (plane, 128), 1)
    goal = lax.div(lax.div(cells, side), 2) * small + lax.div(lax.rem(cells, side), 2)
    per = small * small
    acc = 0.0
    pairs = small * per // 128
    for inner in range(128 // per):
        stack = []
        for pair in range(pairs):
            i = pair * (128 // per) + inner
            tiles = [rest[k, pl.ds(i, count, stride=small), :] for k in range(plane // 128)]
            stack.append(jnp.concatenate(tiles, axis=1))
        pooling = (goal + inner * per == slots).astype(jnp.float32)
        acc = acc + jnp.dot(
            jnp.concatenate(stack, axis=0), pooling, precision=lax.Precision.HIGHEST, preferred_element_type=jnp.float32
        )
    for pair in range(pairs):
        coarse[:, pair * 128 : (pair + 1) * 128] = 0.125 * acc[pair * count : (pair + 1) * count]

    mine = from_pair.shape[0] - 1
    rows1 = lax.broadcasted_iota(jnp.int32, (8, 128), 0)
    cols1 = lax.broadcasted_iota(jnp.int32, (8, 128), 1)
    owner = lax.rem(lax.div(cols1, 8), 8)
    field_of = lax.rem(cols1, 8)
    table_here, opposite = row_table[...], two_on[...]
    pair, other = from_pair[mine], from_other[mine]
    lower, upper = jnp.where(even_node, other, pair), jnp.where(even_node, pair, other)
    rows_of = [(table_here, lower, upper, node), (lower, opposite, table_here, lax.rem(node + nodes - 1, nodes)),
               (upper, table_here, opposite, lax.rem(node + 1, nodes)), (opposite, upper, lower, lax.rem(node + 2, nodes))]
    if not covered:
        rows_of = rows_of[:1]
    lane_of = lax.rem(lane - jnp.where(owner > 4, owner - 8, owner) + 2 * lanes, lanes)
    wrong = jnp.zeros((8, 128), jnp.float32)
    for table, low, high, at_node in rows_of:
        turned = pltpu.roll(table, 4, 0)
        at_low = jnp.where(rows1 >= 4, turned, jnp.where(at_node == 0, -1.0, pltpu.roll(low, 4, 0)))
        at_high = jnp.where(rows1 < 4, turned, jnp.where(at_node == nodes - 1, -1.0, pltpu.roll(high, 4, 0)))
        y_low = jnp.where(lane_of == 0, -1.0, pltpu.roll(table, 128 - 8, 1))
        y_high = jnp.where(lane_of == lanes - 1, -1.0, pltpu.roll(table, 8, 1))
        z_low = jnp.where(lax.rem(rows1, BZB) == 0, -1.0, pltpu.roll(table, 1, 0))
        z_high = jnp.where(lax.rem(rows1, BZB) == BZB - 1, -1.0, pltpu.roll(table, 7, 0))
        bad = jnp.where((field_of == 0) & (table < 0), 1.0, 0.0)
        for face, expected in enumerate((at_low, at_high, y_low, y_high, z_low, z_high)):
            differs = table != pltpu.roll(expected, 1 + face, 1)
            bad = bad + jnp.where((field_of == 1 + face) & differs, 1.0, 0.0)
        if not covered:
            bad = jnp.where(owner == 0, bad, 0.0)
        wrong = wrong + bad
    flag[0, 0] = (jnp.sum(wrong) > 0).astype(jnp.int32)


ROOM = pltpu.CompilerParams(vmem_limit_bytes=32 * 2**20)
FULL = pltpu.CompilerParams(vmem_limit_bytes=60 * 2**20)
SCALARS = pl.BlockSpec(memory_space=pltpu.SMEM)
VECTORS = pl.BlockSpec(memory_space=pltpu.VMEM)


def fast_body(old_field, old_source, diffusivity, target_box, neighbours):
    count, side, plane = old_field.shape
    half = plane // 2
    lanes, nodes = lax.axis_size("lane"), lax.axis_size("node")
    arrays = (old_field, old_source, diffusivity, target_box, neighbours)
    moves, plan = lane_plan(lanes)
    covered = lanes == 8 and nodes == 4
    units = [plan_units(count, *parts) for parts in plan.values()]
    f32 = jnp.float32
    packed = pl.pallas_call(
        lambda *refs: pack_kernel(moves, plan, lanes, count, *refs),
        name="pack_moves",
        out_shape=[pltpu.VMEM((n, side, half), f32) for n in units]
        + [pltpu.VMEM(array.shape, array.dtype) for array in arrays]
        + [pltpu.VMEM((8, 128), f32)],
        in_specs=[pl.BlockSpec(memory_space=pltpu.HBM)] * 5,
        out_specs=[VECTORS] * (len(units) + 6),
        scratch_shapes=[
            pltpu.SMEM(target_box.shape, jnp.int32),
            pltpu.SMEM(neighbours.shape, jnp.int32),
            pltpu.SMEM((count,), jnp.int32),
            pltpu.SemaphoreType.DMA((7,)),
        ],
        compiler_params=FULL,
    )(*arrays)
    messages, own_table = packed[:-6], packed[-1]
    field, source, beta, target_held, neighbours_held = packed[-6:-1]
    got = {}
    late = [lanes // 2, lanes // 2 + 1]
    near = [1, lanes - 1, 2, lanes - 2]
    for offset in near + [offset for offset in plan if offset not in near + late] + late:
        message = messages[list(plan).index(offset)]
        if offset in late:
            message, _ = lax.optimization_barrier((message, got[2]))
        got[offset] = lax.ppermute(message, "lane", [(i, (i + offset) % lanes) for i in range(lanes)])
    got = [got[offset] for offset in plan]
    width = plane + 128
    strips = BZB // 2 * 9 + 1
    sides = pltpu.VMEM((5, BZB + 1, BXD * side, 128), f32)
    block, fifth, to_pair, to_other, row_table = pl.pallas_call(
        lambda *refs: assemble_kernel(moves, plan, lanes, count, *refs),
        name="assemble_block",
        out_shape=[
            pltpu.VMEM((3, BZB + 1, BXD * side, width), f32),
            pltpu.VMEM((2, BZB, BXD * side, 128), f32),
            pltpu.VMEM((strips, 8, 128), f32),
            pltpu.VMEM((strips, 8, 128), f32),
            pltpu.VMEM((8, 128), f32),
        ],
        in_specs=[VECTORS] * (4 + len(units)),
        out_specs=[VECTORS] * 5,
        scratch_shapes=[
            sides,
            sides,
        ],
        compiler_params=ROOM,
    )(own_table, field, source, beta, *got)
    from_pair = lax.ppermute(to_pair, "node", [(i, i ^ 1) for i in range(nodes)])
    from_other = lax.ppermute(to_other, "node", [(i, (i - 1 + 2 * (i % 2)) % nodes) for i in range(nodes)])
    two_on = lax.ppermute(row_table, "node", [(i, (i + 2) % nodes) for i in range(nodes)])
    tiles, rows = width // 128, BXD * side
    half_rows = pltpu.VMEM((BZB, rows // 2, width), f32)
    coupled = pl.pallas_call(
        lambda *refs: couple_kernel(lanes, nodes, plane, *refs),
        name="couple_block",
        out_shape=[half_rows] * 17,
        in_specs=[VECTORS] * 2,
        out_specs=[VECTORS] * 17,
        scratch_shapes=[pltpu.VMEM((tiles, BZB, rows, 128), f32)] * 9,
        compiler_params=ROOM,
    )(block, fifth)
    pair_tile = pltpu.VMEM((2, 8, width), f32)
    smoothed, coarse, flag = pl.pallas_call(
        lambda *refs: smooth_kernel(lanes, nodes, covered, *refs),
        name="smooth_block",
        out_shape=[
            jax.ShapeDtypeStruct((count, side, plane), f32),
            jax.ShapeDtypeStruct((count, (side // 2) ** 3), f32),
            jax.ShapeDtypeStruct((1, 1), jnp.int32),
        ],
        in_specs=[VECTORS] * (2 + 17 + 4),
        out_specs=[VECTORS, VECTORS, SCALARS],
        scratch_shapes=[pltpu.VMEM((BZB, rows // 2 + 16, width), f32)] * 2
        + [pair_tile] * 2
        + [half_rows] * 6
        + [pair_tile] * 16
        + [pltpu.VMEM((tiles, 2, 16, 128), f32)] * 9
        + [pltpu.VMEM((plane // 128, count * side, 128), f32), pltpu.VMEM((plane // 128, count * side // 2, 128), f32)]
        + [pltpu.SMEM((8, 128), f32), pltpu.SemaphoreType.DMA],
        compiler_params=ROOM,
    )(own_table, block, *coupled, from_pair, from_other, row_table, two_on)
    irregular = flag[0, 0]
    if not covered:
        irregular = lax.pmax(irregular, ("node", "lane"))

    def again(carry):
        out = general_body(field, source, beta, target_held, neighbours_held)
        return (*out, jnp.int32(0))

    smoothed, coarse, _ = lax.while_loop(lambda carry: carry[2] > 0, again, (smoothed, coarse, irregular))
    return smoothed, coarse


def solution(mesh):
    in_specs = (
        P(("node", "lane"), None, None),
        P(("node", "lane"), None, None),
        P(("node", "lane"), None, None),
        P(("node", "lane")),
        P(("node", "lane"), None),
    )
    out_specs = (P(("node", "lane"), None, None), P(("node", "lane"), None))
    return jax.shard_map(fast_body, mesh=mesh, in_specs=in_specs, out_specs=out_specs, check_vma=False)
```
